32 devices in a mesh: dp: 8 (over z, y), head: 4 (over x, core).
Axes of the slice: x: 2, y: 2, z: 4, core: 2. Of those that a mesh axis runs over, the one named last changes fastest.
Arguments:
- tokens: int32 [8, 1024], P('dp'), may hold values from 0 to 32767
- targets: int32 [8, 1024], P('dp'), may hold values from 0 to 32767
- lengths: int32 [8], P('dp'), may hold values from 341 to 1024
- table: float32 [512, 32768], P('dp', 'head'), may hold values from -0.6629126 to 0.6629126
- table_first: float32 [512, 32768], P('dp', 'head'), may hold values from -9.691891e-05 to 9.691891e-05
- table_second: float32 [512, 32768], P('dp', 'head'), may hold values from 3.75731e-11 to 1.502924e-10
- attn_in: float32 [3, 512, 8, 224], P(None, 'dp', 'head'), may hold values from -0.25 to 0.25
- attn_in_first: float32 [3, 512, 8, 224], P(None, 'dp', 'head'), may hold values from -9.691891e-05 to 9.691891e-05
- attn_in_second: float32 [3, 512, 8, 224], P(None, 'dp', 'head'), may hold values from 3.75731e-11 to 1.502924e-10
- attn_out: float32 [3, 8, 64, 512], P(None, 'head', None, 'dp'), may hold values from -1 to 1
- attn_out_first: float32 [3, 8, 64, 512], P(None, 'head', None, 'dp'), may hold values from -9.691891e-05 to 9.691891e-05
- attn_out_second: float32 [3, 8, 64, 512], P(None, 'head', None, 'dp'), may hold values from 3.75731e-11 to 1.502924e-10
- ffn_up: float32 [3, 512, 2048], P(None, 'dp', 'head'), may hold values from -0.25 to 0.25
- ffn_up_first: float32 [3, 512, 2048], P(None, 'dp', 'head'), may hold values from -9.691891e-05 to 9.691891e-05
- ffn_up_second: float32 [3, 512, 2048], P(None, 'dp', 'head'), may hold values from 3.75731e-11 to 1.502924e-10
- ffn_down: float32 [3, 2048, 512], P(None, 'head', 'dp'), may hold values from -0.1875 to 0.1875
- ffn_down_first: float32 [3, 2048, 512], P(None, 'head', 'dp'), may hold values from -9.691891e-05 to 9.691891e-05
- ffn_down_second: float32 [3, 2048, 512], P(None, 'head', 'dp'), may hold values from 3.75731e-11 to 1.502924e-10
- norms: float32 [7, 2, 512], P(None, None, 'head'), may hold values from -1.5 to 1.8
- norms_first: float32 [7, 2, 512], P(None, None, 'head'), may hold values from -9.691891e-05 to 9.691891e-05
- norms_second: float32 [7, 2, 512], P(None, None, 'head'), may hold values from 3.75731e-11 to 1.502924e-10
Outputs:
- loss_parts: float32 [2], replicated
- clip_norm: float32 [], replicated
- refreshed_table: float32 [512, 32768], P('dp', 'head')
- table_copy: bfloat16 [512, 32768], P('dp', 'head')
- table_first_new: float32 [512, 32768], P('dp', 'head')
- table_second_new: float32 [512, 32768], P('dp', 'head')
- attn_in_new: float32 [3, 512, 8, 224], P(None, 'dp', 'head')
- attn_in_copy: bfloat16 [3, 512, 8, 224], P(None, 'dp', 'head')
- attn_in_first_new: float32 [3, 512, 8, 224], P(None, 'dp', 'head')
- attn_in_second_new: float32 [3, 512, 8, 224], P(None, 'dp', 'head')
- attn_out_new: float32 [3, 8, 64, 512], P(None, 'head', None, 'dp')
- attn_out_copy: bfloat16 [3, 8, 64, 512], P(None, 'head', None, 'dp')
- attn_out_first_new: float32 [3, 8, 64, 512], P(None, 'head', None, 'dp')
- attn_out_second_new: float32 [3, 8, 64, 512], P(None, 'head', None, 'dp')
- ffn_up_new: float32 [3, 512, 2048], P(None, 'dp', 'head')
- ffn_up_copy: bfloat16 [3, 512, 2048], P(None, 'dp', 'head')
- ffn_up_first_new: float32 [3, 512, 2048], P(None, 'dp', 'head')
- ffn_up_second_new: float32 [3, 512, 2048], P(None, 'dp', 'head')
- ffn_down_new: float32 [3, 2048, 512], P(None, 'head', 'dp')
- ffn_down_copy: bfloat16 [3, 2048, 512], P(None, 'head', 'dp')
- ffn_down_first_new: float32 [3, 2048, 512], P(None, 'head', 'dp')
- ffn_down_second_new: float32 [3, 2048, 512], P(None, 'head', 'dp')
- norms_new: float32 [7, 2, 512], P(None, None, 'head')
- norms_first_new: float32 [7, 2, 512], P(None, None, 'head')
- norms_second_new: float32 [7, 2, 512], P(None, None, 'head')
The draws below stay inside these ranges and needn't reach their ends.
All inputs are finite; a program needn't handle non-finite values.
Results may differ from the reference program's by a relative error of at most 0.0092.
Values may be sent and summed in bfloat16 or wider, within the bound.
A program may use at most 256 MiB of HBM per device.

```python
import math
import jax
import jax.numpy as jnp
import numpy as np
from jax import lax

D = 512
H = 8
HD = 64
FF = 2048
V = 32768
BLOCK = 32
SINK = 8
L = 3
STEP = 10
LEN = 1024
SEQS = 8
NB = 32
PARAMS = 26614784


def draw_lengths(key, part):
    key = jax.random.fold_in(key, 11)
    seq_index = jnp.arange(SEQS, dtype=jnp.int32)
    base = LEN // 3 + 2 * LEN // 3 * seq_index // max(SEQS - 1, 1)
    extra = jax.random.randint(key, (SEQS,), 0, LEN // 4 + 1, dtype=jnp.int32)
    return jnp.minimum(base + extra, LEN).astype(jnp.int32)


def draw_table(key, part):
    key = jax.random.fold_in(key, 12)
    column = jnp.arange(V, dtype=jnp.float32) / V
    noise = jnp.clip(jax.random.normal(key, (D, V), jnp.float32), -5.0, 5.0)
    ramp = 1.0 + 2.0 * column
    return (noise * ramp[None, :] / math.sqrt(D)).astype(jnp.float32)


def draw_norms(key, part):
    key = jax.random.fold_in(key, 13)
    gain_key, bias_random_key = jax.random.split(key)
    ramp = 0.5 + jnp.arange(D, dtype=jnp.float32) / D
    gain = ramp[None, :] * jax.random.uniform(gain_key, (2 * L + 1, D), jnp.float32, 0.8, 1.2)
    bias = 0.3 * jnp.clip(jax.random.normal(bias_random_key, (2 * L + 1, D), jnp.float32), -5.0, 5.0)
    return jnp.stack([gain, bias], 1)


def plant(drawn, rng, low, high):
    longest = drawn.shape.index(max(drawn.shape))
    spots = []
    for shift in (0, 1):
        where = [jax.random.randint(jax.random.fold_in(rng, axis), (), 0, length) for axis, length in enumerate(drawn.shape)]
        where[longest] = (where[longest] + shift) % drawn.shape[longest]
        spots.append(tuple(where))
    return drawn.at[spots[0]].set(low).at[spots[1]].set(high)


def block_scale(rng, dims, shards, low, top_value):
    level = 1.0
    for axis_at, blocks in shards:
        heights = jax.random.uniform(jax.random.fold_in(jax.random.fold_in(rng, 6), axis_at), (blocks,), jnp.float32, low / len(shards), top_value / len(shards))
        level = level * jnp.repeat(jnp.exp(heights), dims[axis_at] // blocks).reshape((-1,) + (1,) * (len(dims) - 1 - axis_at))
    return level


def rank_bounds(count, skew):
    loads = [(1 << 20) // math.isqrt(grade ** skew) + 1 for grade in range(1, count + 1)]
    deviation = 1 + sum(loads) // (1 << 30)
    return np.cumsum(np.array([max(1, weight // deviation) for weight in loads]))


def ranked(key, extent, number_of, lean):
    listing = rank_bounds(number_of, lean)
    lot = jax.random.randint(jax.random.fold_in(key, 1), extent, 0, int(listing[number_of - 1]))
    standing = jnp.searchsorted(jnp.asarray(listing, jnp.int32), lot, side="right")
    return jax.random.permutation(jax.random.fold_in(key, 2), number_of)[standing].astype(jnp.int32)


def scatter_about(rng, dims, scale, bound, pieces=(), kind=jnp.bfloat16):
    values = scale * jax.random.normal(rng, dims, jnp.float32)
    if pieces:
        values = values * block_scale(rng, dims, pieces, -0.22, 0.18)
    return jnp.clip(values, -bound, bound).astype(kind)


def setup_inputs(seed: int = 0) -> dict:
    splits = jax.random.split(jax.random.key(seed), 22)
    tokens = plant(ranked(splits[0], (SEQS, LEN), V, 2), jax.random.fold_in(splits[0], 3), 0, V - 1).astype(jnp.int32)
    targets = plant(ranked(splits[1], (SEQS, LEN), V, 2), jax.random.fold_in(splits[1], 3), 0, V - 1).astype(jnp.int32)
    lengths = draw_lengths(jax.random.fold_in(splits[21], 71), 0)
    table = draw_table(jax.random.fold_in(splits[21], 71), 0)
    table_first = scatter_about(splits[4], (D, V), (0.11 * PARAMS ** -0.5), 9.691891318652779e-05, ((0, 8), (1, 4)), jnp.float32)
    table_second = jnp.clip(jnp.exp(math.log(1.502924035223785e-10) - 1.3862944 * jax.random.uniform(splits[5], (D, V), jnp.float32) ** block_scale(splits[5], (D, V), ((0, 8), (1, 4)), -0.2, 0.2)), 3.757310088059462e-11, 1.502924035223785e-10)
    attn_in = scatter_about(splits[6], (L, D, H, 3 * HD + NB), D ** -0.5, 0.25, ((1, 8), (2, 4)), jnp.float32)
    attn_in_first = scatter_about(splits[7], (L, D, H, 3 * HD + NB), (0.11 * PARAMS ** -0.5), 9.691891318652779e-05, ((1, 8), (2, 4)), jnp.float32)
    attn_in_second = jnp.clip(jnp.exp(math.log(1.502924035223785e-10) - 1.3862944 * jax.random.uniform(splits[8], (L, D, H, 3 * HD + NB), jnp.float32) ** block_scale(splits[8], (L, D, H, 3 * HD + NB), ((1, 8), (2, 4)), -0.2, 0.2)), 3.757310088059462e-11, 1.502924035223785e-10)
    attn_out = scatter_about(splits[9], (L, H, HD, D), (H * HD // 16) ** -0.5, 1.0, ((1, 4), (3, 8)), jnp.float32)
    attn_out_first = scatter_about(splits[10], (L, H, HD, D), (0.11 * PARAMS ** -0.5), 9.691891318652779e-05, ((1, 4), (3, 8)), jnp.float32)
    attn_out_second = jnp.clip(jnp.exp(math.log(1.502924035223785e-10) - 1.3862944 * jax.random.uniform(splits[11], (L, H, HD, D), jnp.float32) ** block_scale(splits[11], (L, H, HD, D), ((1, 4), (3, 8)), -0.2, 0.2)), 3.757310088059462e-11, 1.502924035223785e-10)
    ffn_up = scatter_about(splits[12], (L, D, FF), D ** -0.5, 0.25, ((1, 8), (2, 4)), jnp.float32)
    ffn_up_first = scatter_about(splits[13], (L, D, FF), (0.11 * PARAMS ** -0.5), 9.691891318652779e-05, ((1, 8), (2, 4)), jnp.float32)
    ffn_up_second = jnp.clip(jnp.exp(math.log(1.502924035223785e-10) - 1.3862944 * jax.random.uniform(splits[14], (L, D, FF), jnp.float32) ** block_scale(splits[14], (L, D, FF), ((1, 8), (2, 4)), -0.2, 0.2)), 3.757310088059462e-11, 1.502924035223785e-10)
    ffn_down = scatter_about(splits[15], (L, FF, D), (FF // 2) ** -0.5, 0.1875, ((1, 4), (2, 8)), jnp.float32)
    ffn_down_first = scatter_about(splits[16], (L, FF, D), (0.11 * PARAMS ** -0.5), 9.691891318652779e-05, ((1, 4), (2, 8)), jnp.float32)
    ffn_down_second = jnp.clip(jnp.exp(math.log(1.502924035223785e-10) - 1.3862944 * jax.random.uniform(splits[17], (L, FF, D), jnp.float32) ** block_scale(splits[17], (L, FF, D), ((1, 4), (2, 8)), -0.2, 0.2)), 3.757310088059462e-11, 1.502924035223785e-10)
    norms = draw_norms(jax.random.fold_in(splits[21], 71), 0)
    norms_first = scatter_about(splits[19], (2 * L + 1, 2, D), (0.11 * PARAMS ** -0.5), 9.691891318652779e-05, ((2, 4),), jnp.float32)
    norms_second = jnp.clip(jnp.exp(math.log(1.502924035223785e-10) - 1.3862944 * jax.random.uniform(splits[20], (2 * L + 1, 2, D), jnp.float32) ** block_scale(splits[20], (2 * L + 1, 2, D), ((2, 4),), -0.2, 0.2)), 3.757310088059462e-11, 1.502924035223785e-10)
    return dict(tokens=tokens, targets=targets, lengths=lengths, table=table, table_first=table_first, table_second=table_second, attn_in=attn_in, attn_in_first=attn_in_first, attn_in_second=attn_in_second, attn_out=attn_out, attn_out_first=attn_out_first, attn_out_second=attn_out_second, ffn_up=ffn_up, ffn_up_first=ffn_up_first, ffn_up_second=ffn_up_second, ffn_down=ffn_down, ffn_down_first=ffn_down_first, ffn_down_second=ffn_down_second, norms=norms, norms_first=norms_first, norms_second=norms_second)


@jax.custom_vjp
def narrow_float_format(v):
    return lax.optimization_barrier(v.astype(jnp.bfloat16)).astype(jnp.float32)

@jax.custom_vjp
def low_back(v):
    return v

def low_keep(v):
    return (narrow_float_format(v), None)

def low_pass(kept, grad):
    return (grad,)

def back_keep(v):
    return (v, None)

def back_low(kept, grad):
    return (narrow_float_format(grad),)
narrow_float_format.defvjp(low_keep, low_pass)
low_back.defvjp(back_keep, back_low)
HIGHEST = lax.Precision.HIGHEST
EPSILON = 1e-05
NEGATIVE = -1000000000.0
TEMPER = 0.75
BETA_ONE = 0.9
BETA_TWO = 0.999
ADAM_FLOOR = 1e-08
WEIGHT_DECAY = 0.01
RATE_MATRIX = 0.1
RATE_NORM = 0.5
CLIP_LIMIT = 1.0

def layer_norm(stream, gain, bias):
    average = lax.optimization_barrier(jnp.mean(stream, -1, keepdims=True))
    variance = lax.optimization_barrier(jnp.mean(stream * stream, -1, keepdims=True)) - average * average
    return (stream - average) * lax.rsqrt(variance + EPSILON) * gain + bias

def alternating_marginal_scaling(vocabulary_score_lines):
    block_total = vocabulary_score_lines.shape[-1]
    row_index = lax.broadcasted_iota(jnp.int32, (block_total, block_total), 0)
    column_index = lax.broadcasted_iota(jnp.int32, (block_total, block_total), 1)
    allowed = column_index < row_index
    log_plan = jnp.where(allowed, vocabulary_score_lines / TEMPER, NEGATIVE)
    for sweep_index in range(SINK):
        log_plan = jnp.where(allowed, log_plan - jax.nn.logsumexp(log_plan, -2, keepdims=True), NEGATIVE)
        log_plan = jnp.where(allowed, log_plan - jax.nn.logsumexp(log_plan, -1, keepdims=True), NEGATIVE)
    return jnp.where(allowed, jnp.exp(log_plan), 0.0)

def block_view(tensor, block_count):
    seq_count, length_all, group_count, trailing = tensor.shape
    return tensor.reshape(seq_count, block_count, length_all // block_count, group_count, trailing).transpose(0, 3, 1, 2, 4)

def attend_mask(block_count, block_size):
    shape = (block_count, block_size, 2 * block_size)
    block_index = lax.broadcasted_iota(jnp.int32, shape, 0)
    query_index = lax.broadcasted_iota(jnp.int32, shape, 1)
    slot_index = lax.broadcasted_iota(jnp.int32, shape, 2)
    own_block = (slot_index >= block_size) & (slot_index - block_size <= query_index)
    return own_block | (slot_index < block_size) & (block_index >= 1)

def attention(hidden, w_in, w_out):
    seq_count, length_all, full_width = hidden.shape
    block_count = length_all // BLOCK
    projected = low_back(jnp.einsum('snd,dhc->snhc', hidden, w_in, precision=HIGHEST))
    queries = block_view(narrow_float_format(projected[..., :HD]), block_count)
    key_blocks = block_view(narrow_float_format(projected[..., HD:2 * HD]), block_count)
    value_blocks = block_view(narrow_float_format(projected[..., 2 * HD:3 * HD]), block_count)
    vocabulary_score_lines = lax.optimization_barrier(jnp.sum(block_view(projected[..., 3 * HD:], block_count), 3)) / math.sqrt(BLOCK)
    doubly_stochastic_matrix = narrow_float_format(alternating_marginal_scaling(vocabulary_score_lines))
    sorted_keys = narrow_float_format(low_back(jnp.einsum('shij,shjtc->shitc', doubly_stochastic_matrix, key_blocks, precision=HIGHEST)))
    permuted_value_blocks = narrow_float_format(low_back(jnp.einsum('shij,shjtc->shitc', doubly_stochastic_matrix, value_blocks, precision=HIGHEST)))
    key_set = jnp.concatenate([sorted_keys, key_blocks], 3)
    value_set = jnp.concatenate([permuted_value_blocks, value_blocks], 3)
    scores = low_back(jnp.einsum('shitc,shiuc->shitu', queries, key_set, precision=HIGHEST) / math.sqrt(HD))
    scores = jnp.where(attend_mask(block_count, BLOCK), scores, NEGATIVE)
    attn_weights = narrow_float_format(jax.nn.softmax(scores, -1))
    mixed = narrow_float_format(low_back(jnp.einsum('shitu,shiuc->shitc', attn_weights, value_set, precision=HIGHEST)))
    mixed = mixed.transpose(0, 2, 3, 1, 4).reshape(seq_count, length_all, H * HD)
    return jnp.einsum('snk,kd->snd', mixed, w_out.reshape(H * HD, full_width), precision=HIGHEST)

def forward(weights, tokens, targets, counted):
    table, attn_in, attn_out, ffn_up, ffn_down, norms = weights
    stream = low_back(jnp.take(table, tokens, axis=1).transpose(1, 2, 0) * math.sqrt(D))
    for layer_at in range(L):
        hidden = narrow_float_format(layer_norm(stream, norms[2 * layer_at, 0], norms[2 * layer_at, 1]))
        stream = stream + low_back(attention(hidden, attn_in[layer_at], attn_out[layer_at]))
        hidden = narrow_float_format(layer_norm(stream, norms[2 * layer_at + 1, 0], norms[2 * layer_at + 1, 1]))
        upward = low_back(jnp.einsum('snd,df->snf', hidden, ffn_up[layer_at], precision=HIGHEST))
        stream = stream + low_back(jnp.einsum('snf,fd->snd', narrow_float_format(jax.nn.gelu(upward)), ffn_down[layer_at], precision=HIGHEST))
    final_rows = narrow_float_format(layer_norm(stream, norms[2 * L, 0], norms[2 * L, 1]))

    def sequence_loss(carry, item):
        rows_here, goals, weighting = item
        vocabulary_score_lines = low_back(jnp.dot(rows_here, table, precision=HIGHEST))
        top_logit = lax.optimization_barrier(jnp.max(vocabulary_score_lines, -1, keepdims=True))
        log_total = top_logit[:, 0] + jnp.log(lax.optimization_barrier(jnp.sum(jnp.exp(vocabulary_score_lines - top_logit), -1)))
        picked = jnp.take_along_axis(vocabulary_score_lines, goals[:, None], 1)[:, 0]
        return (carry + jnp.sum((log_total - picked) * weighting), None)
    loss_sum, unused = lax.scan(jax.checkpoint(sequence_loss), jnp.zeros((), jnp.float32), (final_rows, targets, counted))
    return loss_sum

def adamw(weight, gradient, moment_one, moment_two, factor, step_rate):
    gradient = gradient * factor
    moment_one = BETA_ONE * moment_one + (1.0 - BETA_ONE) * gradient
    moment_two = BETA_TWO * moment_two + (1.0 - BETA_TWO) * gradient * gradient
    adam_step = moment_one / (1.0 - BETA_ONE ** STEP) / (jnp.sqrt(moment_two / (1.0 - BETA_TWO ** STEP)) + ADAM_FLOOR)
    return (weight - step_rate * (adam_step + WEIGHT_DECAY * weight), moment_one, moment_two)

def reference(tokens, targets, lengths, table, table_first, table_second, attn_in, attn_in_first, attn_in_second, attn_out, attn_out_first, attn_out_second, ffn_up, ffn_up_first, ffn_up_second, ffn_down, ffn_down_first, ffn_down_second, norms, norms_first, norms_second):
    positions = jnp.arange(LEN, dtype=jnp.int32)
    counted = (positions[None, :] < lengths[:, None]).astype(jnp.float32)
    used = (narrow_float_format(table), narrow_float_format(attn_in), narrow_float_format(attn_out), narrow_float_format(ffn_up), narrow_float_format(ffn_down), norms)

    def objective(*weights):
        return forward(weights, tokens, targets, counted)
    loss_sum, pull = jax.vjp(objective, *used)
    grads = pull(jnp.ones_like(loss_sum))
    squares = jnp.sum(jnp.stack([jnp.sum(member * member) for member in grads]))
    grad_norm = jnp.sqrt(squares)
    factor = jnp.minimum(1.0, CLIP_LIMIT / (grad_norm + 1e-06))
    refreshed_table, table_one, table_two = adamw(table, grads[0], table_first, table_second, factor, RATE_MATRIX)
    in_new, in_one, in_two = adamw(attn_in, grads[1], attn_in_first, attn_in_second, factor, RATE_MATRIX)
    out_new, out_one, out_two = adamw(attn_out, grads[2], attn_out_first, attn_out_second, factor, RATE_MATRIX)
    up_new, up_one, up_two = adamw(ffn_up, grads[3], ffn_up_first, ffn_up_second, factor, RATE_MATRIX)
    down_new, down_one, down_two = adamw(ffn_down, grads[4], ffn_down_first, ffn_down_second, factor, RATE_MATRIX)
    norms_new, norms_one, norms_two = adamw(norms, grads[5], norms_first, norms_second, factor, RATE_NORM)
    return (jnp.stack([loss_sum, jnp.sum(counted)]), grad_norm, refreshed_table, refreshed_table.astype(jnp.bfloat16), table_one, table_two, in_new, in_new.astype(jnp.bfloat16), in_one, in_two, out_new, out_new.astype(jnp.bfloat16), out_one, out_two, up_new, up_new.astype(jnp.bfloat16), up_one, up_two, down_new, down_new.astype(jnp.bfloat16), down_one, down_two, norms_new, norms_one, norms_two)
```

```python
import functools
import math

import jax
import jax.numpy as jnp
from jax import lax
from jax.experimental import pallas as pl
from jax.experimental.pallas import tpu as pltpu
from jax.sharding import PartitionSpec as P

HD = 64
BLOCK = 32
SINK = 8
STEP = 10
EPSILON = 1e-05
NEGATIVE = -1000000000.0
TEMPER = 0.75
BETA_ONE = 0.9
BETA_TWO = 0.999
ADAM_FLOOR = 1e-08
WEIGHT_DECAY = 0.01
RATE_MATRIX = 0.1
RATE_NORM = 0.5
CLIP_LIMIT = 1.0

BF = jnp.bfloat16
F32 = jnp.float32
GROUP = 2
GELU_C = math.sqrt(2.0 / math.pi)
GELU_A = 0.044715

C_Q = (0, 128)
C_KVS = (128, 512)
C_OUT = (512, 640)
C_UP = (640, 1152)
C_DOWN = (1152, 1664)
PACKED = 1664
VMEM_LIMIT = 56 * 1024 * 1024


def dot_nn(a, b):
    return lax.dot_general(a, b, (((1,), (0,)), ((), ())), preferred_element_type=F32)


def dot_nt(a, b):
    return lax.dot_general(a, b, (((1,), (1,)), ((), ())), preferred_element_type=F32)


def dot_tn(a, b):
    return lax.dot_general(a, b, (((0,), (0,)), ((), ())), preferred_element_type=F32)


def iota(shape, axis):
    return lax.broadcasted_iota(jnp.int32, shape, axis)


def norm_stats(stream):
    average = jnp.mean(stream, -1, keepdims=True)
    variance = jnp.mean(stream * stream, -1, keepdims=True) - average * average
    inv_std = lax.rsqrt(variance + EPSILON)
    return (stream - average) * inv_std, inv_std


def norm_apply(stream, gain, bias):
    normed, _ = norm_stats(stream)
    return (normed * gain + bias).astype(BF)


def norm_back(upstream, stream, gain):
    normed, inv_std = norm_stats(stream)
    scaled = upstream * gain
    back = inv_std * (
        scaled
        - jnp.mean(scaled, -1, keepdims=True)
        - normed * jnp.mean(scaled * normed, -1, keepdims=True)
    )
    pair = jnp.concatenate(
        [jnp.sum(upstream * normed, 0, keepdims=True), jnp.sum(upstream, 0, keepdims=True)], 0
    )
    return back, pair


def allowed_mask(shape):
    return iota(shape, len(shape) - 1) < iota(shape, len(shape) - 2)


def log_total(x, axis):
    top = jnp.max(x, axis, keepdims=True)
    return top + jnp.log(jnp.sum(jnp.exp(x - top), axis, keepdims=True))


def balance(scores, keep):
    allowed = allowed_mask(scores.shape)
    plan = jnp.where(allowed, scores / TEMPER, NEGATIVE)
    for _ in range(SINK):
        for axis in (-2, -1):
            plan = jnp.where(allowed, plan - log_total(plan, axis), NEGATIVE)
            if keep is not None:
                keep.append(plan)
    return jnp.where(allowed, jnp.exp(plan), 0.0)


def balance_back(scores, upstream):
    allowed = allowed_mask(scores.shape)
    plans = []
    perm = balance(scores, plans)
    grad = jnp.where(allowed, upstream * perm, 0.0)
    for step in reversed(range(2 * SINK)):
        axis = (-2, -1)[step % 2]
        share = jnp.exp(plans[step])
        grad = jnp.where(allowed, grad - share * jnp.sum(grad, axis, keepdims=True), 0.0)
    return grad / TEMPER


def kron_rows(perm_rows, length):
    own, blocks = perm_rows.shape
    rows = own * BLOCK
    tall = jnp.broadcast_to(perm_rows[:, None, :], (own, BLOCK, blocks)).reshape(rows, blocks)
    spread = (iota((blocks, length), 1) // BLOCK == iota((blocks, length), 0)).astype(BF)
    wide = dot_nn(tall.astype(BF), spread)
    same = (iota((rows, length), 0) & (BLOCK - 1)) == (iota((rows, length), 1) & (BLOCK - 1))
    return jnp.where(same, wide, 0.0).astype(BF)


def group_mask(first_block, rows):
    shape = (rows, 2 * rows)
    row, slot = iota(shape, 0), iota(shape, 1)
    row_block = row // BLOCK
    in_sorted = slot < rows
    place = jnp.where(in_sorted, slot, slot - rows)
    same = (place // BLOCK) == row_block
    sorted_ok = in_sorted & (row_block + first_block >= 1)
    own_ok = (slot >= rows) & (place <= row)
    return same & (sorted_ok | own_ok)


def load_weights(pieces, w_ref, sems):
    copies = [pltpu.make_async_copy(piece, w_ref.at[p], sems.at[p]) for p, piece in enumerate(pieces)]
    for copy in copies:
        copy.start()
    return copies


def forward_kernel(
    me_ref, hid0_ref, hid1_ref, hid2in_ref, hid3_ref, stream_ref, w0_ref, w1_ref, w2_ref, w3_ref, nrm_ref,
    stream_out, mid_out, hnext_out, hid_ref, kv_out, q_out, skv_out, attw_out, mixed_out,
    permo_out, sort_out, hid2_out, upw_out, act_out,
    w_ref, perm_scr, acc_scr, sems,
):
    length, width = hid_ref.shape
    rows = stream_ref.shape[0]
    pairs = w_ref.shape[0]
    own_blocks = rows // BLOCK
    blocks = length // BLOCK
    my = me_ref[0]
    own = pl.multiple_of(my * rows, rows)
    own_block = pl.multiple_of(my * own_blocks, own_blocks)
    lower = iota((1, 128), 1) < HD
    copies = load_weights((w0_ref, w1_ref, w2_ref, w3_ref), w_ref, sems)
    for p, piece in enumerate((hid0_ref, hid1_ref, hid2in_ref, hid3_ref)):
        hid_ref[pl.ds(pl.multiple_of((my ^ p) * rows, rows), rows), :] = piece[...]
    for copy in copies:
        copy.wait()

    def project(step, _):
        j, tile = step // (length // rows), step % (length // rows)
        at = pl.multiple_of(tile * rows, rows)
        w = w_ref[j, :, :, C_KVS[0]:C_KVS[1]].reshape(width, C_KVS[1] - C_KVS[0])
        got = dot_nn(hid_ref[pl.ds(at, rows), :], w)
        kv_out[j, pl.ds(at, rows), :] = got[:, :256].astype(BF)
        sort_out[j, pl.ds(pl.multiple_of(tile * own_blocks, own_blocks), own_blocks), :] = jnp.sum(
            got[:, 256:].reshape(own_blocks, BLOCK, 128), 1
        ) / math.sqrt(BLOCK)
        return 0

    lax.fori_loop(0, pairs * (length // rows), project, 0)

    scores = jnp.stack(
        [sort_out[h // 2][:, (h % 2) * BLOCK:(h % 2) * BLOCK + blocks] for h in range(2 * pairs)]
    )
    perm_scr[...] = balance(scores, None)
    permo_out[...] = perm_scr[:, pl.ds(own_block, own_blocks), :]
    acc_scr[...] = stream_ref[...]
    take = GROUP * BLOCK

    def attend(j, _):
        wq = w_ref[j, :, :, C_Q[0]:C_Q[1]].reshape(width, 128)
        q = dot_nn(hid_ref[pl.ds(own, rows), :], wq).astype(BF)
        q_out[j] = q
        mixes = []
        for h in range(2):
            kron = kron_rows(permo_out[2 * j + h], length)
            skv = dot_nn(kron, kv_out[j, :, h * 128:(h + 1) * 128]).astype(BF)
            skv_out[j, h] = skv
            q_mine = jnp.where(lower if h == 0 else ~lower, q, jnp.zeros_like(q))
            kv_own = kv_out[j, pl.ds(own, rows), h * 128:(h + 1) * 128]
            pieces = []
            for g in range(rows // take):
                cut = slice(g * take, (g + 1) * take)
                kv_set = jnp.concatenate([skv[cut], kv_own[cut]], 0)
                raw = dot_nt(q_mine[cut], kv_set) * (1.0 / math.sqrt(HD))
                raw = jnp.where(group_mask(own_block + g * GROUP, take), raw, NEGATIVE)
                grown = jnp.exp(raw - jnp.max(raw, -1, keepdims=True))
                share = grown / jnp.sum(grown, -1, keepdims=True)
                attw_out[j, h, cut, :] = share
                pieces.append(dot_nn(share.astype(BF), kv_set))
            mixes.append(jnp.concatenate(pieces, 0))
        mixed = jnp.where(lower, mixes[1], mixes[0]).astype(BF)
        mixed_out[j] = mixed
        w_o = w_ref[j, :, :, C_OUT[0]:C_OUT[1]].reshape(width, 128)
        acc_scr[...] += dot_nt(mixed, w_o)
        return 0

    lax.fori_loop(0, pairs, attend, 0)

    middle = acc_scr[...]
    mid_out[...] = middle
    hid2_out[...] = norm_apply(middle, nrm_ref[0:1, :], nrm_ref[1:2, :])

    def feed(j, _):
        w_up = w_ref[j, :, :, C_UP[0]:C_UP[1]].reshape(width, 512)
        upward = dot_nn(hid2_out[...], w_up)
        upw_out[j] = upward
        bent = jnp.tanh(GELU_C * (upward + GELU_A * upward * upward * upward))
        act = (0.5 * upward * (1.0 + bent)).astype(BF)
        act_out[j] = act
        w_dn = w_ref[j, :, :, C_DOWN[0]:C_DOWN[1]].reshape(width, 512)
        acc_scr[...] += dot_nt(act, w_dn)
        return 0

    lax.fori_loop(0, pairs, feed, 0)
    result = acc_scr[...]
    stream_out[...] = result
    hnext_out[...] = norm_apply(result, nrm_ref[2:3, :], nrm_ref[3:4, :])


def ignore_tail(kernel, used, extra):
    def run(*refs):
        kernel(*refs[:used], *refs[used + extra:])
    return run


def layer_forward(me, hidden, stream, weights, nrm, after=()):
    rows, width = stream.shape
    pairs = len(hidden)
    length = rows * pairs
    own_blocks, blocks = rows // BLOCK, length // BLOCK
    shape = jax.ShapeDtypeStruct
    outs = [
        shape((rows, width), F32),
        shape((rows, width), F32),
        shape((rows, width), BF),
        shape((length, width), BF),
        shape((pairs, length, 256), BF),
        shape((pairs, rows, 128), BF),
        shape((pairs, 2, rows, 128), BF),
        shape((pairs, 2, rows, 2 * GROUP * BLOCK), F32),
        shape((pairs, rows, 128), BF),
        shape((2 * pairs, own_blocks, blocks), F32),
        shape((pairs, blocks, 128), F32),
        shape((rows, width), BF),
        shape((pairs, rows, 512), F32),
        shape((pairs, rows, 512), BF),
    ]
    vm = pl.BlockSpec(memory_space=pltpu.VMEM)
    far = pl.BlockSpec(memory_space=pl.ANY)
    return pl.pallas_call(
        ignore_tail(forward_kernel, 2 * pairs + 3, len(after)),
        out_shape=outs,
        in_specs=[pl.BlockSpec(memory_space=pltpu.SMEM)] + [vm] * (pairs + 1) + [far] * pairs + [vm]
        + [far] * len(after),
        out_specs=[vm] * len(outs),
        scratch_shapes=[
            pltpu.VMEM((pairs,) + weights[0].shape, BF),
            pltpu.VMEM((2 * pairs, blocks, blocks), F32),
            pltpu.VMEM((rows, width), F32),
            pltpu.SemaphoreType.DMA((pairs,)),
        ],
        compiler_params=pltpu.CompilerParams(vmem_limit_bytes=VMEM_LIMIT),
        cost_estimate=pl.CostEstimate(flops=20_000_000_000, bytes_accessed=18_000_000, transcendentals=0),
        name="layer_forward",
    )(me, *hidden, stream, *weights, nrm, *after)


def backward_kernel(
    me_ref, keep_ref, near_ref, far_ref, above_ref, carry_ref, gain_above_ref,
    w0_ref, w1_ref, w2_ref, w3_ref, gain_two_ref, mid_ref, hid_ref, kv_ref, q_ref, skv_ref, attw_ref,
    mixed_ref, permo_ref, sort_ref, hid2_ref, upw_ref, act_ref,
    gkeep_out, gsend_out, wkeep_out, wsend_out, carry_out, pair_above_out, pair_two_out,
    w_ref, acc_scr, ghid_scr, gkv_scr, gsrt_scr, gq_scr, dperm_scr, low_scr, wgrad_scr, sems,
):
    length, width = hid_ref.shape
    rows = carry_ref.shape[0]
    pairs, parts, depth = w_ref.shape[:3]
    own_blocks = rows // BLOCK
    blocks = length // BLOCK
    my = me_ref[0]
    own = pl.multiple_of(my * rows, rows)
    own_block = pl.multiple_of(my * own_blocks, own_blocks)
    lower = iota((1, 128), 1) < HD
    take = GROUP * BLOCK
    copies = load_weights((w0_ref, w1_ref, w2_ref, w3_ref), w_ref, sems)

    dy = keep_ref[0].astype(F32) + near_ref[0].astype(F32) + far_ref[...].astype(F32)
    back, pair = norm_back(dy, above_ref[...], gain_above_ref[...])
    pair_above_out[...] = pair
    upstream = carry_ref[...] + back
    carry_out[...] = upstream
    low_scr[...] = upstream.astype(BF)
    acc_scr[...] = jnp.zeros_like(acc_scr)
    for copy in copies:
        copy.wait()

    def put(j, columns, value):
        size = columns[1] - columns[0]
        wgrad_scr[j, :, :, columns[0]:columns[1]] = value.astype(BF).reshape(parts, depth, size)

    def feed(j, _):
        low = low_scr[...]
        w_dn = w_ref[j, :, :, C_DOWN[0]:C_DOWN[1]].reshape(width, 512)
        grad_act = dot_nn(low, w_dn)
        x = upw_ref[j]
        squared = x * x
        bent = jnp.tanh(GELU_C * (x + GELU_A * squared * x))
        slope = 0.5 * (1.0 + bent) + 0.5 * x * (1.0 - bent * bent) * (
            GELU_C * (1.0 + 3.0 * GELU_A * squared)
        )
        grad_up = (grad_act * slope).astype(BF)
        put(j, C_DOWN, dot_tn(low, act_ref[j]))
        put(j, C_UP, dot_tn(hid2_ref[...], grad_up))
        w_up = w_ref[j, :, :, C_UP[0]:C_UP[1]].reshape(width, 512)
        acc_scr[...] += dot_nt(grad_up, w_up)
        return 0

    lax.fori_loop(0, pairs, feed, 0)

    back, pair = norm_back(acc_scr[...], mid_ref[...], gain_two_ref[...])
    pair_two_out[...] = pair
    upstream = carry_out[...] + back
    carry_out[...] = upstream
    low_scr[...] = upstream.astype(BF)
    dperm_scr[...] = jnp.zeros_like(dperm_scr)
    scale_key = 1.0 / math.sqrt(HD)

    def attend(j, _):
        low = low_scr[...]
        w_o = w_ref[j, :, :, C_OUT[0]:C_OUT[1]].reshape(width, 128)
        grad_mixed = dot_nn(low, w_o).astype(BF)
        put(j, C_OUT, dot_tn(low, mixed_ref[j]))
        q = q_ref[j]
        zero = jnp.zeros_like(q)
        queries = []
        for h in range(2):
            key_lanes = lower if h == 0 else ~lower
            kron = kron_rows(permo_ref[2 * j + h], length)
            kv_all = kv_ref[j, :, h * 128:(h + 1) * 128]
            kv_own = kv_ref[j, pl.ds(own, rows), h * 128:(h + 1) * 128]
            skv = skv_ref[j, h]
            q_mine = jnp.where(key_lanes, q, zero)
            gm_mine = jnp.where(key_lanes, zero, grad_mixed)
            scale = jnp.where(key_lanes, scale_key, 1.0)
            gq, g_sorted, g_own = [], [], []
            for g in range(rows // take):
                cut = slice(g * take, (g + 1) * take)
                kv_set = jnp.concatenate([skv[cut], kv_own[cut]], 0)
                share = attw_ref[j, h, cut, :]
                grad_share = dot_nt(gm_mine[cut], kv_set)
                grad_raw = (
                    share * (grad_share - jnp.sum(share * grad_share, -1, keepdims=True))
                ).astype(BF)
                gq.append(dot_nn(grad_raw, kv_set) * scale_key)
                grad_set = (
                    dot_tn(grad_raw, q_mine[cut]) + dot_tn(share.astype(BF), gm_mine[cut])
                ) * scale
                g_sorted.append(grad_set[:take])
                g_own.append(grad_set[take:])
            queries.append(jnp.concatenate(gq, 0))
            grad_sorted = jnp.concatenate(g_sorted, 0).astype(BF)
            crossed = dot_nt(grad_sorted, kv_all)
            same = (iota((rows, length), 0) & (BLOCK - 1)) == (iota((rows, length), 1) & (BLOCK - 1))
            crossed = jnp.where(same, crossed, 0.0).reshape(own_blocks, BLOCK, length)
            dperm_scr[2 * j + h] = jnp.sum(crossed, 1)
            ghid_scr[:, 0:128] = dot_tn(kron, grad_sorted)
            ghid_scr[pl.ds(own, rows), 0:128] += jnp.concatenate(g_own, 0)
            gkv_scr[j, :, h * 128:(h + 1) * 128] = ghid_scr[:, 0:128].astype(BF)
        gq_scr[j] = jnp.where(lower, queries[0], queries[1]).astype(BF)
        return 0

    lax.fori_loop(0, pairs, attend, 0)

    heads = 2 * pairs
    gather = (iota((length, blocks), 0) // BLOCK == iota((length, blocks), 1)).astype(F32)
    dperm = lax.dot_general(
        dperm_scr[...].reshape(heads * own_blocks, length),
        gather,
        (((1,), (0,)), ((), ())),
        precision=lax.Precision.HIGHEST,
        preferred_element_type=F32,
    ).reshape(heads, own_blocks, blocks)
    scores = jnp.stack(
        [sort_ref[h // 2][:, (h % 2) * BLOCK:(h % 2) * BLOCK + blocks] for h in range(heads)]
    )
    full = jnp.concatenate([dperm] * (blocks // own_blocks), 1)
    block_at = iota(full.shape, 1)
    full = jnp.where((block_at >= own_block) & (block_at < own_block + own_blocks), full, 0.0)
    grad_sort = balance_back(scores, full) / math.sqrt(BLOCK)
    blank = jnp.zeros((blocks, 128 - 2 * blocks), F32)
    for j in range(pairs):
        gsrt_scr[j] = jnp.concatenate([grad_sort[2 * j], grad_sort[2 * j + 1], blank], 1)

    ghid_scr[...] = jnp.zeros_like(ghid_scr)

    def inward(j, _):
        w = w_ref[j, :, :, C_KVS[0]:C_KVS[1]].reshape(width, C_KVS[1] - C_KVS[0])
        spread = jnp.broadcast_to(gsrt_scr[j][:, None, :], (blocks, BLOCK, 128)).reshape(length, 128)
        grad = jnp.concatenate([gkv_scr[j], spread.astype(BF)], 1)
        put(j, C_KVS, dot_tn(hid_ref[...], grad))
        ghid_scr[...] += dot_nt(grad, w)
        wq = w_ref[j, :, :, C_Q[0]:C_Q[1]].reshape(width, 128)
        put(j, C_Q, dot_tn(hid_ref[pl.ds(own, rows), :], gq_scr[j]))
        ghid_scr[pl.ds(own, rows), :] += dot_nt(gq_scr[j], wq)
        return 0

    lax.fori_loop(0, pairs, inward, 0)
    for p in range(pairs):
        out = gsend_out if p & 1 else gkeep_out
        at = pl.multiple_of((my ^ p) * rows, rows)
        out[p >> 1] = ghid_scr[pl.ds(at, rows), :].astype(BF)
    outs = []
    for p in range(pairs):
        out = wsend_out if p & 1 else wkeep_out
        outs.append(pltpu.make_async_copy(wgrad_scr.at[p], out.at[p >> 1], sems.at[p]))
        outs[p].start()
    for copy in outs:
        copy.wait()


def layer_backward(me, dy, above, carry, gain_above, weights, gain_two, kept, after=()):
    rows, width = carry.shape
    pairs = len(weights)
    length = rows * pairs
    own_blocks, blocks = rows // BLOCK, length // BLOCK
    shape = jax.ShapeDtypeStruct
    outs = [
        shape((pairs // 2, rows, width), BF),
        shape((pairs // 2, rows, width), BF),
        shape((pairs // 2,) + weights[0].shape, BF),
        shape((pairs // 2,) + weights[0].shape, BF),
        shape((rows, width), F32),
        shape((2, width), F32),
        shape((2, width), F32),
    ]
    vm = pl.BlockSpec(memory_space=pltpu.VMEM)
    far = pl.BlockSpec(memory_space=pl.ANY)
    return pl.pallas_call(
        ignore_tail(backward_kernel, 8 + pairs + len(kept), len(after)),
        out_shape=outs,
        in_specs=[pl.BlockSpec(memory_space=pltpu.SMEM)] + [vm] * 6 + [far] * pairs
        + [vm] * (1 + len(kept)) + [far] * len(after),
        out_specs=[vm, vm, far, far, vm, vm, vm],
        scratch_shapes=[
            pltpu.VMEM((pairs,) + weights[0].shape, BF),
            pltpu.VMEM((rows, width), F32),
            pltpu.VMEM((length, width), F32),
            pltpu.VMEM((pairs, length, 256), BF),
            pltpu.VMEM((pairs, blocks, 128), F32),
            pltpu.VMEM((pairs, rows, 128), BF),
            pltpu.VMEM((2 * pairs, own_blocks, length), F32),
            pltpu.VMEM((rows, width), BF),
            pltpu.VMEM((pairs,) + weights[0].shape, BF),
            pltpu.SemaphoreType.DMA((pairs,)),
        ],
        compiler_params=pltpu.CompilerParams(vmem_limit_bytes=VMEM_LIMIT),
        cost_estimate=pl.CostEstimate(flops=30_000_000_000, bytes_accessed=25_000_000, transcendentals=0),
        name="layer_backward",
    )(me, *dy, above, carry, gain_above, *weights, gain_two, *kept, *after)


def embed_kernel(base_ref, tok_ref, table_ref, out_ref, tall_ref):
    features, vocab = table_ref.shape
    count = out_ref.shape[1]
    bins = vocab // 256

    @pl.when(pl.program_id(0) == 0)
    def _():
        for at in range(bins):
            tall_ref[at * features:(at + 1) * features, :] = table_ref[:, at * 256:(at + 1) * 256]

    local = tok_ref[...] - base_ref[0]
    high, low = local >> 8, local & 255
    hot = (iota((256, count), 0) == low).astype(BF)
    found = dot_nn(tall_ref[...], hot)
    total = jnp.zeros((features, count), F32)
    for at in range(bins):
        total = jnp.where(high == at, found[at * features:(at + 1) * features, :], total)
    out_ref[...] = total.astype(BF)


def embed_lookup(base, tokens, table):
    features, vocab = table.shape
    count = tokens.shape[1]
    tile = 512
    return pl.pallas_call(
        embed_kernel,
        grid=(count // tile,),
        out_shape=jax.ShapeDtypeStruct((features, count), BF),
        in_specs=[
            pl.BlockSpec(memory_space=pltpu.SMEM),
            pl.BlockSpec((1, tile), lambda i: (0, i)),
            pl.BlockSpec((features, vocab), lambda i: (0, 0)),
        ],
        out_specs=pl.BlockSpec((features, tile), lambda i: (0, i)),
        scratch_shapes=[pltpu.VMEM((features * (vocab // 256), 256), BF)],
        compiler_params=pltpu.CompilerParams(vmem_limit_bytes=VMEM_LIMIT),
        cost_estimate=pl.CostEstimate(flops=15_000_000_000, bytes_accessed=4_000_000, transcendentals=0),
        name="embed_lookup",
    )(base, tokens, table)


def embed_back_kernel(base_ref, tok_ref, grad_ref, out_ref, acc_ref):
    features = grad_ref.shape[0]
    count = grad_ref.shape[1]
    bins = acc_ref.shape[0] // features
    step = pl.program_id(0)
    local = tok_ref[...] - base_ref[0]
    high, low = local >> 8, local & 255
    hot = (iota((256, count), 0) == low).astype(BF)
    grad = grad_ref[...]
    wide = jnp.concatenate(
        [jnp.where(high == at, grad, jnp.zeros_like(grad)) for at in range(bins)], 0
    )
    found = dot_nt(wide, hot)

    @pl.when(step == 0)
    def _():
        acc_ref[...] = found

    @pl.when(step > 0)
    def _():
        acc_ref[...] += found

    @pl.when(step == pl.num_programs(0) - 1)
    def _():
        for at in range(bins):
            out_ref[:, at * 256:(at + 1) * 256] = acc_ref[at * features:(at + 1) * features, :]


def embed_back(base, tokens, grad, vocab):
    pieces, features, tile = grad.shape
    return pl.pallas_call(
        embed_back_kernel,
        grid=(pieces,),
        out_shape=jax.ShapeDtypeStruct((features, vocab), F32),
        in_specs=[
            pl.BlockSpec(memory_space=pltpu.SMEM),
            pl.BlockSpec((1, tile), lambda i: (0, i)),
            pl.BlockSpec((None, features, tile), lambda i: (i, 0, 0)),
        ],
        out_specs=pl.BlockSpec((features, vocab), lambda i: (0, 0)),
        scratch_shapes=[pltpu.VMEM((features * (vocab // 256), 256), F32)],
        compiler_params=pltpu.CompilerParams(vmem_limit_bytes=VMEM_LIMIT),
        cost_estimate=pl.CostEstimate(flops=15_000_000_000, bytes_accessed=4_000_000, transcendentals=0),
        name="embed_back",
    )(base, tokens, grad)


def start_kernel(raw_ref, nrm_ref, stream_out, hid_out, *, scale):
    stream = raw_ref[...].astype(F32).T * scale
    stream_out[...] = stream
    hid_out[...] = norm_apply(stream, nrm_ref[0:1, :], nrm_ref[1:2, :])


def start_stream(raw, nrm):
    width, rows = raw.shape
    return pl.pallas_call(
        functools.partial(start_kernel, scale=math.sqrt(width)),
        out_shape=[
            jax.ShapeDtypeStruct((rows, width), F32),
            jax.ShapeDtypeStruct((rows, width), BF),
        ],
        name="start_stream",
    )(raw, nrm)


def finish_kernel(keep_ref, near_ref, far_ref, above_ref, carry_ref, gain_ref, grad_out, pair_out):
    dy = keep_ref[0].astype(F32) + near_ref[0].astype(F32) + far_ref[...].astype(F32)
    back, pair = norm_back(dy, above_ref[...], gain_ref[...])
    pair_out[...] = pair
    grad_out[...] = (carry_ref[...] + back).T.astype(BF)


def finish_stream(dy, above, carry, gain, after=()):
    rows, width = above.shape
    vm = pl.BlockSpec(memory_space=pltpu.VMEM)
    return pl.pallas_call(
        ignore_tail(finish_kernel, 6, len(after)),
        in_specs=[vm] * 6 + [pl.BlockSpec(memory_space=pl.ANY)] * len(after),
        out_shape=[
            jax.ShapeDtypeStruct((width, rows), BF),
            jax.ShapeDtypeStruct((2, width), F32),
        ],
        name="finish_stream",
    )(*dy, above, carry, gain, *after)


def to_lanes(column):
    return jnp.broadcast_to(column, (column.shape[0], 128)).T[0:1, :]


def to_rows(line):
    return jnp.broadcast_to(line, (128, line.shape[1])).T[:, 0:1]


def head_stats_kernel(table_ref, final_ref, goal_ref, stat_out):
    logits = dot_nn(final_ref[...], table_ref[...])
    top = jnp.max(logits, 1, keepdims=True)
    total = jnp.sum(jnp.exp(logits - top), 1, keepdims=True)
    hit = iota(logits.shape, 1) == goal_ref[...]
    pick = jnp.sum(jnp.where(hit, logits, 0.0), 1, keepdims=True)
    stat_out[0:1, :] = to_lanes(top)
    stat_out[1:2, :] = to_lanes(total)
    stat_out[2:3, :] = to_lanes(pick)


def head_stats(table, final_all, goals):
    width, vocab = table.shape
    count = final_all.shape[0]
    tile = 256
    return pl.pallas_call(
        head_stats_kernel,
        grid=(count // tile,),
        out_shape=jax.ShapeDtypeStruct((3, count), F32),
        in_specs=[
            pl.BlockSpec((width, vocab), lambda i: (0, 0)),
            pl.BlockSpec((tile, width), lambda i: (i, 0)),
            pl.BlockSpec((tile, 1), lambda i: (i, 0)),
        ],
        out_specs=pl.BlockSpec((3, tile), lambda i: (0, i)),
        compiler_params=pltpu.CompilerParams(vmem_limit_bytes=VMEM_LIMIT),
        cost_estimate=pl.CostEstimate(flops=16_000_000_000, bytes_accessed=6_000_000, transcendentals=0),
        name="head_stats",
    )(table, final_all, goals)


def head_back_kernel(table_ref, final_ref, goal_ref, line_ref, gfin_out, gtab_out, acc_ref):
    step = pl.program_id(0)
    logits = dot_nn(final_ref[...], table_ref[...])
    hit = iota(logits.shape, 1) == goal_ref[...]
    chance = jnp.exp(logits - to_rows(line_ref[0:1, :]))
    grad = ((chance - jnp.where(hit, 1.0, 0.0)) * to_rows(line_ref[1:2, :])).astype(BF)
    gfin_out[...] = dot_nt(grad, table_ref[...]).astype(BF)
    part = dot_tn(final_ref[...], grad)

    @pl.when(step == 0)
    def _():
        acc_ref[...] = part

    @pl.when(step > 0)
    def _():
        acc_ref[...] += part

    @pl.when(step == pl.num_programs(0) - 1)
    def _():
        gtab_out[...] = acc_ref[...].astype(BF)


def head_back(table, final_all, goals, lines):
    width, vocab = table.shape
    count = final_all.shape[0]
    tile = 256
    return pl.pallas_call(
        head_back_kernel,
        grid=(count // tile,),
        out_shape=[
            jax.ShapeDtypeStruct((count, width), BF),
            jax.ShapeDtypeStruct((width, vocab), BF),
        ],
        in_specs=[
            pl.BlockSpec((width, vocab), lambda i: (0, 0)),
            pl.BlockSpec((tile, width), lambda i: (i, 0)),
            pl.BlockSpec((tile, 1), lambda i: (i, 0)),
            pl.BlockSpec((2, tile), lambda i: (0, i)),
        ],
        out_specs=[
            pl.BlockSpec((tile, width), lambda i: (i, 0)),
            pl.BlockSpec((width, vocab), lambda i: (0, 0)),
        ],
        scratch_shapes=[pltpu.VMEM((width, vocab), F32)],
        compiler_params=pltpu.CompilerParams(vmem_limit_bytes=VMEM_LIMIT),
        cost_estimate=pl.CostEstimate(flops=35_000_000_000, bytes_accessed=14_000_000, transcendentals=0),
        name="head_back",
    )(table, final_all, goals, lines)


def swap(value, axis, bit):
    return lax.ppermute(value, axis, [(at, at ^ bit) for at in range(lax.axis_size(axis))])


def has_bit(axis, bit):
    return (lax.axis_index(axis) & bit) != 0


def bits_of(axis):
    size = lax.axis_size(axis)
    return [1 << at for at in reversed(range(size.bit_length() - 1))]


def in_order(mine, other, axis, bit, dim):
    flag = has_bit(axis, bit)
    return jnp.concatenate([jnp.where(flag, other, mine), jnp.where(flag, mine, other)], dim)


def gather_dp(value):
    bits = bits_of("dp")
    whole = value.reshape((1,) * len(bits) + value.shape)
    for dim, bit in enumerate(bits):
        whole = in_order(whole, swap(whole, "dp", bit), "dp", bit, dim)
    return whole.reshape((-1,) + value.shape)


def scatter_dp(value):
    bits = bits_of("dp")
    value = value.reshape((2,) * len(bits) + value.shape[1:])
    for dim, bit in reversed(list(enumerate(bits))):
        flag = has_bit("dp", bit).astype(jnp.int32)
        low = value.astype(BF)
        other = swap(lax.dynamic_index_in_dim(low, 1 - flag, dim, False), "dp", bit)
        mine = lax.dynamic_index_in_dim(low, flag, dim, False)
        value = mine.astype(F32) + other.astype(F32)
    return value


def sum_all(value, combine=jnp.add):
    for axis in ("head", "dp"):
        for bit in reversed(bits_of(axis)):
            value = combine(value, swap(value, axis, bit))
    return value


def pieces_of_head(value):
    across = swap(value, "head", 2)
    return value, swap(value, "head", 1), across, swap(across, "head", 1)


def settle_head(keep, send):
    near = swap(send, "head", 1)
    across = (keep[1].astype(F32) + near[1].astype(F32)).astype(BF)
    return keep, near, swap(across, "head", 2)


def pack_weights(attn_in, attn_out, ffn_up, ffn_down):
    features = attn_in.shape[0]
    low = attn_in.astype(BF)
    q, k, v = low[..., :HD], low[..., HD:2 * HD], low[..., 2 * HD:3 * HD]
    s = low[..., 3 * HD:].reshape(features, -1)
    blank = jnp.zeros((features, 128 - s.shape[1]), BF)
    out = attn_out.astype(BF)
    out = jnp.concatenate([out[1], out[0]], 0).T
    return jnp.concatenate(
        [
            q[:, 0], q[:, 1], k[:, 0], v[:, 0], v[:, 1], k[:, 1], s, blank,
            out, ffn_up.astype(BF), ffn_down.astype(BF).T,
        ],
        1,
    )


def unpack_grads(packed, sort_width):
    def cut(at, size=HD):
        return packed[:, at:at + size]

    kv = C_KVS[0]
    srt = kv + 256
    first = jnp.concatenate([cut(0), cut(kv), cut(kv + 64), cut(srt, sort_width)], 1)
    second = jnp.concatenate(
        [cut(64), cut(kv + 192), cut(kv + 128), cut(srt + sort_width, sort_width)], 1
    )
    out = packed[:, C_OUT[0]:C_OUT[1]].T
    return (
        jnp.stack([first, second], 1),
        jnp.stack([out[HD:], out[:HD]], 0),
        packed[:, C_UP[0]:C_UP[1]],
        packed[:, C_DOWN[0]:C_DOWN[1]].T,
    )


class Gather:
    def __init__(self, packed):
        whole = gather_dp(packed)
        self.mine = whole.reshape(-1, max(64, packed.shape[0]), packed.shape[1])

    def finish(self):
        return pieces_of_head(self.mine)


class Scatter:
    def __init__(self, keep, send, features):
        self.keep, self.features = keep, features
        self.near = swap(send, "head", 1)
        self.pair = (keep[1].astype(F32) + self.near[1].astype(F32)).astype(BF)
        self.across = swap(self.pair, "head", 2)

    def finish(self):
        whole = self.keep[0].astype(F32) + self.near[0].astype(F32) + self.across.astype(F32)
        return scatter_dp(whole.reshape(-1, self.features, whole.shape[-1]))


def adamw(weight, gradient, moment_one, moment_two, factor, step_rate):
    gradient = gradient * factor
    moment_one = BETA_ONE * moment_one + (1.0 - BETA_ONE) * gradient
    moment_two = BETA_TWO * moment_two + (1.0 - BETA_TWO) * gradient * gradient
    adam_step = (
        moment_one
        / (1.0 - BETA_ONE**STEP)
        / (jnp.sqrt(moment_two / (1.0 - BETA_TWO**STEP)) + ADAM_FLOOR)
    )
    return (weight - step_rate * (adam_step + WEIGHT_DECAY * weight), moment_one, moment_two)


def body(
    tokens, targets, lengths,
    table, table_first, table_second,
    attn_in, attn_in_first, attn_in_second,
    attn_out, attn_out_first, attn_out_second,
    ffn_up, ffn_up_first, ffn_up_second,
    ffn_down, ffn_down_first, ffn_down_second,
    norms, norms_first, norms_second,
):
    dp, head = lax.axis_size("dp"), lax.axis_size("head")
    my_dp, my_head = lax.axis_index("dp"), lax.axis_index("head")
    seq_count, length = tokens.shape
    features, vocab = table.shape
    width = features * dp
    layers = attn_in.shape[0]
    rows = length // head
    total = dp * length
    me = my_head.astype(jnp.int32).reshape(1)
    odd = my_dp & 1
    outer = [[at for at in range(dp) if at % 2 == way] for way in range(2)]

    lines = jnp.concatenate([tokens, targets, jnp.broadcast_to(lengths[:, None], (seq_count, 128))], 1)
    lines = gather_dp(lines.reshape(-1))
    all_tokens = lines[:, :length].reshape(1, total)
    positions = jnp.arange(length, dtype=jnp.int32)
    counted = (positions[None, :] < lines[:, 2 * length:2 * length + 1]).astype(F32)
    nrm = norms
    for bit in (1, 2):
        nrm = in_order(nrm, swap(nrm, "head", bit), "head", bit, 2)

    low_table = table.astype(BF)
    gathers = [
        Gather(pack_weights(attn_in[at], attn_out[at], ffn_up[at], ffn_down[at]))
        for at in range(layers)
    ]
    weights = [one.finish() for one in gathers]

    half = vocab // 2
    other = swap(lax.dynamic_slice_in_dim(low_table, (1 - odd) * half, half, 1), "dp", 1)
    mine = lax.dynamic_slice_in_dim(low_table, odd * half, half, 1)
    head_table = lax.all_gather(
        in_order(mine, other, "dp", 1, 0), "dp", axis=0, tiled=True, axis_index_groups=outer
    )

    base = (my_head * vocab).astype(jnp.int32).reshape(1)
    found = embed_lookup(base, all_tokens, low_table).reshape(features, dp, head, rows)
    for bit in (1, 2):
        flag = (my_head & bit) // bit
        found = found.reshape(features, dp, -1, 2, rows) if bit == 1 else found.reshape(features, dp, 2, rows)
        dim = 3 if bit == 1 else 2
        other = swap(lax.dynamic_index_in_dim(found, 1 - flag, dim, False), "head", bit)
        found = lax.dynamic_index_in_dim(found, flag, dim, False) + other
    found = lax.all_to_all(found, "dp", split_axis=1, concat_axis=0, tiled=True)
    stream, hidden = start_stream(found.reshape(width, rows), nrm[0])

    kept = []
    for at in range(layers):
        pairs_now = jnp.concatenate([nrm[2 * at + 1], nrm[2 * at + 2]], 0)
        after = tuple(one.mine for one in gathers[at + 1:at + 2])
        got = layer_forward(me, pieces_of_head(hidden), stream, weights[at], pairs_now, after)
        kept.append((stream, (got[1],) + tuple(got[3:])))
        stream, hidden = got[0], got[2]

    def spread_rows(value):
        for axis, bit in (("dp", 1), ("head", 2), ("head", 1)):
            value = jnp.stack([value, swap(value, axis, bit)])
        return value

    def line_of(values):
        values = values.reshape(dp, head, rows)
        order = [(my_dp ^ y, my_head ^ (x * 2 + c)) for c in range(2) for x in range(2) for y in range(2)]
        picked = [
            lax.dynamic_slice(values, (d, h, 0), (1, 1, rows)).reshape(rows) for d, h in order
        ]
        return jnp.concatenate(picked)

    final_all = spread_rows(hidden).reshape(-1, width)
    goals = line_of(lines[:, length:2 * length]) - (my_head * vocab + odd * half).astype(jnp.int32)
    goals = goals.reshape(-1, 1)
    counted_here = line_of(counted)
    stats = head_stats(head_table, final_all, goals)
    for dim, (axis, bit) in enumerate((("head", 1), ("head", 2), ("dp", 1))):
        theirs = swap(stats, axis, bit).reshape(3, 2, 2, 2, rows)
        theirs = jnp.flip(theirs, dim + 1).reshape(stats.shape)
        peak = jnp.maximum(stats[0], theirs[0])
        sums = stats[1] * jnp.exp(stats[0] - peak) + theirs[1] * jnp.exp(theirs[0] - peak)
        stats = jnp.stack([peak, sums, stats[2] + theirs[2]])
    lse = stats[0] + jnp.log(stats[1])
    loss_here = jnp.sum((lse - stats[2]) * counted_here) / (2 * head)
    count_total = jnp.sum(counted)
    grad_final, grad_half = head_back(head_table, final_all, goals, jnp.stack([lse, counted_here]))
    grad_final = grad_final.reshape(2, 2, 2, rows, width)
    near = swap(grad_final[1], "head", 1)
    summed = grad_final[0].astype(F32) + near.astype(F32)
    across = swap(summed[1].astype(BF), "head", 2)
    summed = summed[0] + across.astype(F32)
    far = swap(summed[1].astype(BF), "dp", 1)
    nothing = jnp.zeros((1, rows, width), BF)
    dy = (summed[0:1], nothing, far)
    grad_half = lax.psum_scatter(
        grad_half, "dp", scatter_dimension=0, tiled=True, axis_index_groups=outer
    ).reshape(2, features, half)
    other = swap(lax.dynamic_index_in_dim(grad_half, 1 - odd, 0, False), "dp", 1)
    mine = lax.dynamic_index_in_dim(grad_half, odd, 0, False)
    grad_table = in_order(mine, other, "dp", 1, 1).astype(F32)

    carry = jnp.zeros((rows, width), F32)
    above = stream
    pair_grads = [None] * (2 * layers + 1)
    scatters = []
    for at in reversed(range(layers)):
        stream_in, rest = kept[at]
        after = [one.pair for one in scatters[-1:]] + [one.across for one in scatters[-2:-1]]
        if at == 0:
            after.append(grad_half)
        gkeep, gsend, wkeep, wsend, carry, pair_above, pair_two = layer_backward(
            me, dy, above, carry, nrm[2 * at + 2, 0:1], weights[at], nrm[2 * at + 1, 0:1], rest, after
        )
        pair_grads[2 * at + 2] = pair_above
        pair_grads[2 * at + 1] = pair_two
        dy = settle_head(gkeep, gsend)
        scatters.append(Scatter(wkeep, wsend, features))
        above = stream_in
    packed_grads = [one.finish() for one in reversed(scatters)]
    after = [scatters[-1].pair, scatters[-2].across, packed_grads[-1]]
    grad_stream, pair_grads[0] = finish_stream(dy, above, carry, nrm[0, 0:1], after)

    spread = lax.all_to_all(
        grad_stream.reshape(dp, features, rows), "dp", split_axis=0, concat_axis=0, tiled=True
    )
    spread = in_order(spread[:, None], swap(spread[:, None], "head", 1), "head", 1, 1)[:, None]
    spread = in_order(spread, swap(spread, "head", 2), "head", 2, 1)
    spread = spread.reshape(dp * head, features, rows)
    grad_table = grad_table + math.sqrt(width) * embed_back(base, all_tokens, spread, vocab)

    grad_norms = sum_all(jnp.stack(pair_grads))
    grad_norms = lax.dynamic_slice_in_dim(grad_norms, my_head * norms.shape[2], norms.shape[2], 2)
    sort_width = attn_in.shape[3] - 3 * HD
    layer_grads = [unpack_grads(packed, sort_width) for packed in packed_grads]
    grad_in, grad_out, grad_up, grad_down = (
        jnp.stack([one[member] for one in layer_grads]) for member in range(4)
    )
    squares = jnp.sum(grad_table * grad_table) + jnp.sum(grad_norms * grad_norms) / dp
    for packed in packed_grads:
        squares = squares + jnp.sum(packed * packed)
    totals = sum_all(jnp.stack([squares, loss_here]))
    grad_norm = jnp.sqrt(totals[0])
    loss_total = totals[1]
    factor = jnp.minimum(1.0, CLIP_LIMIT / (grad_norm + 1e-06))

    results = [jnp.stack([loss_total, count_total]), grad_norm]
    for weight, gradient, first, second in (
        (table, grad_table, table_first, table_second),
        (attn_in, grad_in, attn_in_first, attn_in_second),
        (attn_out, grad_out, attn_out_first, attn_out_second),
        (ffn_up, grad_up, ffn_up_first, ffn_up_second),
        (ffn_down, grad_down, ffn_down_first, ffn_down_second),
    ):
        new, one, two = adamw(weight, gradient, first, second, factor, RATE_MATRIX)
        results += [new, new.astype(BF), one, two]
    results += list(adamw(norms, grad_norms, norms_first, norms_second, factor, RATE_NORM))
    return tuple(results)


def solution(mesh):
    ints = [P("dp", None), P("dp", None), P("dp")]
    by_table = P("dp", "head")
    by_in = P(None, "dp", "head", None)
    by_out = P(None, "head", None, "dp")
    by_up = P(None, "dp", "head")
    by_down = P(None, "head", "dp")
    by_norm = P(None, None, "head")
    in_specs, out_specs = list(ints), [P(), P()]
    for spec in (by_table, by_in, by_out, by_up, by_down):
        in_specs += [spec] * 3
        out_specs += [spec] * 4
    in_specs += [by_norm] * 3
    out_specs += [by_norm] * 3
    return jax.shard_map(
        body, mesh=mesh, in_specs=tuple(in_specs), out_specs=tuple(out_specs), check_vma=False
    )
```

```python
import functools
import math

import jax
import jax.numpy as jnp
from jax import lax
from jax.experimental import pallas as pl
from jax.experimental.pallas import tpu as pltpu
from jax.sharding import PartitionSpec as P

HD = 64
BLOCK = 32
SINK = 8
STEP = 10
EPSILON = 1e-05
NEGATIVE = -1000000000.0
TEMPER = 0.75
BETA_ONE = 0.9
BETA_TWO = 0.999
ADAM_FLOOR = 1e-08
WEIGHT_DECAY = 0.01
RATE_MATRIX = 0.1
RATE_NORM = 0.5
CLIP_LIMIT = 1.0

BF = jnp.bfloat16
F32 = jnp.float32
GROUP = 2
GELU_C = math.sqrt(2.0 / math.pi)
GELU_A = 0.044715

C_Q = (0, 128)
C_KVS = (128, 512)
C_OUT = (512, 640)
ATTN = 640
C_UP = (0, 512)
C_DOWN = (512, 1024)
FEED = 1024
VMEM_LIMIT = 56 * 1024 * 1024


def dot_nn(a, b):
    return lax.dot_general(a, b, (((1,), (0,)), ((), ())), preferred_element_type=F32)


def dot_nt(a, b):
    return lax.dot_general(a, b, (((1,), (1,)), ((), ())), preferred_element_type=F32)


def dot_tn(a, b):
    return lax.dot_general(a, b, (((0,), (0,)), ((), ())), preferred_element_type=F32)


def iota(shape, axis):
    return lax.broadcasted_iota(jnp.int32, shape, axis)


MESH = pl.DeviceIdType.MESH


def flipped(axis, bit):
    mine = lax.axis_index(axis)
    return mine + bit - 2 * bit * ((mine // bit) % 2)


def call(kernel, outs, in_specs, out_specs, operands, after=(), flows=(), ident=0, **options):
    used, spare, token, riders = len(operands), len(after), len(outs), len(flows)
    asks = [flow.ask for flow in flows]
    pairs = sorted({ask[1:] for ask in asks})
    grid = options.get("grid")
    scratch = list(options.pop("scratch_shapes", []))
    far = pl.BlockSpec(memory_space=pl.ANY)

    def run(*refs):
        ins, rest = refs[:used], refs[used + spare:]
        sends, rest = rest[:riders], rest[riders:]
        results, token_ref, rest = rest[:token], rest[token], rest[token + 1:]
        lands, rest = rest[:riders], rest[riders:]
        if riders:
            rest, (send_sems, recv_sems) = rest[:-2], rest[-2:]

        def copies():
            return [
                pltpu.make_async_remote_copy(
                    src_ref=sends[at],
                    dst_ref=lands[at],
                    send_sem=send_sems.at[at],
                    recv_sem=recv_sems.at[at],
                    device_id={axis: flipped(axis, bit)},
                    device_id_type=MESH,
                )
                for at, (_, axis, bit) in enumerate(asks)
            ]

        def launch():
            barrier = pltpu.get_barrier_semaphore()
            for axis, bit in pairs:
                pl.semaphore_signal(
                    barrier, inc=1, device_id={axis: flipped(axis, bit)}, device_id_type=MESH
                )
            pl.semaphore_wait(barrier, len(pairs))
            for copy in copies():
                copy.start()

        def settle():
            for copy in copies():
                copy.wait()

        if riders:
            pl.when(pl.program_id(0) == 0)(launch) if grid else launch()
        token_ref[...] = jnp.zeros((1, 128), F32)
        kernel(*ins, *results, *rest)
        if riders:
            pl.when(pl.program_id(0) == grid[0] - 1)(settle) if grid else settle()

    if riders:
        options["compiler_params"] = pltpu.CompilerParams(
            vmem_limit_bytes=VMEM_LIMIT, collective_id=ident, has_side_effects=True
        )
        scratch += [pltpu.SemaphoreType.DMA((riders,))] * 2
    token_spec = (
        pl.BlockSpec((1, 128), lambda i: (0, 0)) if grid else pl.BlockSpec(memory_space=pltpu.VMEM)
    )
    got = pl.pallas_call(
        run,
        out_shape=list(outs)
        + [jax.ShapeDtypeStruct((1, 128), F32)]
        + [jax.ShapeDtypeStruct(ask[0].shape, ask[0].dtype) for ask in asks],
        in_specs=list(in_specs) + [far] * (spare + riders),
        out_specs=list(out_specs) + [token_spec] + [far] * riders,
        scratch_shapes=scratch,
        **options,
    )(*operands, *after, *[ask[0] for ask in asks])
    for flow, value in zip(flows, got[token + 1:]):
        flow.give(value)
    return (*got[:token], got[token][0, 0])


class Flow:
    def __init__(self, steps):
        self.steps, self.value = steps, None
        self.give(None)

    def give(self, got):
        try:
            self.ask = self.steps.send(got)
        except StopIteration as stop:
            self.ask, self.value = None, stop.value

    def finish(self):
        while self.ask is not None:
            self.give(swap(*self.ask))
        return self.value


def norm_stats(stream):
    average = jnp.mean(stream, -1, keepdims=True)
    variance = jnp.mean(stream * stream, -1, keepdims=True) - average * average
    inv_std = lax.rsqrt(variance + EPSILON)
    return (stream - average) * inv_std, inv_std


def norm_apply(stream, gain, bias):
    normed, _ = norm_stats(stream)
    return (normed * gain + bias).astype(BF)


def norm_back(upstream, stream, gain):
    normed, inv_std = norm_stats(stream)
    scaled = upstream * gain
    back = inv_std * (
        scaled
        - jnp.mean(scaled, -1, keepdims=True)
        - normed * jnp.mean(scaled * normed, -1, keepdims=True)
    )
    pair = jnp.concatenate(
        [jnp.sum(upstream * normed, 0, keepdims=True), jnp.sum(upstream, 0, keepdims=True)], 0
    )
    return back, pair


def allowed_mask(shape):
    return iota(shape, len(shape) - 1) < iota(shape, len(shape) - 2)


def log_total(x, axis):
    top = jnp.max(x, axis, keepdims=True)
    return top + jnp.log(jnp.sum(jnp.exp(x - top), axis, keepdims=True))


def balance(scores, keep):
    allowed = allowed_mask(scores.shape)
    plan = jnp.where(allowed, scores / TEMPER, NEGATIVE)
    for _ in range(SINK):
        for axis in (-2, -1):
            plan = jnp.where(allowed, plan - log_total(plan, axis), NEGATIVE)
            if keep is not None:
                keep.append(plan)
    return jnp.where(allowed, jnp.exp(plan), 0.0)


def balance_back(scores, upstream):
    allowed = allowed_mask(scores.shape)
    plans = []
    perm = balance(scores, plans)
    grad = jnp.where(allowed, upstream * perm, 0.0)
    for step in reversed(range(2 * SINK)):
        axis = (-2, -1)[step % 2]
        share = jnp.exp(plans[step])
        grad = jnp.where(allowed, grad - share * jnp.sum(grad, axis, keepdims=True), 0.0)
    return grad / TEMPER


def kron_rows(perm_rows, length):
    own, blocks = perm_rows.shape
    rows = own * BLOCK
    tall = jnp.broadcast_to(perm_rows[:, None, :], (own, BLOCK, blocks)).reshape(rows, blocks)
    spread = (iota((blocks, length), 1) // BLOCK == iota((blocks, length), 0)).astype(BF)
    wide = dot_nn(tall.astype(BF), spread)
    same = (iota((rows, length), 0) & (BLOCK - 1)) == (iota((rows, length), 1) & (BLOCK - 1))
    return jnp.where(same, wide, 0.0).astype(BF)


def group_mask(first_block, rows):
    shape = (rows, 2 * rows)
    row, slot = iota(shape, 0), iota(shape, 1)
    row_block = row // BLOCK
    in_sorted = slot < rows
    place = jnp.where(in_sorted, slot, slot - rows)
    same = (place // BLOCK) == row_block
    sorted_ok = in_sorted & (row_block + first_block >= 1)
    own_ok = (slot >= rows) & (place <= row)
    return same & (sorted_ok | own_ok)


def turned(p):
    mine = lax.axis_index("head")
    low, high = mine % 2, (mine // 2) % 2
    rest = mine - low - 2 * high
    return rest + (1 - low if p & 1 else low) + 2 * (1 - high if p & 2 else high)


def load_weights(sources, columns, layer, w_ref, sems):
    copies = []
    for p in range(w_ref.shape[0]):
        if len(sources) > 1:
            source = sources[p]
        else:
            source = sources[0].at[:, turned(p), layer, :, columns[0]:columns[1]]
        copies.append(pltpu.make_async_copy(source, w_ref.at[p], sems.at[p]))
        copies[p].start()
    return copies


def attend_forward_kernel(layer, count, hid0_ref, hid1_ref, hid2in_ref, hid3_ref, stream_ref, nrm_ref, *refs):
    sources = refs[:count]
    (
        mid_out, hid2_out, hid_ref, kv_out, q_out, skv_out, attw_out, mixed_out, permo_out, sort_out,
        w_ref, perm_scr, acc_scr, sems,
    ) = refs[count:]
    length, width = hid_ref.shape
    rows = stream_ref.shape[0]
    pairs = w_ref.shape[0]
    own_blocks = rows // BLOCK
    blocks = length // BLOCK
    my = lax.axis_index("head")
    own = pl.multiple_of(my * rows, rows)
    own_block = pl.multiple_of(my * own_blocks, own_blocks)
    lower = iota((1, 128), 1) < HD
    copies = load_weights(sources, (0, ATTN), layer, w_ref, sems)
    for p, piece in enumerate((hid0_ref, hid1_ref, hid2in_ref, hid3_ref)):
        hid_ref[pl.ds(pl.multiple_of(turned(p) * rows, rows), rows), :] = piece[...]
    for copy in copies:
        copy.wait()

    def project(step, _):
        j, tile = step // (length // rows), step % (length // rows)
        at = pl.multiple_of(tile * rows, rows)
        w = w_ref[j, :, :, C_KVS[0]:C_KVS[1]].reshape(width, C_KVS[1] - C_KVS[0])
        got = dot_nn(hid_ref[pl.ds(at, rows), :], w)
        kv_out[j, pl.ds(at, rows), :] = got[:, :256].astype(BF)
        sort_out[j, pl.ds(pl.multiple_of(tile * own_blocks, own_blocks), own_blocks), :] = jnp.sum(
            got[:, 256:].reshape(own_blocks, BLOCK, 128), 1
        ) / math.sqrt(BLOCK)
        return 0

    lax.fori_loop(0, pairs * (length // rows), project, 0)

    scores = jnp.stack(
        [sort_out[h // 2][:, (h % 2) * BLOCK:(h % 2) * BLOCK + blocks] for h in range(2 * pairs)]
    )
    perm_scr[...] = balance(scores, None)
    permo_out[...] = perm_scr[:, pl.ds(own_block, own_blocks), :]
    acc_scr[...] = stream_ref[...]
    take = GROUP * BLOCK

    def attend(j, _):
        wq = w_ref[j, :, :, C_Q[0]:C_Q[1]].reshape(width, 128)
        q = dot_nn(hid_ref[pl.ds(own, rows), :], wq).astype(BF)
        q_out[j] = q
        mixes = []
        for h in range(2):
            kron = kron_rows(permo_out[2 * j + h], length)
            skv = dot_nn(kron, kv_out[j, :, h * 128:(h + 1) * 128]).astype(BF)
            skv_out[j, h] = skv
            q_mine = jnp.where(lower if h == 0 else ~lower, q, jnp.zeros_like(q))
            kv_own = kv_out[j, pl.ds(own, rows), h * 128:(h + 1) * 128]
            pieces = []
            for g in range(rows // take):
                cut = slice(g * take, (g + 1) * take)
                kv_set = jnp.concatenate([skv[cut], kv_own[cut]], 0)
                raw = dot_nt(q_mine[cut], kv_set) * (1.0 / math.sqrt(HD))
                raw = jnp.where(group_mask(own_block + g * GROUP, take), raw, NEGATIVE)
                grown = jnp.exp(raw - jnp.max(raw, -1, keepdims=True))
                share = grown / jnp.sum(grown, -1, keepdims=True)
                attw_out[j, h, cut, :] = share
                pieces.append(dot_nn(share.astype(BF), kv_set))
            mixes.append(jnp.concatenate(pieces, 0))
        mixed = jnp.where(lower, mixes[1], mixes[0]).astype(BF)
        mixed_out[j] = mixed
        w_o = w_ref[j, :, :, C_OUT[0]:C_OUT[1]].reshape(width, 128)
        acc_scr[...] += dot_nt(mixed, w_o)
        return 0

    lax.fori_loop(0, pairs, attend, 0)

    middle = acc_scr[...]
    mid_out[...] = middle
    hid2_out[...] = norm_apply(middle, nrm_ref[0:1, :], nrm_ref[1:2, :])


def feed_forward_kernel(layer, count, mid_ref, hid2_ref, nrm_ref, *refs):
    sources = refs[:count]
    stream_out, hnext_out, upw_out, act_out, w_ref, acc_scr, sems = refs[count:]
    width = mid_ref.shape[1]
    pairs = w_ref.shape[0]
    copies = load_weights(sources, (ATTN, ATTN + FEED), layer, w_ref, sems)
    acc_scr[...] = mid_ref[...]
    for copy in copies:
        copy.wait()

    def feed(j, _):
        w_up = w_ref[j, :, :, C_UP[0]:C_UP[1]].reshape(width, 512)
        upward = dot_nn(hid2_ref[...], w_up)
        upw_out[j] = upward
        bent = jnp.tanh(GELU_C * (upward + GELU_A * upward * upward * upward))
        act = (0.5 * upward * (1.0 + bent)).astype(BF)
        act_out[j] = act
        w_dn = w_ref[j, :, :, C_DOWN[0]:C_DOWN[1]].reshape(width, 512)
        acc_scr[...] += dot_nt(act, w_dn)
        return 0

    lax.fori_loop(0, pairs, feed, 0)
    result = acc_scr[...]
    stream_out[...] = result
    hnext_out[...] = norm_apply(result, nrm_ref[0:1, :], nrm_ref[1:2, :])


VM = pl.BlockSpec(memory_space=pltpu.VMEM)
SM = pl.BlockSpec(memory_space=pltpu.SMEM)
FAR = pl.BlockSpec(memory_space=pl.ANY)
shape = jax.ShapeDtypeStruct


def settings(flops, traffic, name):
    return dict(
        compiler_params=pltpu.CompilerParams(vmem_limit_bytes=VMEM_LIMIT),
        cost_estimate=pl.CostEstimate(flops=flops, bytes_accessed=traffic, transcendentals=0),
        name=name,
    )


def weight_slots(sources, pairs, columns):
    parts, depth = (sources[0].shape[0], sources[0].shape[-2])
    return pltpu.VMEM((pairs, parts, depth, columns), BF)


def attend_forward(layer, hidden, stream, sources, nrm, after=(), flows=(), ident=0):
    rows, width = stream.shape
    pairs = len(hidden)
    length = rows * pairs
    own_blocks, blocks = rows // BLOCK, length // BLOCK
    outs = [
        shape((rows, width), F32),
        shape((rows, width), BF),
        shape((length, width), BF),
        shape((pairs, length, 256), BF),
        shape((pairs, rows, 128), BF),
        shape((pairs, 2, rows, 128), BF),
        shape((pairs, 2, rows, 2 * GROUP * BLOCK), F32),
        shape((pairs, rows, 128), BF),
        shape((2 * pairs, own_blocks, blocks), F32),
        shape((pairs, blocks, 128), F32),
    ]
    return call(
        functools.partial(attend_forward_kernel, layer, len(sources)),
        outs,
        [VM] * (pairs + 2) + [FAR] * len(sources),
        [VM] * len(outs),
        (*hidden, stream, nrm, *sources),
        after,
        flows,
        ident,
        scratch_shapes=[
            weight_slots(sources, pairs, ATTN),
            pltpu.VMEM((2 * pairs, blocks, blocks), F32),
            pltpu.VMEM((rows, width), F32),
            pltpu.SemaphoreType.DMA((pairs,)),
        ],
        **settings(18_000_000_000, 10_000_000, "attend_forward"),
    )


def feed_forward(layer, middle, hidden, sources, nrm, after=(), flows=(), ident=0):
    rows, width = middle.shape
    pairs = lax.axis_size("head")
    outs = [
        shape((rows, width), F32),
        shape((rows, width), BF),
        shape((pairs, rows, 512), F32),
        shape((pairs, rows, 512), BF),
    ]
    return call(
        functools.partial(feed_forward_kernel, layer, len(sources)),
        outs,
        [VM] * 3 + [FAR] * len(sources),
        [VM] * len(outs),
        (middle, hidden, nrm, *sources),
        after,
        scratch_shapes=[
            weight_slots(sources, pairs, FEED),
            pltpu.VMEM((rows, width), F32),
            pltpu.SemaphoreType.DMA((pairs,)),
        ],
        **settings(8_000_000_000, 8_000_000, "feed_forward"),
    )


def put(wgrad_scr, j, columns, value):
    parts, depth = wgrad_scr.shape[1:3]
    size = columns[1] - columns[0]
    wgrad_scr[j, :, :, columns[0]:columns[1]] = value.astype(BF).reshape(parts, depth, size)


def send_grads(wgrad_scr, keep_out, send_out, sems):
    copies = []
    for p in range(wgrad_scr.shape[0]):
        out = send_out if p & 1 else keep_out
        copies.append(pltpu.make_async_copy(wgrad_scr.at[p], out.at[p >> 1], sems.at[p]))
        copies[p].start()
    for copy in copies:
        copy.wait()


def feed_backward_kernel(
    layer, count, keep_ref, near_ref, far_ref, above_ref, carry_ref, gain_above_ref, gain_two_ref,
    mid_ref, hid2_ref, upw_ref, act_ref, *refs
):
    sources = refs[:count]
    (
        wkeep_out, wsend_out, carry_out, pair_above_out, pair_two_out,
        w_ref, acc_scr, low_scr, wgrad_scr, sems,
    ) = refs[count:]
    width = carry_ref.shape[1]
    pairs = w_ref.shape[0]
    copies = load_weights(sources, (ATTN, ATTN + FEED), layer, w_ref, sems)

    dy = keep_ref[0].astype(F32) + near_ref[0].astype(F32) + far_ref[...].astype(F32)
    back, pair = norm_back(dy, above_ref[...], gain_above_ref[...])
    pair_above_out[...] = pair
    upstream = carry_ref[...] + back
    carry_out[...] = upstream
    low_scr[...] = upstream.astype(BF)
    acc_scr[...] = jnp.zeros_like(acc_scr)
    for copy in copies:
        copy.wait()

    def feed(j, _):
        low = low_scr[...]
        w_dn = w_ref[j, :, :, C_DOWN[0]:C_DOWN[1]].reshape(width, 512)
        grad_act = dot_nn(low, w_dn)
        x = upw_ref[j]
        squared = x * x
        bent = jnp.tanh(GELU_C * (x + GELU_A * squared * x))
        slope = 0.5 * (1.0 + bent) + 0.5 * x * (1.0 - bent * bent) * (
            GELU_C * (1.0 + 3.0 * GELU_A * squared)
        )
        grad_up = (grad_act * slope).astype(BF)
        put(wgrad_scr, j, C_DOWN, dot_tn(low, act_ref[j]))
        put(wgrad_scr, j, C_UP, dot_tn(hid2_ref[...], grad_up))
        w_up = w_ref[j, :, :, C_UP[0]:C_UP[1]].reshape(width, 512)
        acc_scr[...] += dot_nt(grad_up, w_up)
        return 0

    lax.fori_loop(0, pairs, feed, 0)

    back, pair = norm_back(acc_scr[...], mid_ref[...], gain_two_ref[...])
    pair_two_out[...] = pair
    carry_out[...] += back
    send_grads(wgrad_scr, wkeep_out, wsend_out, sems)


def attend_backward_kernel(
    layer, count, carry_ref, hid_ref, kv_ref, q_ref, skv_ref, attw_ref, mixed_ref, permo_ref, sort_ref,
    *refs
):
    sources = refs[:count]
    (
        gkeep_out, gsend_out, wkeep_out, wsend_out,
        w_ref, ghid_scr, gkv_scr, gsrt_scr, gq_scr, dperm_scr, low_scr, wgrad_scr, sems,
    ) = refs[count:]
    length, width = hid_ref.shape
    rows = carry_ref.shape[0]
    pairs, parts, depth = w_ref.shape[:3]
    own_blocks = rows // BLOCK
    blocks = length // BLOCK
    my = lax.axis_index("head")
    own = pl.multiple_of(my * rows, rows)
    own_block = pl.multiple_of(my * own_blocks, own_blocks)
    lower = iota((1, 128), 1) < HD
    take = GROUP * BLOCK
    copies = load_weights(sources, (0, ATTN), layer, w_ref, sems)
    low_scr[...] = carry_ref[...].astype(BF)
    dperm_scr[...] = jnp.zeros_like(dperm_scr)
    for copy in copies:
        copy.wait()
    scale_key = 1.0 / math.sqrt(HD)

    def attend(j, _):
        low = low_scr[...]
        w_o = w_ref[j, :, :, C_OUT[0]:C_OUT[1]].reshape(width, 128)
        grad_mixed = dot_nn(low, w_o).astype(BF)
        put(wgrad_scr, j, C_OUT, dot_tn(low, mixed_ref[j]))
        q = q_ref[j]
        zero = jnp.zeros_like(q)
        queries = []
        for h in range(2):
            key_lanes = lower if h == 0 else ~lower
            kron = kron_rows(permo_ref[2 * j + h], length)
            kv_all = kv_ref[j, :, h * 128:(h + 1) * 128]
            kv_own = kv_ref[j, pl.ds(own, rows), h * 128:(h + 1) * 128]
            skv = skv_ref[j, h]
            q_mine = jnp.where(key_lanes, q, zero)
            gm_mine = jnp.where(key_lanes, zero, grad_mixed)
            scale = jnp.where(key_lanes, scale_key, 1.0)
            gq, g_sorted, g_own = [], [], []
            for g in range(rows // take):
                cut = slice(g * take, (g + 1) * take)
                kv_set = jnp.concatenate([skv[cut], kv_own[cut]], 0)
                share = attw_ref[j, h, cut, :]
                grad_share = dot_nt(gm_mine[cut], kv_set)
                grad_raw = (
                    share * (grad_share - jnp.sum(share * grad_share, -1, keepdims=True))
                ).astype(BF)
                gq.append(dot_nn(grad_raw, kv_set) * scale_key)
                grad_set = (
                    dot_tn(grad_raw, q_mine[cut]) + dot_tn(share.astype(BF), gm_mine[cut])
                ) * scale
                g_sorted.append(grad_set[:take])
                g_own.append(grad_set[take:])
            queries.append(jnp.concatenate(gq, 0))
            grad_sorted = jnp.concatenate(g_sorted, 0).astype(BF)
            crossed = dot_nt(grad_sorted, kv_all)
            same = (iota((rows, length), 0) & (BLOCK - 1)) == (iota((rows, length), 1) & (BLOCK - 1))
            crossed = jnp.where(same, crossed, 0.0).reshape(own_blocks, BLOCK, length)
            dperm_scr[2 * j + h] = jnp.sum(crossed, 1)
            ghid_scr[:, 0:128] = dot_tn(kron, grad_sorted)
            ghid_scr[pl.ds(own, rows), 0:128] += jnp.concatenate(g_own, 0)
            gkv_scr[j, :, h * 128:(h + 1) * 128] = ghid_scr[:, 0:128].astype(BF)
        gq_scr[j] = jnp.where(lower, queries[0], queries[1]).astype(BF)
        return 0

    lax.fori_loop(0, pairs, attend, 0)

    heads = 2 * pairs
    gather = (iota((length, blocks), 0) // BLOCK == iota((length, blocks), 1)).astype(F32)
    dperm = lax.dot_general(
        dperm_scr[...].reshape(heads * own_blocks, length),
        gather,
        (((1,), (0,)), ((), ())),
        precision=lax.Precision.HIGHEST,
        preferred_element_type=F32,
    ).reshape(heads, own_blocks, blocks)
    scores = jnp.stack(
        [sort_ref[h // 2][:, (h % 2) * BLOCK:(h % 2) * BLOCK + blocks] for h in range(heads)]
    )
    full = jnp.concatenate([dperm] * (blocks // own_blocks), 1)
    block_at = iota(full.shape, 1)
    full = jnp.where((block_at >= own_block) & (block_at < own_block + own_blocks), full, 0.0)
    grad_sort = balance_back(scores, full) / math.sqrt(BLOCK)
    blank = jnp.zeros((blocks, 128 - 2 * blocks), F32)
    for j in range(pairs):
        gsrt_scr[j] = jnp.concatenate([grad_sort[2 * j], grad_sort[2 * j + 1], blank], 1)

    ghid_scr[...] = jnp.zeros_like(ghid_scr)

    def inward(j, _):
        w = w_ref[j, :, :, C_KVS[0]:C_KVS[1]].reshape(width, C_KVS[1] - C_KVS[0])
        spread = jnp.broadcast_to(gsrt_scr[j][:, None, :], (blocks, BLOCK, 128)).reshape(length, 128)
        grad = jnp.concatenate([gkv_scr[j], spread.astype(BF)], 1)
        put(wgrad_scr, j, C_KVS, dot_tn(hid_ref[...], grad))
        ghid_scr[...] += dot_nt(grad, w)
        wq = w_ref[j, :, :, C_Q[0]:C_Q[1]].reshape(width, 128)
        put(wgrad_scr, j, C_Q, dot_tn(hid_ref[pl.ds(own, rows), :], gq_scr[j]))
        ghid_scr[pl.ds(own, rows), :] += dot_nt(gq_scr[j], wq)
        return 0

    lax.fori_loop(0, pairs, inward, 0)
    for p in range(pairs):
        out = gsend_out if p & 1 else gkeep_out
        at = pl.multiple_of(turned(p) * rows, rows)
        out[p >> 1] = ghid_scr[pl.ds(at, rows), :].astype(BF)
    send_grads(wgrad_scr, wkeep_out, wsend_out, sems)


def feed_backward(layer, dy, above, carry, gain_above, sources, gain_two, kept, after=(), flows=(), ident=0):
    rows, width = carry.shape
    pairs = lax.axis_size("head")
    slots = weight_slots(sources, pairs, FEED)
    half = shape((pairs // 2,) + slots.shape[1:], BF)
    outs = [half, half, shape((rows, width), F32), shape((2, width), F32), shape((2, width), F32)]
    return call(
        functools.partial(feed_backward_kernel, layer, len(sources)),
        outs,
        [VM] * (7 + len(kept)) + [FAR] * len(sources),
        [FAR, FAR, VM, VM, VM],
        (*dy, above, carry, gain_above, gain_two, *kept, *sources),
        after,
        flows,
        ident,
        scratch_shapes=[
            slots,
            pltpu.VMEM((rows, width), F32),
            pltpu.VMEM((rows, width), BF),
            slots,
            pltpu.SemaphoreType.DMA((pairs,)),
        ],
        **settings(12_000_000_000, 12_000_000, "feed_backward"),
    )


def attend_backward(layer, carry, sources, kept, after=(), flows=(), ident=0):
    rows, width = carry.shape
    pairs = lax.axis_size("head")
    length = rows * pairs
    own_blocks, blocks = rows // BLOCK, length // BLOCK
    slots = weight_slots(sources, pairs, ATTN)
    piece = shape((pairs // 2, rows, width), BF)
    half = shape((pairs // 2,) + slots.shape[1:], BF)
    return call(
        functools.partial(attend_backward_kernel, layer, len(sources)),
        [piece, piece, half, half],
        [VM] * (1 + len(kept)) + [FAR] * len(sources),
        [VM, VM, FAR, FAR],
        (carry, *kept, *sources),
        after,
        flows,
        ident,
        scratch_shapes=[
            slots,
            pltpu.VMEM((length, width), F32),
            pltpu.VMEM((pairs, length, 256), BF),
            pltpu.VMEM((pairs, blocks, 128), F32),
            pltpu.VMEM((pairs, rows, 128), BF),
            pltpu.VMEM((2 * pairs, own_blocks, length), F32),
            pltpu.VMEM((rows, width), BF),
            slots,
            pltpu.SemaphoreType.DMA((pairs,)),
        ],
        **settings(20_000_000_000, 16_000_000, "attend_backward"),
    )


def embed_kernel(base_ref, tok_ref, table_ref, out_ref, tall_ref):
    features, vocab = table_ref.shape
    count = out_ref.shape[1]
    bins = vocab // 256

    @pl.when(pl.program_id(0) == 0)
    def _():
        for at in range(bins):
            tall_ref[at * features:(at + 1) * features, :] = table_ref[:, at * 256:(at + 1) * 256]

    local = tok_ref[...] - base_ref[0]
    high, low = local >> 8, local & 255
    hot = (iota((256, count), 0) == low).astype(BF)
    found = dot_nn(tall_ref[...], hot)
    total = jnp.zeros((features, count), F32)
    for at in range(bins):
        total = jnp.where(high == at, found[at * features:(at + 1) * features, :], total)
    out_ref[...] = total.astype(BF)


def embed_lookup(base, tokens, table, after=()):
    features, vocab = table.shape
    count = tokens.shape[1]
    tile = 512
    return call(
        embed_kernel,
        [jax.ShapeDtypeStruct((features, count), BF)],
        [
            pl.BlockSpec(memory_space=pltpu.SMEM),
            pl.BlockSpec((1, tile), lambda i: (0, i)),
            pl.BlockSpec((features, vocab), lambda i: (0, 0)),
        ],
        [pl.BlockSpec((features, tile), lambda i: (0, i))],
        (base, tokens, table),
        after,
        grid=(count // tile,),
        scratch_shapes=[pltpu.VMEM((features * (vocab // 256), 256), BF)],
        compiler_params=pltpu.CompilerParams(vmem_limit_bytes=VMEM_LIMIT),
        cost_estimate=pl.CostEstimate(flops=15_000_000_000, bytes_accessed=4_000_000, transcendentals=0),
        name="embed_lookup",
    )


def embed_back_kernel(base_ref, tok_ref, grad_ref, out_ref, acc_ref):
    features = grad_ref.shape[0]
    count = grad_ref.shape[1]
    bins = acc_ref.shape[0] // features
    step = pl.program_id(0)
    local = tok_ref[...] - base_ref[0]
    high, low = local >> 8, local & 255
    hot = (iota((256, count), 0) == low).astype(BF)
    grad = grad_ref[...]
    wide = jnp.concatenate(
        [jnp.where(high == at, grad, jnp.zeros_like(grad)) for at in range(bins)], 0
    )
    found = dot_nt(wide, hot)

    @pl.when(step == 0)
    def _():
        acc_ref[...] = found

    @pl.when(step > 0)
    def _():
        acc_ref[...] += found

    @pl.when(step == pl.num_programs(0) - 1)
    def _():
        for at in range(bins):
            out_ref[:, at * 256:(at + 1) * 256] = acc_ref[at * features:(at + 1) * features, :]


def embed_back(base, tokens, grad, vocab, after=(), flows=(), ident=0):
    pieces, features, tile = grad.shape
    return call(
        embed_back_kernel,
        [shape((features, vocab), F32)],
        [
            SM,
            pl.BlockSpec((1, tile), lambda i: (0, i)),
            pl.BlockSpec((None, features, tile), lambda i: (i, 0, 0)),
        ],
        [pl.BlockSpec((features, vocab), lambda i: (0, 0))],
        (base, tokens, grad),
        after,
        flows,
        ident,
        grid=(pieces,),
        scratch_shapes=[pltpu.VMEM((features * (vocab // 256), 256), F32)],
        **settings(15_000_000_000, 4_000_000, "embed_back"),
    )


def start_kernel(raw_ref, nrm_ref, stream_out, hid_out, *, scale):
    stream = raw_ref[...].astype(F32).T * scale
    stream_out[...] = stream
    hid_out[...] = norm_apply(stream, nrm_ref[0:1, :], nrm_ref[1:2, :])


def start_stream(raw, nrm, after=()):
    width, rows = raw.shape
    vm = pl.BlockSpec(memory_space=pltpu.VMEM)
    return call(
        functools.partial(start_kernel, scale=math.sqrt(width)),
        [
            jax.ShapeDtypeStruct((rows, width), F32),
            jax.ShapeDtypeStruct((rows, width), BF),
        ],
        [vm] * 2,
        [vm] * 2,
        (raw, nrm),
        after,
        name="start_stream",
    )


def finish_kernel(keep_ref, near_ref, far_ref, above_ref, carry_ref, gain_ref, grad_out, pair_out):
    dy = keep_ref[0].astype(F32) + near_ref[0].astype(F32) + far_ref[...].astype(F32)
    back, pair = norm_back(dy, above_ref[...], gain_ref[...])
    pair_out[...] = pair
    grad_out[...] = (carry_ref[...] + back).T.astype(BF)


def finish_stream(dy, above, carry, gain, after=(), flows=(), ident=0):
    rows, width = above.shape
    vm = pl.BlockSpec(memory_space=pltpu.VMEM)
    return call(
        finish_kernel,
        [
            jax.ShapeDtypeStruct((width, rows), BF),
            jax.ShapeDtypeStruct((2, width), F32),
        ],
        [vm] * 6,
        [vm] * 2,
        (*dy, above, carry, gain),
        after,
        flows,
        ident,
        name="finish_stream",
    )


def to_lanes(column):
    return jnp.broadcast_to(column, (column.shape[0], 128)).T[0:1, :]


def to_rows(line):
    return jnp.broadcast_to(line, (128, line.shape[1])).T[:, 0:1]


def head_stats_kernel(table_ref, final_ref, goal_ref, stat_out):
    logits = dot_nn(final_ref[...], table_ref[...])
    top = jnp.max(logits, 1, keepdims=True)
    total = jnp.sum(jnp.exp(logits - top), 1, keepdims=True)
    hit = iota(logits.shape, 1) == goal_ref[...]
    pick = jnp.sum(jnp.where(hit, logits, 0.0), 1, keepdims=True)
    stat_out[0:1, :] = to_lanes(top)
    stat_out[1:2, :] = to_lanes(total)
    stat_out[2:3, :] = to_lanes(pick)


def head_stats(table, final_all, goals):
    width, vocab = table.shape
    count = final_all.shape[0]
    tile = 256
    return pl.pallas_call(
        head_stats_kernel,
        grid=(count // tile,),
        out_shape=jax.ShapeDtypeStruct((3, count), F32),
        in_specs=[
            pl.BlockSpec((width, vocab), lambda i: (0, 0)),
            pl.BlockSpec((tile, width), lambda i: (i, 0)),
            pl.BlockSpec((tile, 1), lambda i: (i, 0)),
        ],
        out_specs=pl.BlockSpec((3, tile), lambda i: (0, i)),
        compiler_params=pltpu.CompilerParams(vmem_limit_bytes=VMEM_LIMIT),
        cost_estimate=pl.CostEstimate(flops=16_000_000_000, bytes_accessed=6_000_000, transcendentals=0),
        name="head_stats",
    )(table, final_all, goals)


def head_back_kernel(table_ref, final_ref, goal_ref, line_ref, gfin_out, gtab_out, acc_ref):
    step = pl.program_id(0)
    logits = dot_nn(final_ref[...], table_ref[...])
    hit = iota(logits.shape, 1) == goal_ref[...]
    chance = jnp.exp(logits - to_rows(line_ref[0:1, :]))
    grad = ((chance - jnp.where(hit, 1.0, 0.0)) * to_rows(line_ref[1:2, :])).astype(BF)
    gfin_out[...] = dot_nt(grad, table_ref[...]).astype(BF)
    part = dot_tn(final_ref[...], grad)

    @pl.when(step == 0)
    def _():
        acc_ref[...] = part

    @pl.when(step > 0)
    def _():
        acc_ref[...] += part

    @pl.when(step == pl.num_programs(0) - 1)
    def _():
        gtab_out[...] = acc_ref[...].astype(BF)


def head_back(table, final_all, goals, lines):
    width, vocab = table.shape
    count = final_all.shape[0]
    tile = 256
    return pl.pallas_call(
        head_back_kernel,
        grid=(count // tile,),
        out_shape=[
            jax.ShapeDtypeStruct((count, width), BF),
            jax.ShapeDtypeStruct((width, vocab), BF),
        ],
        in_specs=[
            pl.BlockSpec((width, vocab), lambda i: (0, 0)),
            pl.BlockSpec((tile, width), lambda i: (i, 0)),
            pl.BlockSpec((tile, 1), lambda i: (i, 0)),
            pl.BlockSpec((2, tile), lambda i: (0, i)),
        ],
        out_specs=[
            pl.BlockSpec((tile, width), lambda i: (i, 0)),
            pl.BlockSpec((width, vocab), lambda i: (0, 0)),
        ],
        scratch_shapes=[pltpu.VMEM((width, vocab), F32)],
        compiler_params=pltpu.CompilerParams(vmem_limit_bytes=VMEM_LIMIT),
        cost_estimate=pl.CostEstimate(flops=35_000_000_000, bytes_accessed=14_000_000, transcendentals=0),
        name="head_back",
    )(table, final_all, goals, lines)


def swap(value, axis, bit):
    return lax.ppermute(value, axis, [(at, at ^ bit) for at in range(lax.axis_size(axis))])


def has_bit(axis, bit):
    return (lax.axis_index(axis) & bit) != 0


def bits_of(axis):
    size = lax.axis_size(axis)
    return [1 << at for at in reversed(range(size.bit_length() - 1))]


def in_order(mine, other, axis, bit, dim):
    flag = has_bit(axis, bit)
    return jnp.concatenate([jnp.where(flag, other, mine), jnp.where(flag, mine, other)], dim)


def gather_dp(value):
    bits = bits_of("dp")
    whole = value.reshape((1,) * len(bits) + value.shape)
    for dim, bit in enumerate(bits):
        whole = in_order(whole, swap(whole, "dp", bit), "dp", bit, dim)
    return whole.reshape((-1,) + value.shape)


def split(value, axis, bit, dim):
    flag = has_bit(axis, bit).astype(jnp.int32)
    low = value.astype(BF)
    return (
        lax.dynamic_index_in_dim(low, flag, dim, False),
        lax.dynamic_index_in_dim(low, 1 - flag, dim, False),
    )


def nothing_of(value):
    return value[(0,) * value.ndim].astype(F32) * 0.0


def add_up(*values):
    result = values[0].astype(F32)
    for value in values[1:]:
        result = result + (value.astype(F32) if value.ndim else value)
    return result


def sum_all(value, combine=jnp.add):
    for axis in ("head", "dp"):
        for bit in reversed(bits_of(axis)):
            value = combine(value, swap(value, axis, bit))
    return value


def pieces_of_head(value):
    across = swap(value, "head", 2)
    return value, swap(value, "head", 1), across, swap(across, "head", 1)


def settle_head(keep, send):
    near = swap(send, "head", 1)
    across = (keep[1].astype(F32) + near[1].astype(F32)).astype(BF)
    return keep, near, swap(across, "head", 2)


def pack_weights(attn_in, attn_out, ffn_up, ffn_down):
    features = attn_in.shape[0]
    low = attn_in.astype(BF)
    q, k, v = low[..., :HD], low[..., HD:2 * HD], low[..., 2 * HD:3 * HD]
    s = low[..., 3 * HD:].reshape(features, -1)
    blank = jnp.zeros((features, 128 - s.shape[1]), BF)
    out = attn_out.astype(BF)
    out = jnp.concatenate([out[1], out[0]], 0).T
    return jnp.concatenate(
        [
            q[:, 0], q[:, 1], k[:, 0], v[:, 0], v[:, 1], k[:, 1], s, blank,
            out, ffn_up.astype(BF), ffn_down.astype(BF).T,
        ],
        1,
    )


def depth_of(features):
    return max(64, features)


def unpack_grads(packed, sort_width):
    def cut(at, size=HD):
        return packed[:, at:at + size]

    kv = C_KVS[0]
    srt = kv + 256
    first = jnp.concatenate([cut(0), cut(kv), cut(kv + 64), cut(srt, sort_width)], 1)
    second = jnp.concatenate(
        [cut(64), cut(kv + 192), cut(kv + 128), cut(srt + sort_width, sort_width)], 1
    )
    out = packed[:, C_OUT[0]:C_OUT[1]].T
    return (
        jnp.stack([first, second], 1),
        jnp.stack([out[HD:], out[:HD]], 0),
        packed[:, ATTN + C_UP[0]:ATTN + C_UP[1]],
        packed[:, ATTN + C_DOWN[0]:ATTN + C_DOWN[1]].T,
    )


class Gather:
    def __init__(self, packed):
        self.bits = bits_of("dp")
        self.features = packed.shape[0]
        value = packed.reshape((1,) * len(self.bits) + packed.shape)
        for dim, bit in enumerate(self.bits[:-1]):
            value = in_order(value, swap(value, "dp", bit), "dp", bit, dim)
        self.value = value

    def last(self, value):
        dim, bit = len(self.bits) - 1, self.bits[-1]
        return in_order(value, swap(value, "dp", bit), "dp", bit, dim)

    def first_step(self):
        self.one, two = self.value[..., :ATTN], self.value[..., ATTN:]
        self.across = swap(self.one, "head", 2)
        self.two = two, swap(two, "dp", self.bits[-1])

    def second_step(self, token):
        dim, bit = len(self.bits) - 1, self.bits[-1]
        self.two = in_order(self.two[0], self.two[1] + token.astype(BF), "dp", bit, dim)
        self.one = self.last(self.one)
        self.across = self.last(self.across + token.astype(BF))

    def pieces(self, mine, across):
        return self.shape_pieces(mine, swap(mine, "head", 1), across, swap(across, "head", 1))

    def shape_pieces(self, *got):
        return [one.reshape(-1, depth_of(self.features), one.shape[-1]) for one in got]

    def finish(self):
        return self.pieces(self.one, self.across)

    def feed_flows(self):
        def once(bit):
            return (yield self.two, "head", bit)

        self.flows = [Flow(once(2)), Flow(once(1))]
        return self.flows

    def finish_feed(self):
        across, near = (flow.finish() for flow in self.flows)
        return self.shape_pieces(self.two, near, across, swap(across, "head", 1))


def gather_rest(packed):
    dp, head = lax.axis_size("dp"), lax.axis_size("head")
    layers, features, columns = packed.shape
    whole = lax.all_gather(packed, ("dp", "head"), axis=0, tiled=True)
    fold = depth_of(features) // features
    if fold > 1:
        whole = whole.reshape(dp // fold, fold, head, layers, features, columns)
        whole = whole.transpose(0, 2, 3, 1, 4, 5)
    return whole.reshape(dp // fold, head, layers, fold * features, columns)


def adamw(weight, gradient, moment_one, moment_two, factor, step_rate):
    gradient = gradient * factor
    moment_one = BETA_ONE * moment_one + (1.0 - BETA_ONE) * gradient
    moment_two = BETA_TWO * moment_two + (1.0 - BETA_TWO) * gradient * gradient
    adam_step = (
        moment_one
        / (1.0 - BETA_ONE**STEP)
        / (jnp.sqrt(moment_two / (1.0 - BETA_TWO**STEP)) + ADAM_FLOOR)
    )
    return (weight - step_rate * (adam_step + WEIGHT_DECAY * weight), moment_one, moment_two)


def body(
    tokens, targets, lengths,
    table, table_first, table_second,
    attn_in, attn_in_first, attn_in_second,
    attn_out, attn_out_first, attn_out_second,
    ffn_up, ffn_up_first, ffn_up_second,
    ffn_down, ffn_down_first, ffn_down_second,
    norms, norms_first, norms_second,
):
    dp, head = lax.axis_size("dp"), lax.axis_size("head")
    my_dp, my_head = lax.axis_index("dp"), lax.axis_index("head")
    seq_count, length = tokens.shape
    features, vocab = table.shape
    width = features * dp
    layers = attn_in.shape[0]
    rows = length // head
    total = dp * length
    odd = my_dp & 1
    outer = [[at for at in range(dp) if at % 2 == way] for way in range(2)]

    lines = jnp.concatenate([tokens, targets, jnp.broadcast_to(lengths[:, None], (seq_count, 128))], 1)
    lines = gather_dp(lines.reshape(-1))
    all_tokens = lines[:, :length].reshape(1, total)
    positions = jnp.arange(length, dtype=jnp.int32)
    counted = (positions[None, :] < lines[:, 2 * length:2 * length + 1]).astype(F32)
    nrm = norms
    for bit in (1, 2):
        nrm = in_order(nrm, swap(nrm, "head", bit), "head", bit, 2)

    low_table = table.astype(BF)
    packs = [
        pack_weights(attn_in[at], attn_out[at], ffn_up[at], ffn_down[at]) for at in range(layers)
    ]
    leader = Gather(packs[0])

    half = vocab // 2
    other = swap(lax.dynamic_slice_in_dim(low_table, (1 - odd) * half, half, 1), "dp", 1)
    mine = lax.dynamic_slice_in_dim(low_table, odd * half, half, 1)
    head_table = in_order(mine, other, "dp", 1, 0)

    base = (my_head * vocab).astype(jnp.int32).reshape(1)
    found, token = embed_lookup(base, all_tokens, low_table, [leader.value])
    leader.first_step()
    rest_weights = gather_rest(jnp.stack(packs[1:]) + token.astype(BF))
    found = found.reshape(features, dp, head, rows)
    for bit in (1, 2):
        flag = (my_head & bit) // bit
        found = found.reshape(features, dp, -1, 2, rows) if bit == 1 else found.reshape(features, dp, 2, rows)
        dim = 3 if bit == 1 else 2
        other = swap(lax.dynamic_index_in_dim(found, 1 - flag, dim, False), "head", bit)
        found = lax.dynamic_index_in_dim(found, flag, dim, False) + other
    leader.second_step(token)
    found = lax.all_to_all(found, "dp", split_axis=1, concat_axis=0, tiled=True)
    stream, hidden, token = start_stream(found.reshape(width, rows), nrm[0])
    head_table = lax.all_gather(
        head_table + token.astype(BF), "dp", axis=0, tiled=True, axis_index_groups=outer
    )
    hidden = pieces_of_head(hidden)
    sources = [[leader.finish(), None]] + [[[rest_weights], [rest_weights]]] * (layers - 1)

    kept = []
    for at in range(layers):
        of = max(at - 1, 0)
        for_attend, for_feed = sources[at]
        middle, hidden_two, *saved, token = attend_forward(
            of, hidden, stream, for_attend, nrm[2 * at + 1], [],
            leader.feed_flows() if at == 0 else [],
        )
        if at == 0:
            for_feed = sources[0][1] = leader.finish_feed()
        result, hidden, upward, active, _ = feed_forward(
            of, middle, hidden_two, for_feed, nrm[2 * at + 2]
        )
        kept.append((stream, (middle, hidden_two, upward, active), saved))
        stream = result
        if at + 1 < layers:
            hidden = pieces_of_head(hidden)

    def spread_rows(value):
        for axis, bit in (("dp", 1), ("head", 2), ("head", 1)):
            value = jnp.stack([value, swap(value, axis, bit)])
        return value

    def line_of(values):
        values = values.reshape(dp, head, rows)
        order = [(my_dp ^ y, my_head ^ (x * 2 + c)) for c in range(2) for x in range(2) for y in range(2)]
        picked = [
            lax.dynamic_slice(values, (d, h, 0), (1, 1, rows)).reshape(rows) for d, h in order
        ]
        return jnp.concatenate(picked)

    final_all = spread_rows(hidden).reshape(-1, width)
    goals = line_of(lines[:, length:2 * length]) - (my_head * vocab + odd * half).astype(jnp.int32)
    goals = goals.reshape(-1, 1)
    counted_here = line_of(counted)
    stats = head_stats(head_table, final_all, goals)
    for dim, (axis, bit) in enumerate((("head", 1), ("head", 2), ("dp", 1))):
        theirs = swap(stats, axis, bit).reshape(3, 2, 2, 2, rows)
        theirs = jnp.flip(theirs, dim + 1).reshape(stats.shape)
        peak = jnp.maximum(stats[0], theirs[0])
        sums = stats[1] * jnp.exp(stats[0] - peak) + theirs[1] * jnp.exp(theirs[0] - peak)
        stats = jnp.stack([peak, sums, stats[2] + theirs[2]])
    lse = stats[0] + jnp.log(stats[1])
    loss_here = jnp.sum((lse - stats[2]) * counted_here) / (2 * head)
    count_total = jnp.sum(counted)
    grad_final, grad_half = head_back(head_table, final_all, goals, jnp.stack([lse, counted_here]))
    grad_final = grad_final.reshape(2, 2, 2, rows, width)
    near = swap(grad_final[1], "head", 1)
    summed = grad_final[0].astype(F32) + near.astype(F32)
    across = swap(summed[1].astype(BF), "head", 2)
    summed = summed[0] + across.astype(F32)
    far = swap(summed[1].astype(BF), "dp", 1)
    nothing = jnp.zeros((1, rows, width), BF)
    dy = (summed[0:1], nothing, far)
    grad_half = lax.psum_scatter(
        grad_half, "dp", scatter_dimension=0, tiled=True, axis_index_groups=outer
    ).reshape(2, features, half)

    carry = jnp.zeros((rows, width), F32)
    above = stream
    pair_grads = [None] * (2 * layers + 1)
    bits = bits_of("dp")

    def shaped(value):
        return value.reshape((2,) + (2,) * len(bits) + (features, value.shape[-1]))

    def attn_steps(keep, send):
        keep, near = shaped(keep), shaped((yield send, "head", 1))
        across = yield add_up(keep[1], near[1]).astype(BF), "head", 2
        here, there = split(add_up(keep[0], near[0], across), "dp", bits[-1], len(bits) - 1)
        return add_up(here, (yield there, "dp", bits[-1]))

    def feed_steps(keep, send):
        keep, near = shaped(keep), shaped((yield send, "head", 1))
        here, there = split(add_up(keep, near), "dp", bits[-1], len(bits))
        value = add_up(here, (yield there, "dp", bits[-1]))
        return add_up(value[0], (yield value[1].astype(BF), "head", 2))

    def last_steps(attn, feed):
        value = jnp.concatenate([attn.value, feed.value], -1)
        for dim, bit in reversed(list(enumerate(bits[:-1]))):
            here, there = split(value, "dp", bit, dim)
            value = add_up(here, (yield there, "dp", bit))
        return value

    attns, feeds, lasts = [None] * layers, [None] * layers, [None] * layers

    def active(*candidates):
        return [flow for flow in candidates if flow is not None and flow.ask is not None]

    idents = iter(range(1, 64))
    for at in reversed(range(layers)):
        of = max(at - 1, 0)
        stream_in, for_feed, for_attend = kept[at]
        above_attn, above_feed = (attns + [None])[at + 1], (feeds + [None])[at + 1]
        top_attn, top_feed = (attns + [None] * 2)[at + 2], (feeds + [None] * 2)[at + 2]
        fkeep, fsend, carry, pair_above, pair_two, token = feed_backward(
            of, dy, above, carry, nrm[2 * at + 2, 0:1], sources[at][1], nrm[2 * at + 1, 0:1], for_feed,
            [grad_half] if at == 0 else [], active(above_attn, top_attn, top_feed), next(idents),
        )
        feeds[at] = Flow(feed_steps(fkeep, fsend))
        if at + 2 < layers:
            lasts[at + 2] = Flow(last_steps(top_attn, top_feed))
        gkeep, gsend, akeep, asend, token = attend_backward(
            of, carry, sources[at][0], for_attend, [],
            active(feeds[at], above_attn, above_feed, *lasts), next(idents),
        )
        attns[at] = Flow(attn_steps(akeep, asend))
        dy = settle_head(gkeep, gsend)
        pair_grads[2 * at + 2] = pair_above
        pair_grads[2 * at + 1] = pair_two
        above = stream_in
    grad_stream, pair_grads[0], token = finish_stream(
        dy, above, carry, nrm[0, 0:1], [], active(attns[0]), next(idents)
    )

    spread = lax.all_to_all(
        grad_stream.reshape(dp, features, rows), "dp", split_axis=0, concat_axis=0, tiled=True
    )
    for flow in active(attns[0], feeds[0], attns[1], feeds[1], *lasts):
        flow.give(swap(*flow.ask))
    lasts[1] = Flow(last_steps(attns[1], feeds[1]))
    other = swap(lax.dynamic_index_in_dim(grad_half, 1 - odd, 0, False), "dp", 1)
    mine = lax.dynamic_index_in_dim(grad_half, odd, 0, False)
    spread = in_order(spread[:, None], swap(spread[:, None], "head", 1), "head", 1, 1)[:, None]
    spread = in_order(spread, swap(spread, "head", 2), "head", 2, 1)
    spread = spread.reshape(dp * head, features, rows)
    found, token = embed_back(
        base, all_tokens, spread, vocab, [other], active(attns[0], feeds[0], *lasts), next(idents)
    )
    lasts[0] = Flow(last_steps(attns[0], feeds[0]))
    grad_table = in_order(mine, other, "dp", 1, 1).astype(F32) + math.sqrt(width) * found
    packed_grads = [flow.finish() for flow in lasts]

    grad_norms = sum_all(jnp.stack(pair_grads))
    grad_norms = lax.dynamic_slice_in_dim(grad_norms, my_head * norms.shape[2], norms.shape[2], 2)
    sort_width = attn_in.shape[3] - 3 * HD
    layer_grads = [unpack_grads(packed, sort_width) for packed in packed_grads]
    grad_in, grad_out, grad_up, grad_down = (
        jnp.stack([one[member] for one in layer_grads]) for member in range(4)
    )
    squares = jnp.sum(grad_table * grad_table) + jnp.sum(grad_norms * grad_norms) / dp
    for packed in packed_grads:
        squares = squares + jnp.sum(packed * packed)
    totals = sum_all(jnp.stack([squares, loss_here]))
    grad_norm = jnp.sqrt(totals[0])
    loss_total = totals[1]
    factor = jnp.minimum(1.0, CLIP_LIMIT / (grad_norm + 1e-06))

    results = [jnp.stack([loss_total, count_total]), grad_norm]
    for weight, gradient, first, second in (
        (table, grad_table, table_first, table_second),
        (attn_in, grad_in, attn_in_first, attn_in_second),
        (attn_out, grad_out, attn_out_first, attn_out_second),
        (ffn_up, grad_up, ffn_up_first, ffn_up_second),
        (ffn_down, grad_down, ffn_down_first, ffn_down_second),
    ):
        new, one, two = adamw(weight, gradient, first, second, factor, RATE_MATRIX)
        results += [new, new.astype(BF), one, two]
    results += list(adamw(norms, grad_norms, norms_first, norms_second, factor, RATE_NORM))
    return tuple(results)


def solution(mesh):
    ints = [P("dp", None), P("dp", None), P("dp")]
    by_table = P("dp", "head")
    by_in = P(None, "dp", "head", None)
    by_out = P(None, "head", None, "dp")
    by_up = P(None, "dp", "head")
    by_down = P(None, "head", "dp")
    by_norm = P(None, None, "head")
    in_specs, out_specs = list(ints), [P(), P()]
    for spec in (by_table, by_in, by_out, by_up, by_down):
        in_specs += [spec] * 3
        out_specs += [spec] * 4
    in_specs += [by_norm] * 3
    out_specs += [by_norm] * 3
    return jax.shard_map(
        body, mesh=mesh, in_specs=tuple(in_specs), out_specs=tuple(out_specs), check_vma=False
    )
```

```python
import functools
import math

import jax
import jax.numpy as jnp
from jax import lax
from jax.experimental import pallas as pl
from jax.experimental.pallas import tpu as pltpu
from jax.sharding import PartitionSpec as P

HD = 64
BLOCK = 32
SINK = 8
STEP = 10
EPSILON = 1e-05
NEGATIVE = -1000000000.0
TEMPER = 0.75
BETA_ONE = 0.9
BETA_TWO = 0.999
ADAM_FLOOR = 1e-08
WEIGHT_DECAY = 0.01
RATE_MATRIX = 0.1
RATE_NORM = 0.5
CLIP_LIMIT = 1.0

BF = jnp.bfloat16
F32 = jnp.float32
GROUP = 2
GELU_C = math.sqrt(2.0 / math.pi)
GELU_A = 0.044715

C_Q = (0, 128)
C_KVS = (128, 512)
C_OUT = (512, 640)
ATTN = 640
C_UP = (0, 512)
C_DOWN = (512, 1024)
FEED = 1024
VMEM_LIMIT = 56 * 1024 * 1024


def dot_nn(a, b):
    return lax.dot_general(a, b, (((1,), (0,)), ((), ())), preferred_element_type=F32)


def dot_nt(a, b):
    return lax.dot_general(a, b, (((1,), (1,)), ((), ())), preferred_element_type=F32)


def dot_tn(a, b):
    return lax.dot_general(a, b, (((0,), (0,)), ((), ())), preferred_element_type=F32)


def iota(shape, axis):
    return lax.broadcasted_iota(jnp.int32, shape, axis)


MESH = pl.DeviceIdType.MESH


def flipped(axis, bit):
    mine = lax.axis_index(axis)
    return mine + bit - 2 * bit * ((mine // bit) % 2)


def remote(source, target, send_sem, recv_sem, axis, bit):
    return pltpu.make_async_remote_copy(
        src_ref=source,
        dst_ref=target,
        send_sem=send_sem,
        recv_sem=recv_sem,
        device_id={axis: flipped(axis, bit)},
        device_id_type=MESH,
    )


HEADS = (("head", 1), ("head", 2))


def call(
    kernel, outs, in_specs, out_specs, operands, after=(), flows=(), ident=0, greet=(), greet_all=None, hold=None, **options
):
    used, spare, token, riders = len(operands), len(after), len(outs), len(flows)
    asks = [flow.ask for flow in flows]
    pairs = sorted({ask[1:] for ask in asks} | set(greet))
    pairs = [pair for pair in pairs if pair[0] != greet_all]
    grid = options.get("grid")
    scratch = list(options.pop("scratch_shapes", []))
    far = pl.BlockSpec(memory_space=pl.ANY)

    def run(*refs):
        ins, rest = refs[:used], refs[used + spare:]
        sends, rest = rest[:riders], rest[riders:]
        results, token_ref, rest = rest[:token], rest[token], rest[token + 1:]
        lands, rest = rest[:riders], rest[riders:]
        if riders:
            rest, (send_sems, recv_sems) = rest[:-2], rest[-2:]

        def copies():
            if not riders:
                return []
            return [
                remote(sends[at], lands[at], send_sems.at[at], recv_sems.at[at], axis, bit)
                for at, (_, axis, bit) in enumerate(asks)
            ]

        def launch():
            barrier = pltpu.get_barrier_semaphore()
            for axis, bit in pairs:
                pl.semaphore_signal(
                    barrier, inc=1, device_id={axis: flipped(axis, bit)}, device_id_type=MESH
                )
            others = lax.axis_size(greet_all) - 1 if greet_all else 0
            for step in range(others):
                peer = (lax.axis_index(greet_all) + step + 1) % (others + 1)
                pl.semaphore_signal(barrier, inc=1, device_id={greet_all: peer}, device_id_type=MESH)
            pl.semaphore_wait(barrier, len(pairs) + others)
            if hold is None:
                fly()

        def fly():
            for copy in copies():
                copy.start()

        def settle():
            for copy in copies():
                copy.wait()

        if riders or greet:
            pl.when(pl.program_id(0) == 0)(launch) if grid else launch()
        token_ref[...] = jnp.zeros((1, 128), F32)
        if hold is not None and grid:
            if riders:
                pl.when(pl.program_id(0) == hold)(fly)
            kernel(*ins, *results, *rest)
        elif hold is not None:
            kernel(*ins, *results, *rest, fly=fly)
        else:
            kernel(*ins, *results, *rest)
        if riders:
            pl.when(pl.program_id(0) == grid[0] - 1)(settle) if grid else settle()

    if riders or greet:
        options["compiler_params"] = pltpu.CompilerParams(
            vmem_limit_bytes=VMEM_LIMIT, collective_id=ident, has_side_effects=True
        )
    if riders:
        scratch += [pltpu.SemaphoreType.DMA((riders,))] * 2
    token_spec = (
        pl.BlockSpec((1, 128), lambda i: (0, 0)) if grid else pl.BlockSpec(memory_space=pltpu.VMEM)
    )
    got = pl.pallas_call(
        run,
        out_shape=list(outs)
        + [jax.ShapeDtypeStruct((1, 128), F32)]
        + [jax.ShapeDtypeStruct(ask[0].shape, ask[0].dtype) for ask in asks],
        in_specs=list(in_specs) + [far] * (spare + riders),
        out_specs=list(out_specs) + [token_spec] + [far] * riders,
        scratch_shapes=scratch,
        **options,
    )(*operands, *after, *[ask[0] for ask in asks])
    for flow, value in zip(flows, got[token + 1:]):
        flow.give(value)
    return (*got[:token], got[token][0, 0])


class Flow:
    def __init__(self, steps):
        self.steps, self.parts = steps, None
        self.give(None)

    @property
    def value(self):
        return self.parts

    def give(self, got):
        try:
            self.ask = self.steps.send(got)
        except StopIteration as stop:
            self.ask, self.parts = None, stop.value

    def finish(self):
        while self.ask is not None:
            self.give(swap(*self.ask))
        return add_up(*self.parts) if isinstance(self.parts, tuple) else self.parts


def norm_stats(stream):
    average = jnp.mean(stream, -1, keepdims=True)
    variance = jnp.mean(stream * stream, -1, keepdims=True) - average * average
    inv_std = lax.rsqrt(variance + EPSILON)
    return (stream - average) * inv_std, inv_std


def norm_apply(stream, gain, bias):
    normed, _ = norm_stats(stream)
    return (normed * gain + bias).astype(BF)


def norm_back(upstream, stream, gain):
    normed, inv_std = norm_stats(stream)
    scaled = upstream * gain
    back = inv_std * (
        scaled
        - jnp.mean(scaled, -1, keepdims=True)
        - normed * jnp.mean(scaled * normed, -1, keepdims=True)
    )
    pair = jnp.concatenate(
        [jnp.sum(upstream * normed, 0, keepdims=True), jnp.sum(upstream, 0, keepdims=True)], 0
    )
    return back, pair


def allowed_mask(shape):
    return iota(shape, len(shape) - 1) < iota(shape, len(shape) - 2)


def log_total(x, axis):
    top = jnp.max(x, axis, keepdims=True)
    return top + jnp.log(jnp.sum(jnp.exp(x - top), axis, keepdims=True))


def balance(scores, keep):
    allowed = allowed_mask(scores.shape)
    plan = jnp.where(allowed, scores / TEMPER, NEGATIVE)
    for _ in range(SINK):
        for axis in (-2, -1):
            plan = jnp.where(allowed, plan - log_total(plan, axis), NEGATIVE)
            if keep is not None:
                keep.append(plan)
    return jnp.where(allowed, jnp.exp(plan), 0.0)


def balance_back(scores, upstream):
    allowed = allowed_mask(scores.shape)
    plans = []
    perm = balance(scores, plans)
    grad = jnp.where(allowed, upstream * perm, 0.0)
    for step in reversed(range(2 * SINK)):
        axis = (-2, -1)[step % 2]
        share = jnp.exp(plans[step])
        grad = jnp.where(allowed, grad - share * jnp.sum(grad, axis, keepdims=True), 0.0)
    return grad / TEMPER


def kron_rows(perm_rows, length):
    own, blocks = perm_rows.shape
    rows = own * BLOCK
    tall = jnp.broadcast_to(perm_rows[:, None, :], (own, BLOCK, blocks)).reshape(rows, blocks)
    spread = (iota((blocks, length), 1) // BLOCK == iota((blocks, length), 0)).astype(BF)
    wide = dot_nn(tall.astype(BF), spread)
    same = (iota((rows, length), 0) & (BLOCK - 1)) == (iota((rows, length), 1) & (BLOCK - 1))
    return jnp.where(same, wide, 0.0).astype(BF)


def group_mask(first_block, rows):
    shape = (rows, 2 * rows)
    row, slot = iota(shape, 0), iota(shape, 1)
    row_block = row // BLOCK
    in_sorted = slot < rows
    place = jnp.where(in_sorted, slot, slot - rows)
    same = (place // BLOCK) == row_block
    sorted_ok = in_sorted & (row_block + first_block >= 1)
    own_ok = (slot >= rows) & (place <= row)
    return same & (sorted_ok | own_ok)


def turned(p):
    mine = lax.axis_index("head")
    low, high = mine % 2, (mine // 2) % 2
    rest = mine - low - 2 * high
    return rest + (1 - low if p & 1 else low) + 2 * (1 - high if p & 2 else high)


def load_weights(sources, columns, layer, w_ref, sems):
    copies = []
    for p in range(w_ref.shape[0]):
        if len(sources) > 1:
            source = sources[p]
        else:
            source = sources[0].at[:, turned(p), layer, :, columns[0]:columns[1]]
        copies.append(pltpu.make_async_copy(source, w_ref.at[p], sems.at[p]))
        copies[p].start()
    return copies


def attend_forward_kernel(layer, count, hid0_ref, hid1_ref, hid2in_ref, hid3_ref, stream_ref, nrm_ref, *refs):
    sources = refs[:count]
    (
        mid_out, hid2_out, hid_ref, kv_out, q_out, skv_out, attw_out, mixed_out, permo_out, sort_out,
        w_ref, perm_scr, acc_scr, sems,
    ) = refs[count:]
    length, width = hid_ref.shape
    rows = stream_ref.shape[0]
    pairs = w_ref.shape[0]
    own_blocks = rows // BLOCK
    blocks = length // BLOCK
    my = lax.axis_index("head")
    own = pl.multiple_of(my * rows, rows)
    own_block = pl.multiple_of(my * own_blocks, own_blocks)
    lower = iota((1, 128), 1) < HD
    copies = load_weights(sources, (0, ATTN), layer, w_ref, sems)
    for p, piece in enumerate((hid0_ref, hid1_ref, hid2in_ref, hid3_ref)):
        hid_ref[pl.ds(pl.multiple_of(turned(p) * rows, rows), rows), :] = piece[...]
    for copy in copies:
        copy.wait()

    def project(step, _):
        j, tile = step // (length // rows), step % (length // rows)
        at = pl.multiple_of(tile * rows, rows)
        w = w_ref[j, :, :, C_KVS[0]:C_KVS[1]].reshape(width, C_KVS[1] - C_KVS[0])
        got = dot_nn(hid_ref[pl.ds(at, rows), :], w)
        kv_out[j, pl.ds(at, rows), :] = got[:, :256].astype(BF)
        sort_out[j, pl.ds(pl.multiple_of(tile * own_blocks, own_blocks), own_blocks), :] = jnp.sum(
            got[:, 256:].reshape(own_blocks, BLOCK, 128), 1
        ) / math.sqrt(BLOCK)
        return 0

    lax.fori_loop(0, pairs * (length // rows), project, 0)

    scores = jnp.stack(
        [sort_out[h // 2][:, (h % 2) * BLOCK:(h % 2) * BLOCK + blocks] for h in range(2 * pairs)]
    )
    perm_scr[...] = balance(scores, None)
    permo_out[...] = perm_scr[:, pl.ds(own_block, own_blocks), :]
    acc_scr[...] = stream_ref[...]
    take = GROUP * BLOCK

    def attend(j, _):
        wq = w_ref[j, :, :, C_Q[0]:C_Q[1]].reshape(width, 128)
        q = dot_nn(hid_ref[pl.ds(own, rows), :], wq).astype(BF)
        q_out[j] = q
        mixes = []
        for h in range(2):
            kron = kron_rows(permo_out[2 * j + h], length)
            skv = dot_nn(kron, kv_out[j, :, h * 128:(h + 1) * 128]).astype(BF)
            skv_out[j, h] = skv
            q_mine = jnp.where(lower if h == 0 else ~lower, q, jnp.zeros_like(q))
            kv_own = kv_out[j, pl.ds(own, rows), h * 128:(h + 1) * 128]
            pieces = []
            for g in range(rows // take):
                cut = slice(g * take, (g + 1) * take)
                kv_set = jnp.concatenate([skv[cut], kv_own[cut]], 0)
                raw = dot_nt(q_mine[cut], kv_set) * (1.0 / math.sqrt(HD))
                raw = jnp.where(group_mask(own_block + g * GROUP, take), raw, NEGATIVE)
                grown = jnp.exp(raw - jnp.max(raw, -1, keepdims=True))
                share = grown / jnp.sum(grown, -1, keepdims=True)
                attw_out[j, h, cut, :] = share
                pieces.append(dot_nn(share.astype(BF), kv_set))
            mixes.append(jnp.concatenate(pieces, 0))
        mixed = jnp.where(lower, mixes[1], mixes[0]).astype(BF)
        mixed_out[j] = mixed
        w_o = w_ref[j, :, :, C_OUT[0]:C_OUT[1]].reshape(width, 128)
        acc_scr[...] += dot_nt(mixed, w_o)
        return 0

    lax.fori_loop(0, pairs, attend, 0)

    middle = acc_scr[...]
    mid_out[...] = middle
    hid2_out[...] = norm_apply(middle, nrm_ref[0:1, :], nrm_ref[1:2, :])


def feed_forward_kernel(layer, count, mid_ref, hid2_ref, nrm_ref, *refs):
    sources = refs[:count]
    stream_out, hnext_out, upw_out, act_out, w_ref, acc_scr, sems = refs[count:]
    width = mid_ref.shape[1]
    pairs = w_ref.shape[0]
    copies = load_weights(sources, (ATTN, ATTN + FEED), layer, w_ref, sems)
    acc_scr[...] = mid_ref[...]
    for copy in copies:
        copy.wait()

    def feed(j, _):
        w_up = w_ref[j, :, :, C_UP[0]:C_UP[1]].reshape(width, 512)
        upward = dot_nn(hid2_ref[...], w_up)
        upw_out[j] = upward
        bent = jnp.tanh(GELU_C * (upward + GELU_A * upward * upward * upward))
        act = (0.5 * upward * (1.0 + bent)).astype(BF)
        act_out[j] = act
        w_dn = w_ref[j, :, :, C_DOWN[0]:C_DOWN[1]].reshape(width, 512)
        acc_scr[...] += dot_nt(act, w_dn)
        return 0

    lax.fori_loop(0, pairs, feed, 0)
    result = acc_scr[...]
    stream_out[...] = result
    hnext_out[...] = norm_apply(result, nrm_ref[0:1, :], nrm_ref[1:2, :])


VM = pl.BlockSpec(memory_space=pltpu.VMEM)
SM = pl.BlockSpec(memory_space=pltpu.SMEM)
FAR = pl.BlockSpec(memory_space=pl.ANY)
shape = jax.ShapeDtypeStruct


def settings(flops, traffic, name):
    return dict(
        compiler_params=pltpu.CompilerParams(vmem_limit_bytes=VMEM_LIMIT),
        cost_estimate=pl.CostEstimate(flops=flops, bytes_accessed=traffic, transcendentals=0),
        name=name,
    )


def weight_slots(sources, pairs, columns):
    parts, depth = (sources[0].shape[0], sources[0].shape[-2])
    return pltpu.VMEM((pairs, parts, depth, columns), BF)


def attend_forward(layer, hidden, stream, sources, nrm, after=(), flows=(), ident=0):
    rows, width = stream.shape
    pairs = len(hidden)
    length = rows * pairs
    own_blocks, blocks = rows // BLOCK, length // BLOCK
    outs = [
        shape((rows, width), F32),
        shape((rows, width), BF),
        shape((length, width), BF),
        shape((pairs, length, 256), BF),
        shape((pairs, rows, 128), BF),
        shape((pairs, 2, rows, 128), BF),
        shape((pairs, 2, rows, 2 * GROUP * BLOCK), F32),
        shape((pairs, rows, 128), BF),
        shape((2 * pairs, own_blocks, blocks), F32),
        shape((pairs, blocks, 128), F32),
    ]
    return call(
        functools.partial(attend_forward_kernel, layer, len(sources)),
        outs,
        [VM] * (pairs + 2) + [FAR] * len(sources),
        [VM] * len(outs),
        (*hidden, stream, nrm, *sources),
        after,
        flows,
        ident,
        scratch_shapes=[
            weight_slots(sources, pairs, ATTN),
            pltpu.VMEM((2 * pairs, blocks, blocks), F32),
            pltpu.VMEM((rows, width), F32),
            pltpu.SemaphoreType.DMA((pairs,)),
        ],
        **settings(18_000_000_000, 10_000_000, "attend_forward"),
    )


def feed_forward(layer, middle, hidden, sources, nrm, after=(), flows=(), ident=0):
    rows, width = middle.shape
    pairs = lax.axis_size("head")
    outs = [
        shape((rows, width), F32),
        shape((rows, width), BF),
        shape((pairs, rows, 512), F32),
        shape((pairs, rows, 512), BF),
    ]
    return call(
        functools.partial(feed_forward_kernel, layer, len(sources)),
        outs,
        [VM] * 3 + [FAR] * len(sources),
        [VM] * len(outs),
        (middle, hidden, nrm, *sources),
        after,
        scratch_shapes=[
            weight_slots(sources, pairs, FEED),
            pltpu.VMEM((rows, width), F32),
            pltpu.SemaphoreType.DMA((pairs,)),
        ],
        **settings(8_000_000_000, 8_000_000, "feed_forward"),
    )


def put(wgrad_scr, j, columns, value):
    parts, depth = wgrad_scr.shape[1:3]
    size = columns[1] - columns[0]
    wgrad_scr[j, :, :, columns[0]:columns[1]] = value.astype(BF).reshape(parts, depth, size)


def take_part(ref, index, features):
    depth = ref.shape[1]
    if depth == features:
        return ref[index].astype(F32)
    fold = depth // features
    whole = ref[index // fold].astype(F32).reshape(fold, features, ref.shape[2])
    return jnp.sum(jnp.where(iota(whole.shape, 0) == index % fold, whole, 0.0), 0)


def near_first(at):
    return 2 * at + 1 - 5 * (at // 2)


def feed_backward_kernel(
    layer, count, dy_ref, above_ref, carry_ref, gain_above_ref, gain_two_ref,
    mid_ref, hid2_ref, upw_ref, act_ref, *refs
):
    sources = refs[:count]
    (
        here_out, there_out, carry_out, pair_above_out, pair_two_out,
        w_ref, acc_scr, low_scr, wgrad_scr, near_scr, sems, send_sems, recv_sems,
    ) = refs[count:]
    width = carry_ref.shape[1]
    pairs = w_ref.shape[0]
    copies = load_weights(sources, (ATTN, ATTN + FEED), layer, w_ref, sems)

    back, pair = norm_back(dy_ref[...], above_ref[...], gain_above_ref[...])
    pair_above_out[...] = pair
    upstream = carry_ref[...] + back
    carry_out[...] = upstream
    low_scr[...] = upstream.astype(BF)
    acc_scr[...] = jnp.zeros_like(acc_scr)
    for copy in copies:
        copy.wait()

    def to_near(at):
        return remote(
            wgrad_scr.at[near_first(at)], near_scr.at[at], send_sems.at[at], recv_sems.at[at], *HEADS[0]
        )

    def feed(at, _):
        j = near_first(at)
        low = low_scr[...]
        w_dn = w_ref[j, :, :, C_DOWN[0]:C_DOWN[1]].reshape(width, 512)
        grad_act = dot_nn(low, w_dn)
        x = upw_ref[j]
        squared = x * x
        bent = jnp.tanh(GELU_C * (x + GELU_A * squared * x))
        slope = 0.5 * (1.0 + bent) + 0.5 * x * (1.0 - bent * bent) * (
            GELU_C * (1.0 + 3.0 * GELU_A * squared)
        )
        grad_up = (grad_act * slope).astype(BF)
        put(wgrad_scr, j, C_DOWN, dot_tn(low, act_ref[j]))
        put(wgrad_scr, j, C_UP, dot_tn(hid2_ref[...], grad_up))
        w_up = w_ref[j, :, :, C_UP[0]:C_UP[1]].reshape(width, 512)
        acc_scr[...] += dot_nt(grad_up, w_up)

        @pl.when(at < pairs // 2)
        def _():
            to_near(at).start()

        return 0

    lax.fori_loop(0, pairs, feed, 0)

    back, pair = norm_back(acc_scr[...], mid_ref[...], gain_two_ref[...])
    pair_two_out[...] = pair
    carry_out[...] += back
    odd = lax.axis_index("dp") % 2
    for x in range(pairs // 2):
        to_near(x).wait()
        for at in range(here_out.shape[1]):
            for out, way in ((here_out, odd), (there_out, 1 - odd)):
                out[x, at] = (
                    take_part(wgrad_scr.at[2 * x], 2 * at + way, out.shape[2])
                    + take_part(near_scr.at[x], 2 * at + way, out.shape[2])
                ).astype(BF)


def attend_backward_kernel(
    layer, count, carry_ref, hid_ref, kv_ref, q_ref, skv_ref, attw_ref, mixed_ref, permo_ref, sort_ref,
    *refs
):
    sources = refs[:count]
    (
        dy_out, mine_out, across_out,
        w_ref, ghid_scr, gkv_scr, gsrt_scr, gq_scr, dperm_scr, low_scr, wgrad_scr, near_scr,
        gsend_scr, gnear_scr, afar_scr, gfar_scr, sems, send_sems, recv_sems,
    ) = refs[count:]
    length, width = hid_ref.shape
    rows = carry_ref.shape[0]
    pairs, parts, depth = w_ref.shape[:3]
    own_blocks = rows // BLOCK
    blocks = length // BLOCK
    my = lax.axis_index("head")
    own = pl.multiple_of(my * rows, rows)
    own_block = pl.multiple_of(my * own_blocks, own_blocks)
    lower = iota((1, 128), 1) < HD
    take = GROUP * BLOCK
    copies = load_weights(sources, (0, ATTN), layer, w_ref, sems)
    low_scr[...] = carry_ref[...].astype(BF)
    dperm_scr[...] = jnp.zeros_like(dperm_scr)
    for copy in copies:
        copy.wait()
    scale_key = 1.0 / math.sqrt(HD)

    def attend(j, _):
        low = low_scr[...]
        w_o = w_ref[j, :, :, C_OUT[0]:C_OUT[1]].reshape(width, 128)
        grad_mixed = dot_nn(low, w_o).astype(BF)
        put(wgrad_scr, j, C_OUT, dot_tn(low, mixed_ref[j]))
        q = q_ref[j]
        zero = jnp.zeros_like(q)
        queries = []
        for h in range(2):
            key_lanes = lower if h == 0 else ~lower
            kron = kron_rows(permo_ref[2 * j + h], length)
            kv_all = kv_ref[j, :, h * 128:(h + 1) * 128]
            kv_own = kv_ref[j, pl.ds(own, rows), h * 128:(h + 1) * 128]
            skv = skv_ref[j, h]
            q_mine = jnp.where(key_lanes, q, zero)
            gm_mine = jnp.where(key_lanes, zero, grad_mixed)
            scale = jnp.where(key_lanes, scale_key, 1.0)
            gq, g_sorted, g_own = [], [], []
            for g in range(rows // take):
                cut = slice(g * take, (g + 1) * take)
                kv_set = jnp.concatenate([skv[cut], kv_own[cut]], 0)
                share = attw_ref[j, h, cut, :]
                grad_share = dot_nt(gm_mine[cut], kv_set)
                grad_raw = (
                    share * (grad_share - jnp.sum(share * grad_share, -1, keepdims=True))
                ).astype(BF)
                gq.append(dot_nn(grad_raw, kv_set) * scale_key)
                grad_set = (
                    dot_tn(grad_raw, q_mine[cut]) + dot_tn(share.astype(BF), gm_mine[cut])
                ) * scale
                g_sorted.append(grad_set[:take])
                g_own.append(grad_set[take:])
            queries.append(jnp.concatenate(gq, 0))
            grad_sorted = jnp.concatenate(g_sorted, 0).astype(BF)
            crossed = dot_nt(grad_sorted, kv_all)
            same = (iota((rows, length), 0) & (BLOCK - 1)) == (iota((rows, length), 1) & (BLOCK - 1))
            crossed = jnp.where(same, crossed, 0.0).reshape(own_blocks, BLOCK, length)
            dperm_scr[2 * j + h] = jnp.sum(crossed, 1)
            ghid_scr[:, 0:128] = dot_tn(kron, grad_sorted)
            ghid_scr[pl.ds(own, rows), 0:128] += jnp.concatenate(g_own, 0)
            gkv_scr[j, :, h * 128:(h + 1) * 128] = ghid_scr[:, 0:128].astype(BF)
        gq_scr[j] = jnp.where(lower, queries[0], queries[1]).astype(BF)
        return 0

    lax.fori_loop(0, pairs, attend, 0)

    heads = 2 * pairs
    gather = (iota((length, blocks), 0) // BLOCK == iota((length, blocks), 1)).astype(F32)
    dperm = lax.dot_general(
        dperm_scr[...].reshape(heads * own_blocks, length),
        gather,
        (((1,), (0,)), ((), ())),
        precision=lax.Precision.HIGHEST,
        preferred_element_type=F32,
    ).reshape(heads, own_blocks, blocks)
    scores = jnp.stack(
        [sort_ref[h // 2][:, (h % 2) * BLOCK:(h % 2) * BLOCK + blocks] for h in range(heads)]
    )
    full = jnp.concatenate([dperm] * (blocks // own_blocks), 1)
    block_at = iota(full.shape, 1)
    full = jnp.where((block_at >= own_block) & (block_at < own_block + own_blocks), full, 0.0)
    grad_sort = balance_back(scores, full) / math.sqrt(BLOCK)
    blank = jnp.zeros((blocks, 128 - 2 * blocks), F32)
    for j in range(pairs):
        gsrt_scr[j] = jnp.concatenate([grad_sort[2 * j], grad_sort[2 * j + 1], blank], 1)

    ghid_scr[...] = jnp.zeros_like(ghid_scr)

    def inward_of(j):
        spread = jnp.broadcast_to(gsrt_scr[j][:, None, :], (blocks, BLOCK, 128)).reshape(length, 128)
        return jnp.concatenate([gkv_scr[j], spread.astype(BF)], 1)

    def inward(j, _):
        w = w_ref[j, :, :, C_KVS[0]:C_KVS[1]].reshape(width, C_KVS[1] - C_KVS[0])
        ghid_scr[...] += dot_nt(inward_of(j), w)
        wq = w_ref[j, :, :, C_Q[0]:C_Q[1]].reshape(width, 128)
        ghid_scr[pl.ds(own, rows), :] += dot_nt(gq_scr[j], wq)
        return 0

    lax.fori_loop(0, pairs, inward, 0)

    def piece(p):
        return ghid_scr[pl.ds(pl.multiple_of(turned(p) * rows, rows), rows), :]

    for p in (1, 3):
        gsend_scr[p // 2] = piece(p).astype(BF)
    near = remote(gsend_scr, gnear_scr, send_sems.at[2], recv_sems.at[2], *HEADS[0])
    near.start()

    def to_near(at):
        return remote(
            wgrad_scr.at[near_first(at)], near_scr.at[at], send_sems.at[at], recv_sems.at[at], *HEADS[0]
        )

    def weigh(at, _):
        j = near_first(at)
        put(wgrad_scr, j, C_KVS, dot_tn(hid_ref[...], inward_of(j)))
        put(wgrad_scr, j, C_Q, dot_tn(hid_ref[pl.ds(own, rows), :], gq_scr[j]))

        @pl.when(at < pairs // 2)
        def _():
            to_near(at).start()

        return 0

    lax.fori_loop(0, pairs // 2, weigh, 0)
    near.wait()
    afar_scr[...] = (piece(2) + gnear_scr[1].astype(F32)).astype(BF)
    far = remote(afar_scr, gfar_scr, send_sems.at[3], recv_sems.at[3], *HEADS[1])
    far.start()
    lax.fori_loop(pairs // 2, pairs, weigh, 0)
    for x in range(pairs // 2):
        to_near(x).wait()
        out = across_out if x else mine_out
        for at in range(parts):
            out[at] = (wgrad_scr[2 * x, at].astype(F32) + near_scr[x, at].astype(F32)).astype(BF)
    far.wait()
    dy_out[...] = piece(0) + gnear_scr[0].astype(F32) + gfar_scr[...].astype(F32)


def feed_backward(layer, dy, above, carry, gain_above, sources, gain_two, kept, features, after=(), flows=(), ident=0):
    rows, width = carry.shape
    pairs = lax.axis_size("head")
    slots = weight_slots(sources, pairs, FEED)
    half = shape((pairs // 2, lax.axis_size("dp") // 2, features, FEED), BF)
    outs = [half, half, shape((rows, width), F32), shape((2, width), F32), shape((2, width), F32)]
    return call(
        functools.partial(feed_backward_kernel, layer, len(sources)),
        outs,
        [VM] * (5 + len(kept)) + [FAR] * len(sources),
        [VM] * 5,
        (dy, above, carry, gain_above, gain_two, *kept, *sources),
        after,
        flows,
        ident,
        HEADS[:1],
        scratch_shapes=[
            slots,
            pltpu.VMEM((rows, width), F32),
            pltpu.VMEM((rows, width), BF),
            slots,
            pltpu.VMEM((pairs // 2,) + slots.shape[1:], BF),
            pltpu.SemaphoreType.DMA((pairs,)),
            pltpu.SemaphoreType.DMA((2,)),
            pltpu.SemaphoreType.DMA((2,)),
        ],
        **settings(12_000_000_000, 12_000_000, "feed_backward"),
    )


def attend_backward(layer, carry, sources, kept, after=(), flows=(), ident=0):
    rows, width = carry.shape
    pairs = lax.axis_size("head")
    length = rows * pairs
    own_blocks, blocks = rows // BLOCK, length // BLOCK
    slots = weight_slots(sources, pairs, ATTN)
    return call(
        functools.partial(attend_backward_kernel, layer, len(sources)),
        [shape((rows, width), F32)] + [shape(slots.shape[1:], BF)] * 2,
        [VM] * (1 + len(kept)) + [FAR] * len(sources),
        [VM] * 3,
        (carry, *kept, *sources),
        after,
        flows,
        ident,
        HEADS,
        scratch_shapes=[
            slots,
            pltpu.VMEM((length, width), F32),
            pltpu.VMEM((pairs, length, 256), BF),
            pltpu.VMEM((pairs, blocks, 128), F32),
            pltpu.VMEM((pairs, rows, 128), BF),
            pltpu.VMEM((2 * pairs, own_blocks, length), F32),
            pltpu.VMEM((rows, width), BF),
            slots,
            pltpu.VMEM((pairs // 2,) + slots.shape[1:], BF),
            pltpu.VMEM((2, rows, width), BF),
            pltpu.VMEM((2, rows, width), BF),
            pltpu.VMEM((rows, width), BF),
            pltpu.VMEM((rows, width), BF),
            pltpu.SemaphoreType.DMA((pairs,)),
            pltpu.SemaphoreType.DMA((4,)),
            pltpu.SemaphoreType.DMA((4,)),
        ],
        **settings(20_000_000_000, 16_000_000, "attend_backward"),
    )


def embed_kernel(base_ref, tok_ref, table_ref, out_ref, tall_ref):
    features, vocab = table_ref.shape
    count = out_ref.shape[1]
    bins = vocab // 256

    @pl.when(pl.program_id(0) == 0)
    def _():
        for at in range(bins):
            tall_ref[at * features:(at + 1) * features, :] = table_ref[:, at * 256:(at + 1) * 256]

    local = tok_ref[...] - base_ref[0]
    high, low = local >> 8, local & 255
    hot = (iota((256, count), 0) == low).astype(BF)
    found = dot_nn(tall_ref[...], hot)
    total = jnp.zeros((features, count), F32)
    for at in range(bins):
        total = jnp.where(high == at, found[at * features:(at + 1) * features, :], total)
    out_ref[...] = total.astype(BF)


def embed_lookup(base, tokens, table, after=()):
    features, vocab = table.shape
    count = tokens.shape[1]
    tile = 512
    return call(
        embed_kernel,
        [jax.ShapeDtypeStruct((features, count), BF)],
        [
            pl.BlockSpec(memory_space=pltpu.SMEM),
            pl.BlockSpec((1, tile), lambda i: (0, i)),
            pl.BlockSpec((features, vocab), lambda i: (0, 0)),
        ],
        [pl.BlockSpec((features, tile), lambda i: (0, i))],
        (base, tokens, table),
        after,
        grid=(count // tile,),
        scratch_shapes=[pltpu.VMEM((features * (vocab // 256), 256), BF)],
        compiler_params=pltpu.CompilerParams(vmem_limit_bytes=VMEM_LIMIT),
        cost_estimate=pl.CostEstimate(flops=15_000_000_000, bytes_accessed=4_000_000, transcendentals=0),
        name="embed_lookup",
    )


def stages_of_all():
    return [(axis, bit) for axis in ("head", "dp") for bit in reversed(bits_of(axis))]


def embed_back_kernel(
    base_ref, tok_ref, grad_ref, head_ref, *refs, scale, count_pairs
):
    pair_refs = refs[:count_pairs]
    out_ref, square_out, pair_out, acc_ref, sum_scr, come_scr, send_sems, recv_sems = refs[count_pairs:]
    features = grad_ref.shape[0]
    count = grad_ref.shape[1]
    bins = acc_ref.shape[0] // features
    step = pl.program_id(0)
    stages = stages_of_all()
    first_hop = pl.num_programs(0) // 2

    def hop(at):
        return remote(sum_scr, come_scr.at[at], send_sems.at[at], recv_sems.at[at], *stages[at])

    for at in range(len(stages) + 1):

        @pl.when(step == first_hop + 3 * at)
        def _(at=at):
            if at == 0:
                for place, pair_ref in enumerate(pair_refs):
                    sum_scr[place] = pair_ref[...]
            else:
                hop(at - 1).wait()
                sum_scr[...] += come_scr[at - 1]
            if at < len(stages):
                hop(at).start()
            else:
                pair_out[...] = sum_scr[...]

    local = tok_ref[...] - base_ref[0]
    high, low = local >> 8, local & 255
    hot = (iota((256, count), 0) == low).astype(BF)
    grad = grad_ref[...]
    wide = jnp.concatenate(
        [jnp.where(high == at, grad, jnp.zeros_like(grad)) for at in range(bins)], 0
    )
    found = dot_nt(wide, hot)

    @pl.when(step == 0)
    def _():
        acc_ref[...] = found

    @pl.when(step > 0)
    def _():
        acc_ref[...] += found

    @pl.when(step == pl.num_programs(0) - 1)
    def _():
        squares = jnp.zeros((features, 256), F32)
        for at in range(bins):
            cut = slice(at * 256, (at + 1) * 256)
            total = scale * acc_ref[at * features:(at + 1) * features, :] + head_ref[:, cut].astype(F32)
            out_ref[:, cut] = total
            squares += total * total
        square_out[...] = squares


def embed_back(base, tokens, grad, head_grad, pair_grads, after=(), flows=(), ident=0):
    pieces, features, tile = grad.shape
    vocab = head_grad.shape[1]
    width = pair_grads[0].shape[1]
    count_pairs = len(pair_grads)
    all_pairs = (count_pairs, 2, width)
    stages = len(stages_of_all())
    still = lambda i: (0, 0)
    return call(
        functools.partial(embed_back_kernel, scale=math.sqrt(width), count_pairs=count_pairs),
        [shape((features, vocab), F32), shape((features, 256), F32), shape(all_pairs, F32)],
        [
            SM,
            pl.BlockSpec((1, tile), lambda i: (0, i)),
            pl.BlockSpec((None, features, tile), lambda i: (i, 0, 0)),
            pl.BlockSpec((features, vocab), still),
        ]
        + [pl.BlockSpec((2, width), still)] * count_pairs,
        [
            pl.BlockSpec((features, vocab), still),
            pl.BlockSpec((features, 256), still),
            pl.BlockSpec(all_pairs, lambda i: (0, 0, 0)),
        ],
        (base, tokens, grad, head_grad, *pair_grads),
        after,
        flows,
        ident,
        tuple(stages_of_all()),
        grid=(pieces,),
        scratch_shapes=[
            pltpu.VMEM((features * (vocab // 256), 256), F32),
            pltpu.VMEM(all_pairs, F32),
            pltpu.VMEM((stages,) + all_pairs, F32),
            pltpu.SemaphoreType.DMA((stages,)),
            pltpu.SemaphoreType.DMA((stages,)),
        ],
        **settings(15_000_000_000, 4_000_000, "embed_back"),
    )


def last_sums_kernel(
    a_ref, a_more_ref, b_ref, b_more_ref, other_ref, other_more_ref, third_ref, square_ref, pair_ref, loss_ref,
    out_ref, other_out, total_out,
    sum_scr, low_scr, come_scr, part_scr, parts_scr, send_sems, recv_sems, part_send, part_recv, *, bits, shared
):
    count = a_ref.shape[0]
    for t in range(count):
        sum_scr[t, :, 0:ATTN] = a_ref[t].astype(F32) + a_more_ref[t].astype(F32)
        sum_scr[t, :, ATTN:] = b_ref[t].astype(F32) + b_more_ref[t].astype(F32)
    at = 0
    place = 0
    for bit in bits:
        flag = (lax.axis_index("dp") // bit) % 2
        half = count // 2
        copies = []
        for t in range(half):
            low_scr[place + t] = sum_scr[2 * t + 1 - flag].astype(BF)
            copies.append(
                remote(
                    low_scr.at[place + t], come_scr.at[place + t], send_sems.at[at], recv_sems.at[at], "dp", bit
                )
            )
            copies[t].start()
            at += 1
        if place == 0:
            other = other_ref[...].astype(F32) + other_more_ref[...].astype(F32)
            other_out[...] = other
            pairs = pair_ref[...]
            square = jnp.sum(square_ref[...]) + jnp.sum(pairs * pairs) / shared + jnp.sum(other * other)
            for piece in third_ref:
                value = piece[...]
                square = square + jnp.sum(value * value)
        for t in range(half):
            copies[t].wait()
            sum_scr[t] = sum_scr[2 * t + flag] + come_scr[place + t].astype(F32)
        place += half
        count = half
    value = sum_scr[0]
    out_ref[...] = value
    square = square + jnp.sum(value * value)
    row, lane = iota((8, 128), 0), iota((8, 128), 1)
    part_scr[...] = jnp.where(
        row == 0, jnp.where(lane == 0, square, jnp.where(lane == 1, loss_ref[...], 0.0)), 0.0
    )
    for at, (axis, bit) in enumerate(stages_of_all()):
        hop = remote(part_scr, parts_scr.at[at], part_send.at[at], part_recv.at[at], axis, bit)
        hop.start()
        hop.wait()
        part_scr[...] += parts_scr[at]
    total_out[...] = part_scr[...]


def last_sums(attn, feed, other, thirds, squares, pair_grads, loss, bits, ident):
    def flat(value):
        return value.reshape((-1,) + value.shape[-2:])

    operands = [flat(one) for one in (*attn, *feed)] + [*other]
    count, features = operands[0].shape[:2]
    columns = ATTN + FEED
    stages = len(stages_of_all())
    one = shape((features, columns), F32)
    fixed, extra = len(operands), len(thirds)

    def kernel(*refs):
        last_sums_kernel(
            *refs[:fixed], refs[fixed:fixed + extra], *refs[fixed + extra:], bits=bits,
            shared=lax.axis_size("dp") * lax.axis_size("head"),
        )

    return call(
        kernel,
        [one, one, shape((8, 128), F32)],
        [VM] * (fixed + extra + 3),
        [VM] * 3,
        (*operands, *thirds, squares, pair_grads, loss),
        ident=ident,
        greet=tuple(stages_of_all()),
        scratch_shapes=[
            pltpu.VMEM((count, features, columns), F32),
            pltpu.VMEM((count - 1, features, columns), BF),
            pltpu.VMEM((count - 1, features, columns), BF),
            pltpu.VMEM((8, 128), F32),
            pltpu.VMEM((stages, 8, 128), F32),
            pltpu.SemaphoreType.DMA((count - 1,)),
            pltpu.SemaphoreType.DMA((count - 1,)),
            pltpu.SemaphoreType.DMA((stages,)),
            pltpu.SemaphoreType.DMA((stages,)),
        ],
        **settings(1_000_000, 4_000_000, "last_sums"),
    )


def update_kernel(layers, sort_width, total_ref, table_grad_ref, norm_grad_ref, *refs):
    packs, ins, outs = refs[:layers], list(refs[layers:layers + 18]), list(refs[layers + 18:])
    norm = jnp.sqrt(total_ref[0:1, 0:1])
    factor = jnp.minimum(1.0, CLIP_LIMIT / (norm + 1e-06))

    def run(member, at, grad):
        weight_ref, first_ref, second_ref = ins[3 * member:3 * member + 3]
        rate = RATE_NORM if member == 5 else RATE_MATRIX
        scale = factor.reshape((1,) * grad.ndim)
        new, one, two = adamw(weight_ref[at], grad, first_ref[at], second_ref[at], scale, rate)
        results = (new, one, two) if member == 5 else (new, new.astype(BF), one, two)
        for target, result in zip(outs[4 * member:], results):
            target[at] = result

    def table_part(step, _):
        at = (slice(None), pl.ds(pl.multiple_of(step * 512, 512), 512))
        run(0, at, table_grad_ref[at])
        return 0

    lax.fori_loop(0, table_grad_ref.shape[1] // 512, table_part, 0)
    kv, srt = C_KVS[0], C_KVS[0] + 256
    starts = ((0, kv, kv + 64, srt), (64, kv + 192, kv + 128, srt + sort_width))
    for layer, pack in enumerate(packs):
        for h, (q, k, v, sort) in enumerate(starts):
            parts = [pack[:, at:at + HD] for at in (q, k, v)] + [pack[:, sort:sort + sort_width]]
            run(1, (layer, slice(None), h, slice(None)), jnp.concatenate(parts, 1))
        out = pack[:, C_OUT[0]:C_OUT[1]].T
        for h in range(2):
            run(2, (layer, h), out[(1 - h) * HD:(2 - h) * HD])
        run(3, layer, pack[:, ATTN + C_UP[0]:ATTN + C_UP[1]])
        run(4, layer, pack[:, ATTN + C_DOWN[0]:ATTN + C_DOWN[1]])
    run(5, slice(None), norm_grad_ref[...])


def update(totals, packs, table_grad, norm_grad, sort_width, members):
    outs = []
    for weight, _, _ in members[:-1]:
        full = shape(weight.shape, F32)
        outs += [full, shape(weight.shape, BF), full, full]
    outs += [shape(norm_grad.shape, F32)] * 3
    operands = [totals, table_grad, norm_grad, *packs]
    for member in members:
        operands += member
    return call(
        functools.partial(update_kernel, len(packs), sort_width),
        outs,
        [VM] * len(operands),
        [VM] * len(outs),
        operands,
        **settings(1_000_000, 30_000_000, "update"),
    )[:-1]


def start_kernel(raw_ref, nrm_ref, stream_out, hid_out, *, scale):
    stream = raw_ref[...].astype(F32).T * scale
    stream_out[...] = stream
    hid_out[...] = norm_apply(stream, nrm_ref[0:1, :], nrm_ref[1:2, :])


def start_stream(raw, nrm, after=()):
    width, rows = raw.shape
    vm = pl.BlockSpec(memory_space=pltpu.VMEM)
    return call(
        functools.partial(start_kernel, scale=math.sqrt(width)),
        [
            jax.ShapeDtypeStruct((rows, width), F32),
            jax.ShapeDtypeStruct((rows, width), BF),
        ],
        [vm] * 2,
        [vm] * 2,
        (raw, nrm),
        after,
        name="start_stream",
    )


def finish_kernel(
    dy_ref, above_ref, carry_ref, gain_ref, pair_out, spread_out, piece_scr, own_sem, dp_send, dp_recv, send_sems, recv_sems, *, fly
):
    back, pair = norm_back(dy_ref[...], above_ref[...], gain_ref[...])
    pair_out[...] = pair
    piece_scr[...] = (carry_ref[...] + back).T.reshape(piece_scr.shape).astype(BF)
    count = piece_scr.shape[0]
    mine = lax.axis_index("dp")
    here = spread_out.at[0, mine]
    copies = [pltpu.make_async_copy(piece_scr.at[mine], here, own_sem)]
    for step in range(count - 1):
        peer = (mine + step + 1) % count
        copies.append(
            pltpu.make_async_remote_copy(
                src_ref=piece_scr.at[peer],
                dst_ref=here,
                send_sem=dp_send.at[step],
                recv_sem=dp_recv.at[step],
                device_id={"dp": peer},
                device_id_type=MESH,
            )
        )
    for copy in copies:
        copy.start()
    fly()
    for copy in copies:
        copy.wait()

    def hop(at, source, target, axis, bit):
        return remote(spread_out.at[source], spread_out.at[target], send_sems.at[at], recv_sems.at[at], axis, bit)

    far, near = hop(0, 0, 2, *HEADS[1]), hop(1, 0, 1, *HEADS[0])
    far.start()
    near.start()
    far.wait()
    cross = hop(2, 2, 3, *HEADS[0])
    cross.start()
    near.wait()
    cross.wait()


def finish_stream(dy, above, carry, gain, after=(), flows=(), ident=0):
    rows, width = above.shape
    dp, pairs = lax.axis_size("dp"), lax.axis_size("head")
    features = width // dp
    return call(
        finish_kernel,
        [shape((2, width), F32), shape((pairs, dp, features, rows), BF)],
        [VM] * 4,
        [VM, FAR],
        (dy, above, carry, gain),
        after,
        flows,
        ident,
        HEADS,
        "dp",
        hold=0,
        scratch_shapes=[
            pltpu.VMEM((dp, features, rows), BF),
            pltpu.SemaphoreType.DMA,
            pltpu.SemaphoreType.DMA((dp - 1,)),
            pltpu.SemaphoreType.DMA((dp - 1,)),
            pltpu.SemaphoreType.DMA((3,)),
            pltpu.SemaphoreType.DMA((3,)),
        ],
        name="finish_stream",
    )


def to_lanes(column):
    return jnp.broadcast_to(column, (column.shape[0], 128)).T[0:1, :]


def to_rows(line):
    return jnp.broadcast_to(line, (128, line.shape[1])).T[:, 0:1]


SLOTS = 8
SLOT_HOPS = (("head", 1, 4), ("head", 2, 2), ("dp", 1, 1))
GREET_SLOTS = HEADS + (("dp", 1),)


def head_forward_kernel(
    final_ref, table_ref, goal_ref, count_ref, rows_out, line_out, loss_out,
    rows_scr, stat_scr, come_scr, send_sems, recv_sems, stat_send, stat_recv
):
    def hop(at, source, target, which):
        axis, bit, _ = SLOT_HOPS[which]
        return remote(rows_scr.at[source], rows_scr.at[target], send_sems.at[at], recv_sems.at[at], axis, bit)

    rows_scr[0] = final_ref[...]
    core_own, low_own = hop(0, 0, 4, 0), hop(1, 0, 1, 2)
    far = [hop(2, 0, 2, 1), hop(3, 1, 3, 1)]
    core = [hop(4, 1, 5, 0), hop(5, 2, 6, 0), hop(6, 3, 7, 0)]
    core_own.start()
    low_own.start()
    far[0].start()

    def slot(at, _):
        @pl.when(at == 1)
        def _():
            core_own.wait()
            low_own.wait()
            far[1].start()
            core[0].start()

        @pl.when(at == 3)
        def _():
            core[0].wait()

        @pl.when(at == 4)
        def _():
            far[0].wait()
            core[1].start()
            far[1].wait()
            core[2].start()

        @pl.when(at == 6)
        def _():
            core[1].wait()
            core[2].wait()

        late = at // 4
        place = (1 - late) * (at // 2 + 4 * (at % 2)) + late * (2 + at % 2 + 4 * ((at // 2) % 2))
        logits = dot_nn(rows_scr[place], table_ref[...])
        top = jnp.max(logits, 1, keepdims=True)
        sums = jnp.sum(jnp.exp(logits - top), 1, keepdims=True)
        hit = iota(logits.shape, 1).astype(F32) == to_rows(goal_ref[place])
        pick = jnp.sum(jnp.where(hit, logits, 0.0), 1, keepdims=True)
        stat_scr[place, 0:1, :] = to_lanes(top)
        stat_scr[place, 1:2, :] = to_lanes(sums)
        stat_scr[place, 2:3, :] = to_lanes(pick)
        return 0

    lax.fori_loop(0, SLOTS, slot, 0)
    for at, (axis, bit, mask) in enumerate(SLOT_HOPS):
        meet = remote(stat_scr, come_scr.at[at], stat_send.at[at], stat_recv.at[at], axis, bit)
        meet.start()
        meet.wait()
        for place in range(SLOTS):
            mine, theirs = stat_scr[place], come_scr[at, place ^ mask]
            peak = jnp.maximum(mine[0:1], theirs[0:1])
            stat_scr[place, 1:2, :] = mine[1:2] * jnp.exp(mine[0:1] - peak) + theirs[1:2] * jnp.exp(
                theirs[0:1] - peak
            )
            stat_scr[place, 0:1, :] = peak
            stat_scr[place, 2:3, :] = mine[2:3] + theirs[2:3]
    loss = jnp.zeros((1, 1), F32)
    for place in range(SLOTS):
        mine = stat_scr[place]
        lse = mine[0:1] + jnp.log(mine[1:2])
        line_out[place, 0:1, :] = lse
        line_out[place, 1:2, :] = count_ref[place]
        loss += jnp.sum((lse - mine[2:3]) * count_ref[place], 1, keepdims=True)
    loss_out[...] = loss
    rows_out[...] = rows_scr[...]


def head_forward(final, table, goals, counted, ident):
    rows, width = final.shape
    hops = len(SLOT_HOPS)
    return call(
        head_forward_kernel,
        [shape((SLOTS, rows, width), BF), shape((SLOTS, 2, rows), F32), shape((1, 1), F32)],
        [VM] * 4,
        [VM] * 3,
        (final, table, goals, counted),
        ident=ident,
        greet=GREET_SLOTS,
        scratch_shapes=[
            pltpu.VMEM((SLOTS, rows, width), BF),
            pltpu.VMEM((SLOTS, 8, rows), F32),
            pltpu.VMEM((hops, SLOTS, 8, rows), F32),
            pltpu.SemaphoreType.DMA((7,)),
            pltpu.SemaphoreType.DMA((7,)),
            pltpu.SemaphoreType.DMA((hops,)),
            pltpu.SemaphoreType.DMA((hops,)),
        ],
        **settings(18_000_000_000, 6_000_000, "head_forward"),
    )


def head_backward_kernel(
    rows_ref, table_ref, goal_ref, line_ref, dy_out, gtab_out,
    acc_scr, grad_scr, send_scr, core_scr, far_scr, low_scr, keep_scr,
    core_send, core_recv, far_send, far_recv, low_send, low_recv
):
    rows = rows_ref.shape[1]

    def to_core(place):
        return remote(
            send_scr.at[place + 4], core_scr.at[place], core_send.at[place], core_recv.at[place], *HEADS[0]
        )

    def to_far(place):
        return remote(
            send_scr.at[place + 2], far_scr.at[place], far_send.at[place], far_recv.at[place], *HEADS[1]
        )

    to_low = remote(send_scr.at[1], low_scr, low_send, low_recv, "dp", 1)

    def pair(at, _):
        base = 6 - 4 * (at % 2) - 2 * (at // 2)
        for q in range(2):
            place = base + q + (at // 3) * (1 - 2 * q)
            logits = dot_nn(rows_ref[place], table_ref[...])
            hit = iota(logits.shape, 1).astype(F32) == to_rows(goal_ref[place])
            line = line_ref[place]
            chance = jnp.exp(logits - to_rows(line[0:1]))
            grad = ((chance - jnp.where(hit, 1.0, 0.0)) * to_rows(line[1:2])).astype(BF)
            grad_scr[q * rows:(q + 1) * rows, :] = grad
            part = dot_nt(grad, table_ref[...])

            @pl.when((at == 0) | (at == 2))
            def _():
                send_scr[place] = part.astype(BF)
                to_core(place - 4).start()

            @pl.when(at == 1)
            def _():
                to_core(place).wait()
                send_scr[place] = (part + core_scr[place].astype(F32)).astype(BF)
                to_far(place - 2).start()

            @pl.when(at == 3)
            def _():
                to_core(place).wait()
                to_far(place).wait()
                whole = part + core_scr[place].astype(F32) + far_scr[place].astype(F32)
                if q == 0:
                    send_scr[1] = whole.astype(BF)
                    to_low.start()
                else:
                    keep_scr[...] = whole

        both = [rows_ref[base + q + (at // 3) * (1 - 2 * q)] for q in range(2)]
        part = dot_tn(jnp.concatenate(both, 0), grad_scr[...])

        @pl.when(at == 0)
        def _():
            acc_scr[...] = part

        @pl.when(at > 0)
        def _():
            acc_scr[...] += part

        return 0

    lax.fori_loop(0, SLOTS // 2, pair, 0)
    gtab_out[...] = acc_scr[...].astype(BF)
    to_low.wait()
    dy_out[...] = keep_scr[...] + low_scr[...].astype(F32)


def head_backward(rows_all, table, goals, lines, ident):
    _, rows, width = rows_all.shape
    vocab = table.shape[1]
    return call(
        head_backward_kernel,
        [shape((rows, width), F32), shape((width, vocab), BF)],
        [VM] * 4,
        [VM] * 2,
        (rows_all, table, goals, lines),
        ident=ident,
        greet=GREET_SLOTS,
        scratch_shapes=[
            pltpu.VMEM((width, vocab), F32),
            pltpu.VMEM((2 * rows, vocab), BF),
            pltpu.VMEM((SLOTS, rows, width), BF),
            pltpu.VMEM((4, rows, width), BF),
            pltpu.VMEM((2, rows, width), BF),
            pltpu.VMEM((rows, width), BF),
            pltpu.VMEM((rows, width), F32),
            pltpu.SemaphoreType.DMA((4,)),
            pltpu.SemaphoreType.DMA((4,)),
            pltpu.SemaphoreType.DMA((2,)),
            pltpu.SemaphoreType.DMA((2,)),
            pltpu.SemaphoreType.DMA,
            pltpu.SemaphoreType.DMA,
        ],
        **settings(36_000_000_000, 14_000_000, "head_backward"),
    )


def swap(value, axis, bit):
    return lax.ppermute(value, axis, [(at, at ^ bit) for at in range(lax.axis_size(axis))])


def has_bit(axis, bit):
    return (lax.axis_index(axis) & bit) != 0


def bits_of(axis):
    size = lax.axis_size(axis)
    return [1 << at for at in reversed(range(size.bit_length() - 1))]


def in_order(mine, other, axis, bit, dim):
    flag = has_bit(axis, bit)
    return jnp.concatenate([jnp.where(flag, other, mine), jnp.where(flag, mine, other)], dim)


def gather_dp(value):
    bits = bits_of("dp")
    whole = value.reshape((1,) * len(bits) + value.shape)
    for dim, bit in enumerate(bits):
        whole = in_order(whole, swap(whole, "dp", bit), "dp", bit, dim)
    return whole.reshape((-1,) + value.shape)


def split(value, axis, bit, dim):
    flag = has_bit(axis, bit).astype(jnp.int32)
    low = value.astype(BF)
    return (
        lax.dynamic_index_in_dim(low, flag, dim, False),
        lax.dynamic_index_in_dim(low, 1 - flag, dim, False),
    )


def nothing_of(value):
    return value[(0,) * value.ndim].astype(F32) * 0.0


def add_up(*values):
    result = values[0].astype(F32)
    for value in values[1:]:
        result = result + (value.astype(F32) if value.ndim else value)
    return result


def sum_all(value, combine=jnp.add):
    for axis in ("head", "dp"):
        for bit in reversed(bits_of(axis)):
            value = combine(value, swap(value, axis, bit))
    return value


def pieces_of_head(value):
    across = swap(value, "head", 2)
    return value, swap(value, "head", 1), across, swap(across, "head", 1)


def pack_weights(attn_in, attn_out, ffn_up, ffn_down):
    features = attn_in.shape[0]
    low = attn_in.astype(BF)
    q, k, v = low[..., :HD], low[..., HD:2 * HD], low[..., 2 * HD:3 * HD]
    s = low[..., 3 * HD:].reshape(features, -1)
    blank = jnp.zeros((features, 128 - s.shape[1]), BF)
    out = attn_out.astype(BF)
    out = jnp.concatenate([out[1], out[0]], 0).T
    return jnp.concatenate(
        [
            q[:, 0], q[:, 1], k[:, 0], v[:, 0], v[:, 1], k[:, 1], s, blank,
            out, ffn_up.astype(BF), ffn_down.astype(BF).T,
        ],
        1,
    )


def depth_of(features):
    return max(64, features)


class Gather:
    def __init__(self, packed):
        self.bits = bits_of("dp")
        self.features = packed.shape[0]
        value = packed.reshape((1,) * len(self.bits) + packed.shape)
        for dim, bit in enumerate(self.bits[:-1]):
            value = in_order(value, swap(value, "dp", bit), "dp", bit, dim)
        self.value = value

    def last(self, value):
        dim, bit = len(self.bits) - 1, self.bits[-1]
        return in_order(value, swap(value, "dp", bit), "dp", bit, dim)

    def first_step(self):
        self.one, two = self.value[..., :ATTN], self.value[..., ATTN:]
        self.across = swap(self.one, "head", 2)
        self.two = two, swap(two, "dp", self.bits[-1])

    def second_step(self, token):
        dim, bit = len(self.bits) - 1, self.bits[-1]
        self.two = in_order(self.two[0], self.two[1] + token.astype(BF), "dp", bit, dim)
        self.one = self.last(self.one)
        self.across = self.last(self.across + token.astype(BF))

    def pieces(self, mine, across):
        return self.shape_pieces(mine, swap(mine, "head", 1), across, swap(across, "head", 1))

    def shape_pieces(self, *got):
        return [one.reshape(-1, depth_of(self.features), one.shape[-1]) for one in got]

    def finish(self):
        return self.pieces(self.one, self.across)

    def feed_flows(self):
        def once(bit):
            return (yield self.two, "head", bit)

        self.flows = [Flow(once(2)), Flow(once(1))]
        return self.flows

    def finish_feed(self):
        across, near = (flow.finish() for flow in self.flows)
        return self.shape_pieces(self.two, near, across, swap(across, "head", 1))


def gather_rest(packed):
    dp, head = lax.axis_size("dp"), lax.axis_size("head")
    layers, features, columns = packed.shape
    whole = lax.all_gather(packed, ("dp", "head"), axis=0, tiled=True)
    fold = depth_of(features) // features
    if fold > 1:
        whole = whole.reshape(dp // fold, fold, head, layers, features, columns)
        whole = whole.transpose(0, 2, 3, 1, 4, 5)
    return whole.reshape(dp // fold, head, layers, fold * features, columns)


def adamw(weight, gradient, moment_one, moment_two, factor, step_rate):
    gradient = gradient * factor
    moment_one = BETA_ONE * moment_one + (1.0 - BETA_ONE) * gradient
    moment_two = BETA_TWO * moment_two + (1.0 - BETA_TWO) * gradient * gradient
    adam_step = (
        moment_one
        / (1.0 - BETA_ONE**STEP)
        / (jnp.sqrt(moment_two / (1.0 - BETA_TWO**STEP)) + ADAM_FLOOR)
    )
    return (weight - step_rate * (adam_step + WEIGHT_DECAY * weight), moment_one, moment_two)


def body(
    tokens, targets, lengths,
    table, table_first, table_second,
    attn_in, attn_in_first, attn_in_second,
    attn_out, attn_out_first, attn_out_second,
    ffn_up, ffn_up_first, ffn_up_second,
    ffn_down, ffn_down_first, ffn_down_second,
    norms, norms_first, norms_second,
):
    dp, head = lax.axis_size("dp"), lax.axis_size("head")
    my_dp, my_head = lax.axis_index("dp"), lax.axis_index("head")
    seq_count, length = tokens.shape
    features, vocab = table.shape
    width = features * dp
    layers = attn_in.shape[0]
    rows = length // head
    total_tokens = dp * length
    odd = my_dp & 1
    outer = [[at for at in range(dp) if at % 2 == way] for way in range(2)]

    lines = jnp.concatenate([tokens, targets, jnp.broadcast_to(lengths[:, None], (seq_count, 128))], 1)
    lines = gather_dp(lines.reshape(-1))
    all_tokens = lines[:, :length].reshape(1, total_tokens)
    positions = jnp.arange(length, dtype=jnp.int32)
    counted = (positions[None, :] < lines[:, 2 * length:2 * length + 1]).astype(F32)
    nrm = norms
    for bit in (1, 2):
        nrm = in_order(nrm, swap(nrm, "head", bit), "head", bit, 2)

    low_table = table.astype(BF)
    packs = [
        pack_weights(attn_in[at], attn_out[at], ffn_up[at], ffn_down[at]) for at in range(layers)
    ]
    leader = Gather(packs[0])

    half = vocab // 2
    other = swap(lax.dynamic_slice_in_dim(low_table, (1 - odd) * half, half, 1), "dp", 1)
    mine = lax.dynamic_slice_in_dim(low_table, odd * half, half, 1)
    head_table = in_order(mine, other, "dp", 1, 0)

    base = (my_head * vocab).astype(jnp.int32).reshape(1)
    found, token = embed_lookup(base, all_tokens, low_table, [leader.value])
    leader.first_step()
    rest_weights = gather_rest(jnp.stack(packs[1:]) + token.astype(BF))
    found = found.reshape(features, dp, head, rows)
    for bit in (1, 2):
        flag = (my_head & bit) // bit
        found = found.reshape(features, dp, -1, 2, rows) if bit == 1 else found.reshape(features, dp, 2, rows)
        dim = 3 if bit == 1 else 2
        other = swap(lax.dynamic_index_in_dim(found, 1 - flag, dim, False), "head", bit)
        found = lax.dynamic_index_in_dim(found, flag, dim, False) + other
    leader.second_step(token)
    found = lax.all_to_all(found, "dp", split_axis=1, concat_axis=0, tiled=True)
    stream, hidden, token = start_stream(found.reshape(width, rows), nrm[0])
    head_table = lax.all_gather(
        head_table + token.astype(BF), "dp", axis=0, tiled=True, axis_index_groups=outer
    )
    hidden = pieces_of_head(hidden)
    sources = [[leader.finish(), None]] + [[[rest_weights], [rest_weights]]] * (layers - 1)

    kept = []
    for at in range(layers):
        of = max(at - 1, 0)
        for_attend, for_feed = sources[at]
        middle, hidden_two, *saved, token = attend_forward(
            of, hidden, stream, for_attend, nrm[2 * at + 1], [],
            leader.feed_flows() if at == 0 else [],
        )
        if at == 0:
            for_feed = sources[0][1] = leader.finish_feed()
        result, hidden, upward, active, _ = feed_forward(
            of, middle, hidden_two, for_feed, nrm[2 * at + 2]
        )
        kept.append((stream, (middle, hidden_two, upward, active), saved))
        stream = result
        if at + 1 < layers:
            hidden = pieces_of_head(hidden)

    def line_of(values):
        values = values.reshape(dp, head, rows)
        order = [(my_dp ^ y, my_head ^ (x * 2 + c)) for c in range(2) for x in range(2) for y in range(2)]
        picked = [
            lax.dynamic_slice(values, (d, h, 0), (1, 1, rows)).reshape(rows) for d, h in order
        ]
        return jnp.concatenate(picked)

    goals = line_of(lines[:, length:2 * length]) - (my_head * vocab + odd * half).astype(jnp.int32)
    goals = goals.astype(F32).reshape(SLOTS, 1, rows)
    idents = iter(range(1, 64))
    rows_all, stat_lines, loss_here, token = head_forward(
        hidden, head_table, goals, line_of(counted).reshape(SLOTS, 1, rows), next(idents)
    )
    loss_here = loss_here / (2 * head)
    count_total = jnp.sum(counted)
    dy, grad_half, token = head_backward(rows_all, head_table, goals, stat_lines, next(idents))
    grad_half = lax.psum_scatter(
        grad_half, "dp", scatter_dimension=0, tiled=True, axis_index_groups=outer
    ).reshape(2, features, half)

    carry = jnp.zeros((rows, width), F32)
    above = stream
    pair_grads = [None] * (2 * layers + 1)
    bits = bits_of("dp")

    def shaped(value):
        return value.reshape((2,) * len(bits) + (features, value.shape[-1]))

    def attn_steps(mine, theirs):
        across = yield theirs, "head", 2
        here, there = split(shaped(add_up(mine, across)), "dp", bits[-1], len(bits) - 1)
        return here, (yield there, "dp", bits[-1])

    def feed_steps(here, there):
        value = add_up(here, (yield there, "dp", bits[-1]))
        parts = value[0], (yield value[1].astype(BF), "head", 2)
        return tuple(part.reshape((2,) * (len(bits) - 1) + part.shape[-2:]) for part in parts)

    def last_steps(attn, feed):
        value = jnp.concatenate([add_up(*attn.parts), add_up(*feed.parts)], -1)
        for dim, bit in reversed(list(enumerate(bits[:-1]))):
            here, there = split(value, "dp", bit, dim)
            parts = here, (yield there, "dp", bit)
            value = add_up(*parts)
        return parts

    attns, feeds, lasts = [None] * layers, [None] * layers, [None] * layers

    def active(*candidates):
        return [flow for flow in candidates if flow is not None and flow.ask is not None]

    for at in reversed(range(layers)):
        of = max(at - 1, 0)
        stream_in, for_feed, for_attend = kept[at]
        above_attn, above_feed = (attns + [None])[at + 1], (feeds + [None])[at + 1]
        top_attn, top_feed = (attns + [None] * 2)[at + 2], (feeds + [None] * 2)[at + 2]
        here, there, carry, pair_above, pair_two, token = feed_backward(
            of, dy, above, carry, nrm[2 * at + 2, 0:1], sources[at][1], nrm[2 * at + 1, 0:1], for_feed,
            features, [grad_half] if at == 0 else [], active(top_attn, above_attn if at == 0 else None), next(idents),
        )
        feeds[at] = Flow(feed_steps(here, there))
        if at + 2 < layers:
            lasts[at + 2] = Flow(last_steps(top_attn, top_feed))
        dy, *attn_sums, token = attend_backward(
            of, carry, sources[at][0], for_attend, [],
            active(feeds[at], above_attn, above_feed, *lasts), next(idents),
        )
        attns[at] = Flow(attn_steps(*attn_sums))
        pair_grads[2 * at + 2] = pair_above
        pair_grads[2 * at + 1] = pair_two
        above = stream_in
    def once(value, axis, bit):
        return (yield value, axis, bit)

    grad_half = Flow(once(lax.dynamic_index_in_dim(grad_half, 1 - odd, 0, False), "dp", 1)), (
        lax.dynamic_index_in_dim(grad_half, odd, 0, False)
    )
    lasts[1] = Flow(last_steps(attns[1], feeds[1]))
    pair_grads[0], spread, token = finish_stream(
        dy, above, carry, nrm[0, 0:1], [], active(attns[0], grad_half[0], *lasts), next(idents)
    )

    head_grad = in_order(grad_half[1], grad_half[0].value, "dp", 1, 1)
    spread = spread.reshape(head * dp, features, rows)
    by_rows = all_tokens.reshape(dp, head, rows)
    order = [lax.dynamic_index_in_dim(by_rows, my_head ^ p, 1, False) for p in range(head)]
    grad_table, squares, grad_norms, token = embed_back(
        base, jnp.stack(order).reshape(1, total_tokens), spread, head_grad,
        pair_grads, [],
        active(attns[0], feeds[0], *lasts), next(idents),
    )
    sort_width = attn_in.shape[3] - 3 * HD
    thirds = [flow.finish() for flow in lasts[2:]]
    while lasts[1].ask is not None:
        lasts[1].give(swap(*lasts[1].ask))
    lower, other, totals, token = last_sums(
        attns[0].parts, feeds[0].parts, lasts[1].parts, thirds, squares, grad_norms, loss_here.reshape(1, 1),
        tuple(reversed(bits[:-1])), next(idents),
    )
    grad_norms = lax.dynamic_slice_in_dim(
        grad_norms, my_head * norms.shape[2], norms.shape[2], 2
    )
    results = update(
        totals, [lower, other] + thirds, grad_table, grad_norms, sort_width,
        [
            (table, table_first, table_second),
            (attn_in, attn_in_first, attn_in_second),
            (attn_out, attn_out_first, attn_out_second),
            (ffn_up, ffn_up_first, ffn_up_second),
            [one.transpose(0, 2, 1) for one in (ffn_down, ffn_down_first, ffn_down_second)],
            (norms, norms_first, norms_second),
        ],
    )
    results = list(results)
    results[16:20] = [one.transpose(0, 2, 1) for one in results[16:20]]
    return (jnp.stack([totals[0, 1], count_total]), jnp.sqrt(totals[0, 0]), *results)


def solution(mesh):
    ints = [P("dp", None), P("dp", None), P("dp")]
    by_table = P("dp", "head")
    by_in = P(None, "dp", "head", None)
    by_out = P(None, "head", None, "dp")
    by_up = P(None, "dp", "head")
    by_down = P(None, "head", "dp")
    by_norm = P(None, None, "head")
    in_specs, out_specs = list(ints), [P(), P()]
    for spec in (by_table, by_in, by_out, by_up, by_down):
        in_specs += [spec] * 3
        out_specs += [spec] * 4
    in_specs += [by_norm] * 3
    out_specs += [by_norm] * 3
    return jax.shard_map(
        body, mesh=mesh, in_specs=tuple(in_specs), out_specs=tuple(out_specs), check_vma=False
    )
```

```python
import functools
import math

import jax
import jax.numpy as jnp
from jax import lax
from jax.experimental import pallas as pl
from jax.experimental.pallas import tpu as pltpu
from jax.sharding import PartitionSpec as P

HD = 64
BLOCK = 32
SINK = 8
STEP = 10
EPSILON = 1e-05
NEGATIVE = -1000000000.0
TEMPER = 0.75
BETA_ONE = 0.9
BETA_TWO = 0.999
ADAM_FLOOR = 1e-08
WEIGHT_DECAY = 0.01
RATE_MATRIX = 0.1
RATE_NORM = 0.5
CLIP_LIMIT = 1.0

BF = jnp.bfloat16
F32 = jnp.float32
GROUP = 4
GELU_C = math.sqrt(2.0 / math.pi)
GELU_A = 0.044715

C_Q = (0, 128)
C_KVS = (128, 512)
C_OUT = (512, 640)
ATTN = 640
C_UP = (0, 512)
C_DOWN = (512, 1024)
FEED = 1024
VMEM_LIMIT = 56 * 1024 * 1024


def dot_nn(a, b):
    return lax.dot_general(a, b, (((1,), (0,)), ((), ())), preferred_element_type=F32)


def dot_nt(a, b):
    return lax.dot_general(a, b, (((1,), (1,)), ((), ())), preferred_element_type=F32)


def dot_tn(a, b):
    return lax.dot_general(a, b, (((0,), (0,)), ((), ())), preferred_element_type=F32)


def iota(shape, axis):
    return lax.broadcasted_iota(jnp.int32, shape, axis)


MESH = pl.DeviceIdType.MESH


def flipped(axis, bit):
    mine = lax.axis_index(axis)
    return mine + bit - 2 * bit * ((mine // bit) % 2)


def remote(source, target, send_sem, recv_sem, axis, bit):
    return pltpu.make_async_remote_copy(
        src_ref=source,
        dst_ref=target,
        send_sem=send_sem,
        recv_sem=recv_sem,
        device_id={axis: flipped(axis, bit)},
        device_id_type=MESH,
    )


HEADS = (("head", 1), ("head", 2))


def call(
    kernel, outs, in_specs, out_specs, operands, after=(), flows=(), ident=0, greet=(), greet_all=(), hold=None, **options
):
    used, spare, token, riders = len(operands), len(after), len(outs), len(flows)
    asks = [flow.ask for flow in flows]
    pairs = sorted({ask[1:] for ask in asks} | set(greet))
    pairs = [pair for pair in pairs if pair[0] not in greet_all]
    grid = options.get("grid")
    scratch = list(options.pop("scratch_shapes", []))
    far = pl.BlockSpec(memory_space=pl.ANY)

    def run(*refs):
        ins, rest = refs[:used], refs[used + spare:]
        sends, rest = rest[:riders], rest[riders:]
        results, token_ref, rest = rest[:token], rest[token], rest[token + 1:]
        lands, rest = rest[:riders], rest[riders:]
        if riders:
            rest, (send_sems, recv_sems) = rest[:-2], rest[-2:]

        def copies():
            if not riders:
                return []
            return [
                remote(sends[at], lands[at], send_sems.at[at], recv_sems.at[at], axis, bit)
                for at, (_, axis, bit) in enumerate(asks)
            ]

        def launch():
            barrier = pltpu.get_barrier_semaphore()
            for axis, bit in pairs:
                pl.semaphore_signal(
                    barrier, inc=1, device_id={axis: flipped(axis, bit)}, device_id_type=MESH
                )
            others = 0
            for axis in greet_all:
                count = lax.axis_size(axis)
                for step in range(1, count):
                    peer = (lax.axis_index(axis) + step) % count
                    pl.semaphore_signal(barrier, inc=1, device_id={axis: peer}, device_id_type=MESH)
                others += count - 1
            pl.semaphore_wait(barrier, len(pairs) + others)
            if hold is None:
                fly()

        def fly():
            for copy in copies():
                copy.start()

        def settle():
            for copy in copies():
                copy.wait()

        if riders or greet or greet_all:
            pl.when(pl.program_id(0) == 0)(launch) if grid else launch()
        token_ref[...] = jnp.zeros((1, 128), F32)
        if hold is not None and grid:
            if riders:
                pl.when(pl.program_id(0) == hold)(fly)
            kernel(*ins, *results, *rest)
        elif hold is not None:
            kernel(*ins, *results, *rest, fly=fly)
        else:
            kernel(*ins, *results, *rest)
        if riders:
            pl.when(pl.program_id(0) == grid[0] - 1)(settle) if grid else settle()

    if riders or greet or greet_all:
        options["compiler_params"] = pltpu.CompilerParams(
            vmem_limit_bytes=VMEM_LIMIT, collective_id=ident, has_side_effects=True
        )
    if riders:
        scratch += [pltpu.SemaphoreType.DMA((riders,))] * 2
    token_spec = (
        pl.BlockSpec((1, 128), lambda i: (0, 0)) if grid else pl.BlockSpec(memory_space=pltpu.VMEM)
    )
    got = pl.pallas_call(
        run,
        out_shape=list(outs)
        + [jax.ShapeDtypeStruct((1, 128), F32)]
        + [jax.ShapeDtypeStruct(ask[0].shape, ask[0].dtype) for ask in asks],
        in_specs=list(in_specs) + [far] * (spare + riders),
        out_specs=list(out_specs) + [token_spec] + [far] * riders,
        scratch_shapes=scratch,
        **options,
    )(*operands, *after, *[ask[0] for ask in asks])
    for flow, value in zip(flows, got[token + 1:]):
        flow.give(value)
    return (*got[:token], got[token][0, 0])


class Flow:
    def __init__(self, steps):
        self.steps, self.parts = steps, None
        self.give(None)

    @property
    def value(self):
        return self.parts

    def give(self, got):
        try:
            self.ask = self.steps.send(got)
        except StopIteration as stop:
            self.ask, self.parts = None, stop.value

    def finish(self):
        while self.ask is not None:
            self.give(swap(*self.ask))
        return add_up(*self.parts) if isinstance(self.parts, tuple) else self.parts


def norm_stats(stream):
    average = jnp.mean(stream, -1, keepdims=True)
    variance = jnp.mean(stream * stream, -1, keepdims=True) - average * average
    inv_std = lax.rsqrt(variance + EPSILON)
    return (stream - average) * inv_std, inv_std


def norm_apply(stream, gain, bias):
    normed, _ = norm_stats(stream)
    return (normed * gain + bias).astype(BF)


def norm_back(upstream, stream, gain):
    normed, inv_std = norm_stats(stream)
    scaled = upstream * gain
    back = inv_std * (
        scaled
        - jnp.mean(scaled, -1, keepdims=True)
        - normed * jnp.mean(scaled * normed, -1, keepdims=True)
    )
    pair = jnp.concatenate(
        [jnp.sum(upstream * normed, 0, keepdims=True), jnp.sum(upstream, 0, keepdims=True)], 0
    )
    return back, pair


def allowed_mask(shape):
    return iota(shape, len(shape) - 1) < iota(shape, len(shape) - 2)


def log_total(x, axis):
    top = jnp.max(x, axis, keepdims=True)
    return top + jnp.log(jnp.sum(jnp.exp(x - top), axis, keepdims=True))


def balance(scores, keep):
    allowed = allowed_mask(scores.shape)
    plan = jnp.where(allowed, scores / TEMPER, NEGATIVE)
    for _ in range(SINK):
        for axis in (-2, -1):
            plan = jnp.where(allowed, plan - log_total(plan, axis), NEGATIVE)
            if keep is not None:
                keep.append(plan)
    return jnp.where(allowed, jnp.exp(plan), 0.0)


def balance_back(scores, upstream):
    allowed = allowed_mask(scores.shape)
    plans = []
    perm = balance(scores, plans)
    grad = jnp.where(allowed, upstream * perm, 0.0)
    for step in reversed(range(2 * SINK)):
        axis = (-2, -1)[step % 2]
        share = jnp.exp(plans[step])
        grad = jnp.where(allowed, grad - share * jnp.sum(grad, axis, keepdims=True), 0.0)
    return grad / TEMPER


def kron_rows(perm_rows, length):
    own, blocks = perm_rows.shape
    rows = own * BLOCK
    tall = jnp.broadcast_to(perm_rows[:, None, :], (own, BLOCK, blocks)).reshape(rows, blocks)
    spread = (iota((blocks, length), 1) // BLOCK == iota((blocks, length), 0)).astype(BF)
    wide = dot_nn(tall.astype(BF), spread)
    same = (iota((rows, length), 0) & (BLOCK - 1)) == (iota((rows, length), 1) & (BLOCK - 1))
    return jnp.where(same, wide, 0.0).astype(BF)


def group_mask(first_block, rows):
    shape = (rows, 2 * rows)
    row, slot = iota(shape, 0), iota(shape, 1)
    row_block = row // BLOCK
    in_sorted = slot < rows
    place = jnp.where(in_sorted, slot, slot - rows)
    same = (place // BLOCK) == row_block
    sorted_ok = in_sorted & (row_block + first_block >= 1)
    own_ok = (slot >= rows) & (place <= row)
    return same & (sorted_ok | own_ok)


def turned(p):
    mine = lax.axis_index("head")
    low, high = mine % 2, (mine // 2) % 2
    rest = mine - low - 2 * high
    return rest + (1 - low if p & 1 else low) + 2 * (1 - high if p & 2 else high)


def load_weights(sources, low, w_ref, sems):
    copies = []
    for p in range(w_ref.shape[0]):
        if len(sources) > 1:
            source = sources[p]
        else:
            source = sources[0].at[:, turned(p), :, low:low + w_ref.shape[3]]
        copies.append(pltpu.make_async_copy(source, w_ref.at[p], sems.at[p]))
        copies[p].start()
    return copies


def attend_forward_kernel(low, count, hidden_ref, stream_ref, nrm_ref, *refs):
    sources = refs[:count]
    (
        mid_out, hid2_out, hid_ref, kv_out, q_out, skv_out, attw_out, mixed_out, permo_out, sort_out,
        w_ref, perm_scr, acc_scr, piece_scr, sems, send_sems, recv_sems,
    ) = refs[count:]
    length, width = hid_ref.shape
    rows = stream_ref.shape[0]
    pairs = w_ref.shape[0]
    own_blocks = rows // BLOCK
    blocks = length // BLOCK
    my = lax.axis_index("head")
    own = pl.multiple_of(my * rows, rows)
    own_block = pl.multiple_of(my * own_blocks, own_blocks)
    lower = iota((1, 128), 1) < HD
    copies = load_weights(sources, low, w_ref, sems)

    def hop(at, source, target, which):
        return remote(
            piece_scr.at[source], piece_scr.at[target], send_sems.at[at], recv_sems.at[at], *HEADS[which]
        )

    far, near, cross = hop(0, 0, 2, 1), hop(1, 0, 1, 0), hop(2, 2, 3, 0)
    piece_scr[0] = hidden_ref[...]
    far.start()
    near.start()
    for copy in copies:
        copy.wait()

    def project(p):
        tile = turned(p)
        at = pl.ds(pl.multiple_of(tile * rows, rows), rows)
        blocks_at = pl.ds(pl.multiple_of(tile * own_blocks, own_blocks), own_blocks)
        hid_ref[at, :] = piece_scr[p]

        def columns(j, _):
            w = w_ref[j, :, :, C_KVS[0]:C_KVS[1]].reshape(width, C_KVS[1] - C_KVS[0])
            got = dot_nn(piece_scr[p], w)
            kv_out[j, at, :] = got[:, :256].astype(BF)
            sort_out[j, blocks_at, :] = jnp.sum(got[:, 256:].reshape(own_blocks, BLOCK, 128), 1) / math.sqrt(BLOCK)
            return 0

        lax.fori_loop(0, pairs, columns, 0)

    project(0)
    near.wait()
    project(1)
    far.wait()
    cross.start()
    project(2)
    cross.wait()
    project(3)

    scores = jnp.stack(
        [sort_out[h // 2][:, (h % 2) * BLOCK:(h % 2) * BLOCK + blocks] for h in range(2 * pairs)]
    )
    perm_scr[...] = balance(scores, None)
    permo_out[...] = perm_scr[:, pl.ds(own_block, own_blocks), :]
    acc_scr[...] = stream_ref[...]
    take = GROUP * BLOCK

    def attend(j, _):
        wq = w_ref[j, :, :, C_Q[0]:C_Q[1]].reshape(width, 128)
        q = dot_nn(hid_ref[pl.ds(own, rows), :], wq).astype(BF)
        q_out[j] = q
        mixes = []
        for h in range(2):
            kron = kron_rows(permo_out[2 * j + h], length)
            skv = dot_nn(kron, kv_out[j, :, h * 128:(h + 1) * 128]).astype(BF)
            skv_out[j, h] = skv
            q_mine = jnp.where(lower if h == 0 else ~lower, q, jnp.zeros_like(q))
            kv_own = kv_out[j, pl.ds(own, rows), h * 128:(h + 1) * 128]
            pieces = []
            for g in range(rows // take):
                cut = slice(g * take, (g + 1) * take)
                kv_set = jnp.concatenate([skv[cut], kv_own[cut]], 0)
                raw = dot_nt(q_mine[cut], kv_set) * (1.0 / math.sqrt(HD))
                raw = jnp.where(group_mask(own_block + g * GROUP, take), raw, NEGATIVE)
                grown = jnp.exp(raw - jnp.max(raw, -1, keepdims=True))
                share = grown / jnp.sum(grown, -1, keepdims=True)
                attw_out[j, h, cut, :] = share
                pieces.append(dot_nn(share.astype(BF), kv_set))
            mixes.append(jnp.concatenate(pieces, 0))
        mixed = jnp.where(lower, mixes[1], mixes[0]).astype(BF)
        mixed_out[j] = mixed
        w_o = w_ref[j, :, :, C_OUT[0]:C_OUT[1]].reshape(width, 128)
        acc_scr[...] += dot_nt(mixed, w_o)
        return 0

    lax.fori_loop(0, pairs, attend, 0)

    middle = acc_scr[...]
    mid_out[...] = middle
    hid2_out[...] = norm_apply(middle, nrm_ref[0:1, :], nrm_ref[1:2, :])


def feed_forward_kernel(low, count, mid_ref, hid2_ref, nrm_ref, *refs):
    sources = refs[:count]
    stream_out, hnext_out, upw_out, act_out, w_ref, acc_scr, sems = refs[count:]
    width = mid_ref.shape[1]
    pairs = w_ref.shape[0]
    copies = load_weights(sources, low, w_ref, sems)
    acc_scr[...] = mid_ref[...]
    for copy in copies:
        copy.wait()

    def feed(j, _):
        w_up = w_ref[j, :, :, C_UP[0]:C_UP[1]].reshape(width, 512)
        upward = dot_nn(hid2_ref[...], w_up)
        upw_out[j] = upward
        bent = jnp.tanh(GELU_C * (upward + GELU_A * upward * upward * upward))
        act = (0.5 * upward * (1.0 + bent)).astype(BF)
        act_out[j] = act
        w_dn = w_ref[j, :, :, C_DOWN[0]:C_DOWN[1]].reshape(width, 512)
        acc_scr[...] += dot_nt(act, w_dn)
        return 0

    lax.fori_loop(0, pairs, feed, 0)
    result = acc_scr[...]
    stream_out[...] = result
    hnext_out[...] = norm_apply(result, nrm_ref[0:1, :], nrm_ref[1:2, :])


VM = pl.BlockSpec(memory_space=pltpu.VMEM)
SM = pl.BlockSpec(memory_space=pltpu.SMEM)
FAR = pl.BlockSpec(memory_space=pl.ANY)
shape = jax.ShapeDtypeStruct


def settings(flops, traffic, name):
    return dict(
        compiler_params=pltpu.CompilerParams(vmem_limit_bytes=VMEM_LIMIT),
        cost_estimate=pl.CostEstimate(flops=flops, bytes_accessed=traffic, transcendentals=0),
        name=name,
    )


def weight_slots(sources, pairs, columns):
    parts, depth = (sources[0].shape[0], sources[0].shape[-2])
    return pltpu.VMEM((pairs, parts, depth, columns), BF)


def attend_forward(low, hidden, stream, sources, nrm, after=(), flows=(), ident=0):
    rows, width = stream.shape
    pairs = lax.axis_size("head")
    length = rows * pairs
    own_blocks, blocks = rows // BLOCK, length // BLOCK
    outs = [
        shape((rows, width), F32),
        shape((rows, width), BF),
        shape((length, width), BF),
        shape((pairs, length, 256), BF),
        shape((pairs, rows, 128), BF),
        shape((pairs, 2, rows, 128), BF),
        shape((pairs, 2, rows, 2 * GROUP * BLOCK), F32),
        shape((pairs, rows, 128), BF),
        shape((2 * pairs, own_blocks, blocks), F32),
        shape((pairs, blocks, 128), F32),
    ]
    return call(
        functools.partial(attend_forward_kernel, low, len(sources)),
        outs,
        [VM] * 3 + [FAR] * len(sources),
        [VM] * len(outs),
        (hidden, stream, nrm, *sources),
        after,
        flows,
        ident,
        HEADS,
        scratch_shapes=[
            weight_slots(sources, pairs, ATTN),
            pltpu.VMEM((2 * pairs, blocks, blocks), F32),
            pltpu.VMEM((rows, width), F32),
            pltpu.VMEM((pairs, rows, width), BF),
            pltpu.SemaphoreType.DMA((pairs,)),
            pltpu.SemaphoreType.DMA((3,)),
            pltpu.SemaphoreType.DMA((3,)),
        ],
        **settings(18_000_000_000, 10_000_000, "attend_forward"),
    )


def feed_forward(low, middle, hidden, sources, nrm, after=(), flows=(), ident=0):
    rows, width = middle.shape
    pairs = lax.axis_size("head")
    outs = [
        shape((rows, width), F32),
        shape((rows, width), BF),
        shape((pairs, rows, 512), F32),
        shape((pairs, rows, 512), BF),
    ]
    return call(
        functools.partial(feed_forward_kernel, low, len(sources)),
        outs,
        [VM] * 3 + [FAR] * len(sources),
        [VM] * len(outs),
        (middle, hidden, nrm, *sources),
        after,
        scratch_shapes=[
            weight_slots(sources, pairs, FEED),
            pltpu.VMEM((rows, width), F32),
            pltpu.SemaphoreType.DMA((pairs,)),
        ],
        **settings(8_000_000_000, 8_000_000, "feed_forward"),
    )


def put(wgrad_scr, j, columns, value):
    parts, depth = wgrad_scr.shape[1:3]
    size = columns[1] - columns[0]
    wgrad_scr[j, :, :, columns[0]:columns[1]] = value.astype(BF).reshape(parts, depth, size)


def take_part(ref, index, features):
    depth = ref.shape[1]
    if depth == features:
        return ref[index].astype(F32)
    fold = depth // features
    whole = ref[index // fold].astype(F32).reshape(fold, features, ref.shape[2])
    return jnp.sum(jnp.where(iota(whole.shape, 0) == index % fold, whole, 0.0), 0)


def near_first(at):
    return 2 * at + 1 - 5 * (at // 2)


def feed_backward_kernel(
    low, count, dy_ref, above_ref, carry_ref, gain_above_ref, gain_two_ref,
    mid_ref, hid2_ref, upw_ref, act_ref, *refs
):
    sources = refs[:count]
    (
        here_out, there_out, carry_out, pair_above_out, pair_two_out,
        w_ref, acc_scr, low_scr, wgrad_scr, near_scr, sems, send_sems, recv_sems,
    ) = refs[count:]
    width = carry_ref.shape[1]
    pairs = w_ref.shape[0]
    copies = load_weights(sources, low, w_ref, sems)

    back, pair = norm_back(dy_ref[...], above_ref[...], gain_above_ref[...])
    pair_above_out[...] = pair
    upstream = carry_ref[...] + back
    carry_out[...] = upstream
    low_scr[...] = upstream.astype(BF)
    acc_scr[...] = jnp.zeros_like(acc_scr)
    for copy in copies:
        copy.wait()

    def to_near(at):
        return remote(
            wgrad_scr.at[near_first(at)], near_scr.at[at], send_sems.at[at], recv_sems.at[at], *HEADS[0]
        )

    def feed(at, _):
        j = near_first(at)
        rounded = low_scr[...]
        w_dn = w_ref[j, :, :, C_DOWN[0]:C_DOWN[1]].reshape(width, 512)
        grad_act = dot_nn(rounded, w_dn)
        x = upw_ref[j]
        squared = x * x
        bent = jnp.tanh(GELU_C * (x + GELU_A * squared * x))
        slope = 0.5 * (1.0 + bent) + 0.5 * x * (1.0 - bent * bent) * (
            GELU_C * (1.0 + 3.0 * GELU_A * squared)
        )
        grad_up = (grad_act * slope).astype(BF)
        put(wgrad_scr, j, C_DOWN, dot_tn(rounded, act_ref[j]))
        put(wgrad_scr, j, C_UP, dot_tn(hid2_ref[...], grad_up))
        w_up = w_ref[j, :, :, C_UP[0]:C_UP[1]].reshape(width, 512)
        acc_scr[...] += dot_nt(grad_up, w_up)

        @pl.when(at < pairs // 2)
        def _():
            to_near(at).start()

        return 0

    lax.fori_loop(0, pairs, feed, 0)

    back, pair = norm_back(acc_scr[...], mid_ref[...], gain_two_ref[...])
    pair_two_out[...] = pair
    carry_out[...] += back
    odd = lax.axis_index("dp") % 2
    for x in range(pairs // 2):
        to_near(x).wait()
        for at in range(here_out.shape[1]):
            for out, way in ((here_out, odd), (there_out, 1 - odd)):
                out[x, at] = (
                    take_part(wgrad_scr.at[2 * x], 2 * at + way, out.shape[2])
                    + take_part(near_scr.at[x], 2 * at + way, out.shape[2])
                ).astype(BF)


def attend_backward_kernel(
    low, count, carry_ref, hid_ref, kv_ref, q_ref, skv_ref, attw_ref, mixed_ref, permo_ref, sort_ref,
    *refs
):
    sources = refs[:count]
    (
        dy_out, mine_out, across_out,
        w_ref, ghid_scr, gkv_scr, gsrt_scr, gq_scr, dperm_scr, low_scr, wgrad_scr, near_scr,
        gsend_scr, gnear_scr, afar_scr, gfar_scr, sems, send_sems, recv_sems,
    ) = refs[count:]
    length, width = hid_ref.shape
    rows = carry_ref.shape[0]
    pairs, parts, depth = w_ref.shape[:3]
    own_blocks = rows // BLOCK
    blocks = length // BLOCK
    my = lax.axis_index("head")
    own = pl.multiple_of(my * rows, rows)
    own_block = pl.multiple_of(my * own_blocks, own_blocks)
    lower = iota((1, 128), 1) < HD
    take = GROUP * BLOCK
    copies = load_weights(sources, low, w_ref, sems)
    low_scr[...] = carry_ref[...].astype(BF)
    dperm_scr[...] = jnp.zeros_like(dperm_scr)
    for copy in copies:
        copy.wait()
    scale_key = 1.0 / math.sqrt(HD)

    def attend(j, _):
        rounded = low_scr[...]
        w_o = w_ref[j, :, :, C_OUT[0]:C_OUT[1]].reshape(width, 128)
        grad_mixed = dot_nn(rounded, w_o).astype(BF)
        put(wgrad_scr, j, C_OUT, dot_tn(rounded, mixed_ref[j]))
        q = q_ref[j]
        zero = jnp.zeros_like(q)
        queries = []
        for h in range(2):
            key_lanes = lower if h == 0 else ~lower
            kron = kron_rows(permo_ref[2 * j + h], length)
            kv_all = kv_ref[j, :, h * 128:(h + 1) * 128]
            kv_own = kv_ref[j, pl.ds(own, rows), h * 128:(h + 1) * 128]
            skv = skv_ref[j, h]
            q_mine = jnp.where(key_lanes, q, zero)
            gm_mine = jnp.where(key_lanes, zero, grad_mixed)
            scale = jnp.where(key_lanes, scale_key, 1.0)
            gq, g_sorted, g_own = [], [], []
            for g in range(rows // take):
                cut = slice(g * take, (g + 1) * take)
                kv_set = jnp.concatenate([skv[cut], kv_own[cut]], 0)
                share = attw_ref[j, h, cut, :]
                grad_share = dot_nt(gm_mine[cut], kv_set)
                grad_raw = (
                    share * (grad_share - jnp.sum(share * grad_share, -1, keepdims=True))
                ).astype(BF)
                gq.append(dot_nn(grad_raw, kv_set) * scale_key)
                grad_set = (
                    dot_tn(grad_raw, q_mine[cut]) + dot_tn(share.astype(BF), gm_mine[cut])
                ) * scale
                g_sorted.append(grad_set[:take])
                g_own.append(grad_set[take:])
            queries.append(jnp.concatenate(gq, 0))
            grad_sorted = jnp.concatenate(g_sorted, 0).astype(BF)
            crossed = dot_nt(grad_sorted, kv_all)
            same = (iota((rows, length), 0) & (BLOCK - 1)) == (iota((rows, length), 1) & (BLOCK - 1))
            crossed = jnp.where(same, crossed, 0.0).reshape(own_blocks, BLOCK, length)
            dperm_scr[2 * j + h] = jnp.sum(crossed, 1)
            ghid_scr[:, 0:128] = dot_tn(kron, grad_sorted)
            ghid_scr[pl.ds(own, rows), 0:128] += jnp.concatenate(g_own, 0)
            gkv_scr[j, :, h * 128:(h + 1) * 128] = ghid_scr[:, 0:128].astype(BF)
        gq_scr[j] = jnp.where(lower, queries[0], queries[1]).astype(BF)
        return 0

    lax.fori_loop(0, pairs, attend, 0)

    heads = 2 * pairs
    gather = (iota((length, blocks), 0) // BLOCK == iota((length, blocks), 1)).astype(F32)
    dperm = lax.dot_general(
        dperm_scr[...].reshape(heads * own_blocks, length),
        gather,
        (((1,), (0,)), ((), ())),
        precision=lax.Precision.HIGHEST,
        preferred_element_type=F32,
    ).reshape(heads, own_blocks, blocks)
    scores = jnp.stack(
        [sort_ref[h // 2][:, (h % 2) * BLOCK:(h % 2) * BLOCK + blocks] for h in range(heads)]
    )
    full = jnp.concatenate([dperm] * (blocks // own_blocks), 1)
    block_at = iota(full.shape, 1)
    full = jnp.where((block_at >= own_block) & (block_at < own_block + own_blocks), full, 0.0)
    grad_sort = balance_back(scores, full) / math.sqrt(BLOCK)
    blank = jnp.zeros((blocks, 128 - 2 * blocks), F32)
    for j in range(pairs):
        gsrt_scr[j] = jnp.concatenate([grad_sort[2 * j], grad_sort[2 * j + 1], blank], 1)

    ghid_scr[...] = jnp.zeros_like(ghid_scr)

    def inward_of(j):
        spread = jnp.broadcast_to(gsrt_scr[j][:, None, :], (blocks, BLOCK, 128)).reshape(length, 128)
        return jnp.concatenate([gkv_scr[j], spread.astype(BF)], 1)

    def inward(j, _):
        w = w_ref[j, :, :, C_KVS[0]:C_KVS[1]].reshape(width, C_KVS[1] - C_KVS[0])
        ghid_scr[...] += dot_nt(inward_of(j), w)
        wq = w_ref[j, :, :, C_Q[0]:C_Q[1]].reshape(width, 128)
        ghid_scr[pl.ds(own, rows), :] += dot_nt(gq_scr[j], wq)
        return 0

    lax.fori_loop(0, pairs, inward, 0)

    def piece(p):
        return ghid_scr[pl.ds(pl.multiple_of(turned(p) * rows, rows), rows), :]

    for p in (1, 3):
        gsend_scr[p // 2] = piece(p).astype(BF)
    near = remote(gsend_scr, gnear_scr, send_sems.at[2], recv_sems.at[2], *HEADS[0])
    near.start()

    def to_near(at):
        return remote(
            wgrad_scr.at[near_first(at)], near_scr.at[at], send_sems.at[at], recv_sems.at[at], *HEADS[0]
        )

    def weigh(at, _):
        j = near_first(at)
        put(wgrad_scr, j, C_KVS, dot_tn(hid_ref[...], inward_of(j)))
        put(wgrad_scr, j, C_Q, dot_tn(hid_ref[pl.ds(own, rows), :], gq_scr[j]))

        @pl.when(at < pairs // 2)
        def _():
            to_near(at).start()

        return 0

    lax.fori_loop(0, pairs // 2, weigh, 0)
    near.wait()
    afar_scr[...] = (piece(2) + gnear_scr[1].astype(F32)).astype(BF)
    far = remote(afar_scr, gfar_scr, send_sems.at[3], recv_sems.at[3], *HEADS[1])
    far.start()
    lax.fori_loop(pairs // 2, pairs, weigh, 0)
    for x in range(pairs // 2):
        to_near(x).wait()
        out = across_out if x else mine_out
        for at in range(parts):
            out[at] = (wgrad_scr[2 * x, at].astype(F32) + near_scr[x, at].astype(F32)).astype(BF)
    far.wait()
    dy_out[...] = piece(0) + gnear_scr[0].astype(F32) + gfar_scr[...].astype(F32)


def feed_backward(low, dy, above, carry, gain_above, sources, gain_two, kept, features, after=(), flows=(), ident=0):
    rows, width = carry.shape
    pairs = lax.axis_size("head")
    slots = weight_slots(sources, pairs, FEED)
    half = shape((pairs // 2, lax.axis_size("dp") // 2, features, FEED), BF)
    outs = [half, half, shape((rows, width), F32), shape((2, width), F32), shape((2, width), F32)]
    return call(
        functools.partial(feed_backward_kernel, low, len(sources)),
        outs,
        [VM] * (5 + len(kept)) + [FAR] * len(sources),
        [VM] * 5,
        (dy, above, carry, gain_above, gain_two, *kept, *sources),
        after,
        flows,
        ident,
        HEADS[:1],
        scratch_shapes=[
            slots,
            pltpu.VMEM((rows, width), F32),
            pltpu.VMEM((rows, width), BF),
            slots,
            pltpu.VMEM((pairs // 2,) + slots.shape[1:], BF),
            pltpu.SemaphoreType.DMA((pairs,)),
            pltpu.SemaphoreType.DMA((2,)),
            pltpu.SemaphoreType.DMA((2,)),
        ],
        **settings(12_000_000_000, 12_000_000, "feed_backward"),
    )


def attend_backward(low, carry, sources, kept, after=(), flows=(), ident=0):
    rows, width = carry.shape
    pairs = lax.axis_size("head")
    length = rows * pairs
    own_blocks, blocks = rows // BLOCK, length // BLOCK
    slots = weight_slots(sources, pairs, ATTN)
    return call(
        functools.partial(attend_backward_kernel, low, len(sources)),
        [shape((rows, width), F32)] + [shape(slots.shape[1:], BF)] * 2,
        [VM] * (1 + len(kept)) + [FAR] * len(sources),
        [VM] * 3,
        (carry, *kept, *sources),
        after,
        flows,
        ident,
        HEADS,
        scratch_shapes=[
            slots,
            pltpu.VMEM((length, width), F32),
            pltpu.VMEM((pairs, length, 256), BF),
            pltpu.VMEM((pairs, blocks, 128), F32),
            pltpu.VMEM((pairs, rows, 128), BF),
            pltpu.VMEM((2 * pairs, own_blocks, length), F32),
            pltpu.VMEM((rows, width), BF),
            slots,
            pltpu.VMEM((pairs // 2,) + slots.shape[1:], BF),
            pltpu.VMEM((2, rows, width), BF),
            pltpu.VMEM((2, rows, width), BF),
            pltpu.VMEM((rows, width), BF),
            pltpu.VMEM((rows, width), BF),
            pltpu.SemaphoreType.DMA((pairs,)),
            pltpu.SemaphoreType.DMA((4,)),
            pltpu.SemaphoreType.DMA((4,)),
        ],
        **settings(20_000_000_000, 16_000_000, "attend_backward"),
    )


def embed_kernel(base_ref, tok_ref, table_ref, out_ref, tall_ref):
    features, vocab = table_ref.shape
    count = out_ref.shape[1]
    bins = vocab // 256

    @pl.when(pl.program_id(0) == 0)
    def _():
        for at in range(bins):
            tall_ref[at * features:(at + 1) * features, :] = table_ref[:, at * 256:(at + 1) * 256]

    local = tok_ref[...] - base_ref[0]
    high, low = local >> 8, local & 255
    hot = (iota((256, count), 0) == low).astype(BF)
    found = dot_nn(tall_ref[...], hot)
    total = jnp.zeros((features, count), F32)
    for at in range(bins):
        total = jnp.where(high == at, found[at * features:(at + 1) * features, :], total)
    out_ref[...] = total.astype(BF)


def embed_lookup(base, tokens, table, after=()):
    features, vocab = table.shape
    count = tokens.shape[1]
    tile = 512
    return call(
        embed_kernel,
        [jax.ShapeDtypeStruct((features, count), BF)],
        [
            pl.BlockSpec(memory_space=pltpu.SMEM),
            pl.BlockSpec((1, tile), lambda i: (0, i)),
            pl.BlockSpec((features, vocab), lambda i: (0, 0)),
        ],
        [pl.BlockSpec((features, tile), lambda i: (0, i))],
        (base, tokens, table),
        after,
        grid=(count // tile,),
        scratch_shapes=[pltpu.VMEM((features * (vocab // 256), 256), BF)],
        compiler_params=pltpu.CompilerParams(vmem_limit_bytes=VMEM_LIMIT),
        cost_estimate=pl.CostEstimate(flops=15_000_000_000, bytes_accessed=4_000_000, transcendentals=0),
        name="embed_lookup",
    )


def stages_of_all():
    return [("head", bit) for bit in bits_of("head")] + [("dp", bit) for bit in reversed(bits_of("dp"))]


def embed_back_kernel(
    base_ref, tok_ref, grad_ref, head_ref, *refs, scale, count_pairs
):
    pair_refs = refs[:count_pairs]
    out_ref, square_out, pair_out, acc_ref, sum_scr, come_scr, send_sems, recv_sems = refs[count_pairs:]
    pieces, features, tile = grad_ref.shape
    count = pieces * tile
    bins = acc_ref.shape[0] // features
    step = pl.program_id(0)
    stages = stages_of_all()
    first_hop = pl.num_programs(0) - len(stages) - 1
    hop_step = [0] + [first_hop + at for at in range(1, len(stages) + 1)]

    def hop(at):
        return remote(sum_scr, come_scr.at[at], send_sems.at[at], recv_sems.at[at], *stages[at])

    for at in range(len(stages) + 1):

        @pl.when(step == hop_step[at])
        def _(at=at):
            if at == 0:
                for place, pair_ref in enumerate(pair_refs):
                    sum_scr[place] = pair_ref[...]
            else:
                hop(at - 1).wait()
                sum_scr[...] += come_scr[at - 1]
            if at < len(stages):
                hop(at).start()
            else:
                pair_out[...] = sum_scr[...]

    local = tok_ref[...] - base_ref[0]
    high, low = local >> 8, local & 255
    hot = (iota((256, count), 0) == low).astype(BF)
    grad = jnp.concatenate([grad_ref[at] for at in range(pieces)], 1)
    wide = jnp.concatenate(
        [jnp.where(high == at, grad, jnp.zeros_like(grad)) for at in range(bins)], 0
    )
    found = dot_nt(wide, hot)

    @pl.when(step == 0)
    def _():
        acc_ref[...] = found

    @pl.when(step > 0)
    def _():
        acc_ref[...] += found

    @pl.when(step == pl.num_programs(0) - 1)
    def _():
        squares = jnp.zeros((features, 256), F32)
        for at in range(bins):
            cut = slice(at * 256, (at + 1) * 256)
            total = scale * acc_ref[at * features:(at + 1) * features, :] + head_ref[:, cut].astype(F32)
            out_ref[:, cut] = total
            squares += total * total
        square_out[...] = squares


def embed_back(base, tokens, grad, head_grad, pair_grads, after=(), flows=(), ident=0):
    pieces, features, tile = grad.shape
    vocab = head_grad.shape[1]
    width = pair_grads[0].shape[1]
    count_pairs = len(pair_grads)
    all_pairs = (count_pairs, 2, width)
    stages = len(stages_of_all())
    still = lambda i: (0, 0)
    return call(
        functools.partial(embed_back_kernel, scale=math.sqrt(width), count_pairs=count_pairs),
        [shape((features, vocab), F32), shape((features, 256), F32), shape(all_pairs, F32)],
        [
            SM,
            pl.BlockSpec((1, 4 * tile), lambda i: (0, i)),
            pl.BlockSpec((4, features, tile), lambda i: (i, 0, 0)),
            pl.BlockSpec((features, vocab), still),
        ]
        + [pl.BlockSpec((2, width), still)] * count_pairs,
        [
            pl.BlockSpec((features, vocab), still),
            pl.BlockSpec((features, 256), still),
            pl.BlockSpec(all_pairs, lambda i: (0, 0, 0)),
        ],
        (base, tokens, grad, head_grad, *pair_grads),
        after,
        flows,
        ident,
        tuple(stages_of_all()),
        hold=1,
        grid=(pieces // 4,),
        scratch_shapes=[
            pltpu.VMEM((features * (vocab // 256), 256), F32),
            pltpu.VMEM(all_pairs, F32),
            pltpu.VMEM((stages,) + all_pairs, F32),
            pltpu.SemaphoreType.DMA((stages,)),
            pltpu.SemaphoreType.DMA((stages,)),
        ],
        **settings(15_000_000_000, 4_000_000, "embed_back"),
    )


def last_sums_kernel(
    a_ref, a_more_ref, b_ref, b_more_ref, other_ref, other_more_ref, third_ref, square_ref, pair_ref, loss_ref,
    out_ref, other_out, total_out,
    sum_scr, low_scr, come_scr, part_scr, parts_scr, send_sems, recv_sems, part_send, part_recv, *, bits, shared
):
    count = a_ref.shape[0]
    for t in range(count):
        sum_scr[t, :, 0:ATTN] = a_ref[t].astype(F32) + a_more_ref[t].astype(F32)
        sum_scr[t, :, ATTN:] = b_ref[t].astype(F32) + b_more_ref[t].astype(F32)
    at = 0
    place = 0
    for bit in bits:
        flag = (lax.axis_index("dp") // bit) % 2
        half = count // 2
        copies = []
        for t in range(half):
            low_scr[place + t] = sum_scr[2 * t + 1 - flag].astype(BF)
            copies.append(
                remote(
                    low_scr.at[place + t], come_scr.at[place + t], send_sems.at[at], recv_sems.at[at], "dp", bit
                )
            )
            copies[t].start()
            at += 1
        if place == 0:
            other = other_ref[...].astype(F32) + other_more_ref[...].astype(F32)
            other_out[...] = other
            pairs = pair_ref[...]
            square = jnp.sum(square_ref[...]) + jnp.sum(pairs * pairs) / shared + jnp.sum(other * other)
            for piece in third_ref:
                value = piece[...]
                square = square + jnp.sum(value * value)
        for t in range(half):
            copies[t].wait()
            sum_scr[t] = sum_scr[2 * t + flag] + come_scr[place + t].astype(F32)
        place += half
        count = half
    value = sum_scr[0]
    out_ref[...] = value
    square = square + jnp.sum(value * value)
    row, lane = iota((8, 128), 0), iota((8, 128), 1)
    part_scr[...] = jnp.where(
        row == 0, jnp.where(lane == 0, square, jnp.where(lane == 1, loss_ref[...], 0.0)), 0.0
    )
    place = 0
    for axis in ("head", "dp"):
        count = lax.axis_size(axis)
        hops = []
        here = place + lax.axis_index(axis)
        parts_scr[here] = part_scr[...]
        for step in range(1, count):
            at = place + step - 1
            hops.append(
                pltpu.make_async_remote_copy(
                    src_ref=part_scr,
                    dst_ref=parts_scr.at[here],
                    send_sem=part_send.at[at],
                    recv_sem=part_recv.at[at],
                    device_id={axis: (lax.axis_index(axis) + step) % count},
                    device_id_type=MESH,
                )
            )
            hops[-1].start()
        for hop in hops:
            hop.wait()
        part_scr[...] = jnp.sum(parts_scr[place:place + count], 0)
        place += count
    total_out[...] = part_scr[...]


def last_sums(attn, feed, other, thirds, squares, pair_grads, loss, bits, ident):
    def flat(value):
        return value.reshape((-1,) + value.shape[-2:])

    operands = [flat(one) for one in (*attn, *feed)] + [*other]
    count, features = operands[0].shape[:2]
    columns = ATTN + FEED
    stages = lax.axis_size("head") + lax.axis_size("dp")
    one = shape((features, columns), F32)
    fixed, extra = len(operands), len(thirds)

    def kernel(*refs):
        last_sums_kernel(
            *refs[:fixed], refs[fixed:fixed + extra], *refs[fixed + extra:], bits=bits,
            shared=lax.axis_size("dp") * lax.axis_size("head"),
        )

    return call(
        kernel,
        [one, one, shape((8, 128), F32)],
        [VM] * (fixed + extra + 3),
        [VM] * 3,
        (*operands, *thirds, squares, pair_grads, loss),
        ident=ident,
        greet_all=("head", "dp"),
        scratch_shapes=[
            pltpu.VMEM((count, features, columns), F32),
            pltpu.VMEM((count - 1, features, columns), BF),
            pltpu.VMEM((count - 1, features, columns), BF),
            pltpu.VMEM((8, 128), F32),
            pltpu.VMEM((stages, 8, 128), F32),
            pltpu.SemaphoreType.DMA((count - 1,)),
            pltpu.SemaphoreType.DMA((count - 1,)),
            pltpu.SemaphoreType.DMA((stages,)),
            pltpu.SemaphoreType.DMA((stages,)),
        ],
        **settings(1_000_000, 4_000_000, "last_sums"),
    )


def update_kernel(layers, sort_width, total_ref, table_grad_ref, norm_grad_ref, *refs):
    packs, ins, outs = refs[:layers], list(refs[layers:layers + 18]), list(refs[layers + 18:])
    norm = jnp.sqrt(total_ref[0:1, 0:1])
    factor = jnp.minimum(1.0, CLIP_LIMIT / (norm + 1e-06))

    def run(member, at, grad):
        weight_ref, first_ref, second_ref = ins[3 * member:3 * member + 3]
        rate = RATE_NORM if member == 5 else RATE_MATRIX
        scale = factor.reshape((1,) * grad.ndim)
        new, one, two = adamw(weight_ref[at], grad, first_ref[at], second_ref[at], scale, rate)
        results = (new, one, two) if member == 5 else (new, new.astype(BF), one, two)
        for target, result in zip(outs[4 * member:], results):
            target[at] = result

    def table_part(step, _):
        at = (slice(None), pl.ds(pl.multiple_of(step * 512, 512), 512))
        run(0, at, table_grad_ref[at])
        return 0

    lax.fori_loop(0, table_grad_ref.shape[1] // 512, table_part, 0)
    kv, srt = C_KVS[0], C_KVS[0] + 256
    starts = ((0, kv, kv + 64, srt), (64, kv + 192, kv + 128, srt + sort_width))
    for layer, pack in enumerate(packs):
        for h, (q, k, v, sort) in enumerate(starts):
            parts = [pack[:, at:at + HD] for at in (q, k, v)] + [pack[:, sort:sort + sort_width]]
            run(1, (layer, slice(None), h, slice(None)), jnp.concatenate(parts, 1))
        out = pack[:, C_OUT[0]:C_OUT[1]].T
        for h in range(2):
            run(2, (layer, h), out[(1 - h) * HD:(2 - h) * HD])
        run(3, layer, pack[:, ATTN + C_UP[0]:ATTN + C_UP[1]])
        run(4, layer, pack[:, ATTN + C_DOWN[0]:ATTN + C_DOWN[1]])
    run(5, slice(None), norm_grad_ref[...])


def update(totals, packs, table_grad, norm_grad, sort_width, members):
    outs = []
    for weight, _, _ in members[:-1]:
        full = shape(weight.shape, F32)
        outs += [full, shape(weight.shape, BF), full, full]
    outs += [shape(norm_grad.shape, F32)] * 3
    operands = [totals, table_grad, norm_grad, *packs]
    for member in members:
        operands += member
    return call(
        functools.partial(update_kernel, len(packs), sort_width),
        outs,
        [VM] * len(operands),
        [VM] * len(outs),
        operands,
        **settings(1_000_000, 30_000_000, "update"),
    )[:-1]


def start_kernel(raw_ref, nrm_ref, stream_out, hid_out, *, scale):
    stream = raw_ref[...].astype(F32).T * scale
    stream_out[...] = stream
    hid_out[...] = norm_apply(stream, nrm_ref[0:1, :], nrm_ref[1:2, :])


def start_stream(raw, nrm, after=()):
    width, rows = raw.shape
    vm = pl.BlockSpec(memory_space=pltpu.VMEM)
    return call(
        functools.partial(start_kernel, scale=math.sqrt(width)),
        [
            jax.ShapeDtypeStruct((rows, width), F32),
            jax.ShapeDtypeStruct((rows, width), BF),
        ],
        [vm] * 2,
        [vm] * 2,
        (raw, nrm),
        after,
        name="start_stream",
    )


def finish_kernel(
    dy_ref, above_ref, carry_ref, gain_ref, pair_out, spread_out, piece_scr, own_sem, dp_send, dp_recv, send_sems, recv_sems, *, fly
):
    back, pair = norm_back(dy_ref[...], above_ref[...], gain_ref[...])
    pair_out[...] = pair
    piece_scr[...] = (carry_ref[...] + back).T.reshape(piece_scr.shape).astype(BF)
    count = piece_scr.shape[0]
    mine = lax.axis_index("dp")
    here = spread_out.at[0, mine]
    copies = [pltpu.make_async_copy(piece_scr.at[mine], here, own_sem)]
    for step in range(count - 1):
        peer = (mine + step + 1) % count
        copies.append(
            pltpu.make_async_remote_copy(
                src_ref=piece_scr.at[peer],
                dst_ref=here,
                send_sem=dp_send.at[step],
                recv_sem=dp_recv.at[step],
                device_id={"dp": peer},
                device_id_type=MESH,
            )
        )
    for copy in copies:
        copy.start()
    fly()
    for copy in copies:
        copy.wait()

    def hop(at, source, target, axis, bit):
        return remote(spread_out.at[source], spread_out.at[target], send_sems.at[at], recv_sems.at[at], axis, bit)

    far, near = hop(0, 0, 2, *HEADS[1]), hop(1, 0, 1, *HEADS[0])
    far.start()
    near.start()
    far.wait()
    cross = hop(2, 2, 3, *HEADS[0])
    cross.start()
    near.wait()
    cross.wait()


def finish_stream(dy, above, carry, gain, after=(), flows=(), ident=0):
    rows, width = above.shape
    dp, pairs = lax.axis_size("dp"), lax.axis_size("head")
    features = width // dp
    return call(
        finish_kernel,
        [shape((2, width), F32), shape((pairs, dp, features, rows), BF)],
        [VM] * 4,
        [VM, FAR],
        (dy, above, carry, gain),
        after,
        flows,
        ident,
        HEADS,
        ("dp",),
        hold=0,
        scratch_shapes=[
            pltpu.VMEM((dp, features, rows), BF),
            pltpu.SemaphoreType.DMA,
            pltpu.SemaphoreType.DMA((dp - 1,)),
            pltpu.SemaphoreType.DMA((dp - 1,)),
            pltpu.SemaphoreType.DMA((3,)),
            pltpu.SemaphoreType.DMA((3,)),
        ],
        name="finish_stream",
    )


def to_lanes(column):
    return jnp.broadcast_to(column, (column.shape[0], 128)).T[0:1, :]


def to_rows(line):
    return jnp.broadcast_to(line, (128, line.shape[1])).T[:, 0:1]


SLOTS = 8
SLOT_HOPS = (("head", 1, 4), ("head", 2, 2), ("dp", 1, 1))
GREET_SLOTS = HEADS + (("dp", 1),)


def head_forward_kernel(
    final_ref, table_ref, goal_ref, count_ref, rows_out, line_out, loss_out,
    rows_scr, stat_scr, come_scr, send_sems, recv_sems, stat_send, stat_recv
):
    def hop(at, source, target, which):
        axis, bit, _ = SLOT_HOPS[which]
        return remote(rows_scr.at[source], rows_scr.at[target], send_sems.at[at], recv_sems.at[at], axis, bit)

    rows_scr[0] = final_ref[...]
    core_own, low_own = hop(0, 0, 4, 0), hop(1, 0, 1, 2)
    far = [hop(2, 0, 2, 1), hop(3, 1, 3, 1)]
    core = [hop(4, 1, 5, 0), hop(5, 2, 6, 0), hop(6, 3, 7, 0)]
    core_own.start()
    low_own.start()
    far[0].start()

    def slot(at, _):
        @pl.when(at == 1)
        def _():
            core_own.wait()
            low_own.wait()
            far[1].start()
            core[0].start()

        @pl.when(at == 3)
        def _():
            core[0].wait()

        @pl.when(at == 4)
        def _():
            far[0].wait()
            core[1].start()
            far[1].wait()
            core[2].start()

        @pl.when(at == 6)
        def _():
            core[1].wait()
            core[2].wait()

        late = at // 4
        place = (1 - late) * (at // 2 + 4 * (at % 2)) + late * (2 + at % 2 + 4 * ((at // 2) % 2))
        logits = dot_nn(rows_scr[place], table_ref[...])
        top = jnp.max(logits, 1, keepdims=True)
        sums = jnp.sum(jnp.exp(logits - top), 1, keepdims=True)
        hit = iota(logits.shape, 1).astype(F32) == to_rows(goal_ref[place])
        pick = jnp.sum(jnp.where(hit, logits, 0.0), 1, keepdims=True)
        stat_scr[place, 0:1, :] = to_lanes(top)
        stat_scr[place, 1:2, :] = to_lanes(sums)
        stat_scr[place, 2:3, :] = to_lanes(pick)
        return 0

    lax.fori_loop(0, SLOTS, slot, 0)
    for at, (axis, bit, mask) in enumerate(SLOT_HOPS):
        meet = remote(stat_scr, come_scr.at[at], stat_send.at[at], stat_recv.at[at], axis, bit)
        meet.start()
        meet.wait()
        for place in range(SLOTS):
            mine, theirs = stat_scr[place], come_scr[at, place ^ mask]
            peak = jnp.maximum(mine[0:1], theirs[0:1])
            stat_scr[place, 1:2, :] = mine[1:2] * jnp.exp(mine[0:1] - peak) + theirs[1:2] * jnp.exp(
                theirs[0:1] - peak
            )
            stat_scr[place, 0:1, :] = peak
            stat_scr[place, 2:3, :] = mine[2:3] + theirs[2:3]
    loss = jnp.zeros((1, 1), F32)
    for place in range(SLOTS):
        mine = stat_scr[place]
        lse = mine[0:1] + jnp.log(mine[1:2])
        line_out[place, 0:1, :] = lse
        line_out[place, 1:2, :] = count_ref[place]
        loss += jnp.sum((lse - mine[2:3]) * count_ref[place], 1, keepdims=True)
    loss_out[...] = loss
    rows_out[...] = rows_scr[...]


def head_forward(final, table, goals, counted, ident):
    rows, width = final.shape
    hops = len(SLOT_HOPS)
    return call(
        head_forward_kernel,
        [shape((SLOTS, rows, width), BF), shape((SLOTS, 2, rows), F32), shape((1, 1), F32)],
        [VM] * 4,
        [VM] * 3,
        (final, table, goals, counted),
        ident=ident,
        greet=GREET_SLOTS,
        scratch_shapes=[
            pltpu.VMEM((SLOTS, rows, width), BF),
            pltpu.VMEM((SLOTS, 8, rows), F32),
            pltpu.VMEM((hops, SLOTS, 8, rows), F32),
            pltpu.SemaphoreType.DMA((7,)),
            pltpu.SemaphoreType.DMA((7,)),
            pltpu.SemaphoreType.DMA((hops,)),
            pltpu.SemaphoreType.DMA((hops,)),
        ],
        **settings(18_000_000_000, 6_000_000, "head_forward"),
    )


def head_backward_kernel(
    rows_ref, table_ref, goal_ref, line_ref, dy_out, gtab_out,
    acc_scr, grad_scr, send_scr, core_scr, far_scr, low_scr, keep_scr,
    core_send, core_recv, far_send, far_recv, low_send, low_recv
):
    rows = rows_ref.shape[1]

    def to_core(place):
        return remote(
            send_scr.at[place + 4], core_scr.at[place], core_send.at[place], core_recv.at[place], *HEADS[0]
        )

    def to_far(place):
        return remote(
            send_scr.at[place + 2], far_scr.at[place], far_send.at[place], far_recv.at[place], *HEADS[1]
        )

    to_low = remote(send_scr.at[1], low_scr, low_send, low_recv, "dp", 1)

    def pair(at, _):
        base = 6 - 4 * (at % 2) - 2 * (at // 2)
        for q in range(2):
            place = base + q + (at // 3) * (1 - 2 * q)
            logits = dot_nn(rows_ref[place], table_ref[...])
            hit = iota(logits.shape, 1).astype(F32) == to_rows(goal_ref[place])
            line = line_ref[place]
            chance = jnp.exp(logits - to_rows(line[0:1]))
            grad = ((chance - jnp.where(hit, 1.0, 0.0)) * to_rows(line[1:2])).astype(BF)
            grad_scr[q * rows:(q + 1) * rows, :] = grad
            part = dot_nt(grad, table_ref[...])

            @pl.when((at == 0) | (at == 2))
            def _():
                send_scr[place] = part.astype(BF)
                to_core(place - 4).start()

            @pl.when(at == 1)
            def _():
                to_core(place).wait()
                send_scr[place] = (part + core_scr[place].astype(F32)).astype(BF)
                to_far(place - 2).start()

            @pl.when(at == 3)
            def _():
                to_core(place).wait()
                to_far(place).wait()
                whole = part + core_scr[place].astype(F32) + far_scr[place].astype(F32)
                if q == 0:
                    send_scr[1] = whole.astype(BF)
                    to_low.start()
                else:
                    keep_scr[...] = whole

        both = [rows_ref[base + q + (at // 3) * (1 - 2 * q)] for q in range(2)]
        part = dot_tn(jnp.concatenate(both, 0), grad_scr[...])

        @pl.when(at == 0)
        def _():
            acc_scr[...] = part

        @pl.when(at > 0)
        def _():
            acc_scr[...] += part

        return 0

    lax.fori_loop(0, SLOTS // 2, pair, 0)
    gtab_out[...] = acc_scr[...].astype(BF)
    to_low.wait()
    dy_out[...] = keep_scr[...] + low_scr[...].astype(F32)


def head_backward(rows_all, table, goals, lines, ident):
    _, rows, width = rows_all.shape
    vocab = table.shape[1]
    return call(
        head_backward_kernel,
        [shape((rows, width), F32), shape((width, vocab), BF)],
        [VM] * 4,
        [VM] * 2,
        (rows_all, table, goals, lines),
        ident=ident,
        greet=GREET_SLOTS,
        scratch_shapes=[
            pltpu.VMEM((width, vocab), F32),
            pltpu.VMEM((2 * rows, vocab), BF),
            pltpu.VMEM((SLOTS, rows, width), BF),
            pltpu.VMEM((4, rows, width), BF),
            pltpu.VMEM((2, rows, width), BF),
            pltpu.VMEM((rows, width), BF),
            pltpu.VMEM((rows, width), F32),
            pltpu.SemaphoreType.DMA((4,)),
            pltpu.SemaphoreType.DMA((4,)),
            pltpu.SemaphoreType.DMA((2,)),
            pltpu.SemaphoreType.DMA((2,)),
            pltpu.SemaphoreType.DMA,
            pltpu.SemaphoreType.DMA,
        ],
        **settings(36_000_000_000, 14_000_000, "head_backward"),
    )


def swap(value, axis, bit):
    return lax.ppermute(value, axis, [(at, at ^ bit) for at in range(lax.axis_size(axis))])


def has_bit(axis, bit):
    return (lax.axis_index(axis) & bit) != 0


def bits_of(axis):
    size = lax.axis_size(axis)
    return [1 << at for at in reversed(range(size.bit_length() - 1))]


def in_order(mine, other, axis, bit, dim):
    flag = has_bit(axis, bit)
    return jnp.concatenate([jnp.where(flag, other, mine), jnp.where(flag, mine, other)], dim)


def gather_dp(value):
    bits = bits_of("dp")
    whole = value.reshape((1,) * len(bits) + value.shape)
    for dim, bit in enumerate(bits):
        whole = in_order(whole, swap(whole, "dp", bit), "dp", bit, dim)
    return whole.reshape((-1,) + value.shape)


def split(value, axis, bit, dim):
    flag = has_bit(axis, bit).astype(jnp.int32)
    low = value.astype(BF)
    return (
        lax.dynamic_index_in_dim(low, flag, dim, False),
        lax.dynamic_index_in_dim(low, 1 - flag, dim, False),
    )


def nothing_of(value):
    return value[(0,) * value.ndim].astype(F32) * 0.0


def add_up(*values):
    result = values[0].astype(F32)
    for value in values[1:]:
        result = result + (value.astype(F32) if value.ndim else value)
    return result


def sum_all(value, combine=jnp.add):
    for axis in ("head", "dp"):
        for bit in reversed(bits_of(axis)):
            value = combine(value, swap(value, axis, bit))
    return value


def pack_weights(attn_in, attn_out, ffn_up, ffn_down):
    features = attn_in.shape[0]
    low = attn_in.astype(BF)
    q, k, v = low[..., :HD], low[..., HD:2 * HD], low[..., 2 * HD:3 * HD]
    s = low[..., 3 * HD:].reshape(features, -1)
    blank = jnp.zeros((features, 128 - s.shape[1]), BF)
    out = attn_out.astype(BF)
    out = jnp.concatenate([out[1], out[0]], 0).T
    return jnp.concatenate(
        [
            q[:, 0], q[:, 1], k[:, 0], v[:, 0], v[:, 1], k[:, 1], s, blank,
            out, ffn_up.astype(BF), ffn_down.astype(BF).T,
        ],
        1,
    )


def depth_of(features):
    return max(64, features)


class Gather:
    def __init__(self, packed):
        bits = bits_of("dp")
        value = packed.reshape((1,) * len(bits) + packed.shape)
        for dim, bit in enumerate(bits[:-1]):
            value = in_order(value, swap(value, "dp", bit), "dp", bit, dim)
        self.value = value

    def finish(self):
        bits = bits_of("dp")
        across = swap(self.value, "head", 2)
        got = []
        for value in (self.value, across):
            whole = in_order(value, swap(value, "dp", bits[-1]), "dp", bits[-1], len(bits) - 1)
            got += [whole, swap(whole, "head", 1)]
        features, columns = self.value.shape[-2:]
        return [one.reshape(-1, depth_of(features), columns) for one in got]


def gather_rest(packed):
    dp, head = lax.axis_size("dp"), lax.axis_size("head")
    features, columns = packed.shape
    whole = lax.all_gather(packed, ("dp", "head"), axis=0, tiled=True)
    fold = depth_of(features) // features
    if fold > 1:
        whole = whole.reshape(dp // fold, fold, head, features, columns).transpose(0, 2, 1, 3, 4)
    return whole.reshape(dp // fold, head, fold * features, columns)


def adamw(weight, gradient, moment_one, moment_two, factor, step_rate):
    gradient = gradient * factor
    moment_one = BETA_ONE * moment_one + (1.0 - BETA_ONE) * gradient
    moment_two = BETA_TWO * moment_two + (1.0 - BETA_TWO) * gradient * gradient
    adam_step = (
        moment_one
        / (1.0 - BETA_ONE**STEP)
        / (jnp.sqrt(moment_two / (1.0 - BETA_TWO**STEP)) + ADAM_FLOOR)
    )
    return (weight - step_rate * (adam_step + WEIGHT_DECAY * weight), moment_one, moment_two)


def body(
    tokens, targets, lengths,
    table, table_first, table_second,
    attn_in, attn_in_first, attn_in_second,
    attn_out, attn_out_first, attn_out_second,
    ffn_up, ffn_up_first, ffn_up_second,
    ffn_down, ffn_down_first, ffn_down_second,
    norms, norms_first, norms_second,
):
    dp, head = lax.axis_size("dp"), lax.axis_size("head")
    my_dp, my_head = lax.axis_index("dp"), lax.axis_index("head")
    seq_count, length = tokens.shape
    features, vocab = table.shape
    width = features * dp
    layers = attn_in.shape[0]
    rows = length // head
    total_tokens = dp * length
    odd = my_dp & 1
    outer = [[at for at in range(dp) if at % 2 == way] for way in range(2)]

    lines = jnp.concatenate([tokens, targets, jnp.broadcast_to(lengths[:, None], (seq_count, 128))], 1)
    lines = gather_dp(lines.reshape(-1))
    all_tokens = lines[:, :length].reshape(1, total_tokens)
    positions = jnp.arange(length, dtype=jnp.int32)
    counted = (positions[None, :] < lines[:, 2 * length:2 * length + 1]).astype(F32)
    nrm = norms
    for bit in (1, 2):
        nrm = in_order(nrm, swap(nrm, "head", bit), "head", bit, 2)

    low_table = table.astype(BF)
    packs = [
        pack_weights(attn_in[at], attn_out[at], ffn_up[at], ffn_down[at]) for at in range(layers)
    ]
    leader = Gather(packs[0][:, :ATTN])
    idents = iter(range(1, 64))

    half = vocab // 2
    other = swap(lax.dynamic_slice_in_dim(low_table, (1 - odd) * half, half, 1), "dp", 1)
    mine = lax.dynamic_slice_in_dim(low_table, odd * half, half, 1)
    head_table = in_order(mine, other, "dp", 1, 0)

    base = (my_head * vocab).astype(jnp.int32).reshape(1)
    found, token = embed_lookup(base, all_tokens, low_table, [leader.value])
    rest_weights = gather_rest(jnp.concatenate([packs[0][:, ATTN:]] + packs[1:], 1))
    found = found.reshape(features, dp, head, rows)
    for bit in (1, 2):
        flag = (my_head & bit) // bit
        found = found.reshape(features, dp, -1, 2, rows) if bit == 1 else found.reshape(features, dp, 2, rows)
        dim = 3 if bit == 1 else 2
        other = swap(lax.dynamic_index_in_dim(found, 1 - flag, dim, False), "head", bit)
        found = lax.dynamic_index_in_dim(found, flag, dim, False) + other
    found = lax.all_to_all(found, "dp", split_axis=1, concat_axis=0, tiled=True)
    stream, hidden, token = start_stream(found.reshape(width, rows), nrm[0])
    head_table = lax.all_gather(
        head_table + token.astype(BF), "dp", axis=0, tiled=True, axis_index_groups=outer
    )
    sources = [((leader.finish(), 0), ([rest_weights], 0))]
    for at in range(1, layers):
        start = FEED + (at - 1) * (ATTN + FEED)
        sources.append((([rest_weights], start), ([rest_weights], start + ATTN)))

    kept = []
    for at in range(layers):
        (for_attend, attend_low), (for_feed, feed_low) = sources[at]
        middle, hidden_two, *saved, token = attend_forward(
            attend_low, hidden, stream, for_attend, nrm[2 * at + 1], ident=next(idents)
        )
        result, hidden, upward, active_rows, _ = feed_forward(
            feed_low, middle, hidden_two, for_feed, nrm[2 * at + 2]
        )
        kept.append((stream, (middle, hidden_two, upward, active_rows), saved))
        stream = result

    def line_of(values):
        values = values.reshape(dp, head, rows)
        order = [(my_dp ^ y, my_head ^ (x * 2 + c)) for c in range(2) for x in range(2) for y in range(2)]
        picked = [
            lax.dynamic_slice(values, (d, h, 0), (1, 1, rows)).reshape(rows) for d, h in order
        ]
        return jnp.concatenate(picked)

    goals = line_of(lines[:, length:2 * length]) - (my_head * vocab + odd * half).astype(jnp.int32)
    goals = goals.astype(F32).reshape(SLOTS, 1, rows)
    rows_all, stat_lines, loss_here, token = head_forward(
        hidden, head_table, goals, line_of(counted).reshape(SLOTS, 1, rows), next(idents)
    )
    loss_here = loss_here / (2 * head)
    count_total = jnp.sum(counted)
    dy, grad_half, token = head_backward(rows_all, head_table, goals, stat_lines, next(idents))
    grad_half = lax.psum_scatter(
        grad_half, "dp", scatter_dimension=0, tiled=True, axis_index_groups=outer
    ).reshape(2, features, half)

    carry = jnp.zeros((rows, width), F32)
    above = stream
    pair_grads = [None] * (2 * layers + 1)
    bits = bits_of("dp")

    def shaped(value):
        return value.reshape((2,) * len(bits) + (features, value.shape[-1]))

    def attn_steps(mine, theirs):
        across = yield theirs, "head", 2
        here, there = split(shaped(add_up(mine, across)), "dp", bits[-1], len(bits) - 1)
        return here, (yield there, "dp", bits[-1])

    def feed_steps(here, there):
        value = add_up(here, (yield there, "dp", bits[-1]))
        parts = value[0], (yield value[1].astype(BF), "head", 2)
        return tuple(part.reshape((2,) * (len(bits) - 1) + part.shape[-2:]) for part in parts)

    def last_steps(attn, feed):
        value = jnp.concatenate([add_up(*attn.parts), add_up(*feed.parts)], -1)
        for dim, bit in reversed(list(enumerate(bits[:-1]))):
            here, there = split(value, "dp", bit, dim)
            parts = here, (yield there, "dp", bit)
            value = add_up(*parts)
        return parts

    attns, feeds, lasts = [None] * layers, [None] * layers, [None] * layers

    def active(*candidates):
        return [flow for flow in candidates if flow is not None and flow.ask is not None]

    for at in reversed(range(layers)):
        stream_in, for_feed, for_attend = kept[at]
        (attend_sources, attend_low), (feed_sources, feed_low) = sources[at]
        above_attn, above_feed = (attns + [None])[at + 1], (feeds + [None])[at + 1]
        top_attn, top_feed = (attns + [None] * 2)[at + 2], (feeds + [None] * 2)[at + 2]
        here, there, carry, pair_above, pair_two, token = feed_backward(
            feed_low, dy, above, carry, nrm[2 * at + 2, 0:1], feed_sources, nrm[2 * at + 1, 0:1], for_feed,
            features, [grad_half] if at == 0 else [], active(top_attn, above_attn if at == 0 else None), next(idents),
        )
        feeds[at] = Flow(feed_steps(here, there))
        if at + 2 < layers:
            lasts[at + 2] = Flow(last_steps(top_attn, top_feed))
        dy, *attn_sums, token = attend_backward(
            attend_low, carry, attend_sources, for_attend, [],
            active(feeds[at], above_attn, above_feed, *lasts), next(idents),
        )
        attns[at] = Flow(attn_steps(*attn_sums))
        pair_grads[2 * at + 2] = pair_above
        pair_grads[2 * at + 1] = pair_two
        above = stream_in
    def once(value, axis, bit):
        return (yield value, axis, bit)

    grad_half = Flow(once(lax.dynamic_index_in_dim(grad_half, 1 - odd, 0, False), "dp", 1)), (
        lax.dynamic_index_in_dim(grad_half, odd, 0, False)
    )
    lasts[1] = Flow(last_steps(attns[1], feeds[1]))
    pair_grads[0], spread, token = finish_stream(
        dy, above, carry, nrm[0, 0:1], [], active(attns[0], grad_half[0], *lasts), next(idents)
    )

    head_grad = in_order(grad_half[1], grad_half[0].value, "dp", 1, 1)
    spread = spread.reshape(head * dp, features, rows)
    by_rows = all_tokens.reshape(dp, head, rows)
    order = [lax.dynamic_index_in_dim(by_rows, my_head ^ p, 1, False) for p in range(head)]
    grad_table, squares, grad_norms, token = embed_back(
        base, jnp.stack(order).reshape(1, total_tokens), spread, head_grad,
        pair_grads, [],
        active(attns[0], feeds[0], *lasts), next(idents),
    )
    sort_width = attn_in.shape[3] - 3 * HD
    thirds = [flow.finish() for flow in lasts[2:]]
    while lasts[1].ask is not None:
        lasts[1].give(swap(*lasts[1].ask))
    lower, other, totals, token = last_sums(
        attns[0].parts, feeds[0].parts, lasts[1].parts, thirds, squares, grad_norms, loss_here.reshape(1, 1),
        tuple(reversed(bits[:-1])), next(idents),
    )
    grad_norms = lax.dynamic_slice_in_dim(
        grad_norms, my_head * norms.shape[2], norms.shape[2], 2
    )
    results = update(
        totals, [lower, other] + thirds, grad_table, grad_norms, sort_width,
        [
            (table, table_first, table_second),
            (attn_in, attn_in_first, attn_in_second),
            (attn_out, attn_out_first, attn_out_second),
            (ffn_up, ffn_up_first, ffn_up_second),
            [one.transpose(0, 2, 1) for one in (ffn_down, ffn_down_first, ffn_down_second)],
            (norms, norms_first, norms_second),
        ],
    )
    results = list(results)
    results[16:20] = [one.transpose(0, 2, 1) for one in results[16:20]]
    return (jnp.stack([totals[0, 1], count_total]), jnp.sqrt(totals[0, 0]), *results)


def solution(mesh):
    ints = [P("dp", None), P("dp", None), P("dp")]
    by_table = P("dp", "head")
    by_in = P(None, "dp", "head", None)
    by_out = P(None, "head", None, "dp")
    by_up = P(None, "dp", "head")
    by_down = P(None, "head", "dp")
    by_norm = P(None, None, "head")
    in_specs, out_specs = list(ints), [P(), P()]
    for spec in (by_table, by_in, by_out, by_up, by_down):
        in_specs += [spec] * 3
        out_specs += [spec] * 4
    in_specs += [by_norm] * 3
    out_specs += [by_norm] * 3
    return jax.shard_map(
        body, mesh=mesh, in_specs=tuple(in_specs), out_specs=tuple(out_specs), check_vma=False
    )
```

```python
import functools
import math

import jax
import jax.numpy as jnp
from jax import lax
from jax.experimental import pallas as pl
from jax.experimental.pallas import tpu as pltpu
from jax.sharding import PartitionSpec as P

HD = 64
BLOCK = 32
SINK = 8
STEP = 10
EPSILON = 1e-05
NEGATIVE = -1000000000.0
TEMPER = 0.75
BETA_ONE = 0.9
BETA_TWO = 0.999
ADAM_FLOOR = 1e-08
WEIGHT_DECAY = 0.01
RATE_MATRIX = 0.1
RATE_NORM = 0.5
CLIP_LIMIT = 1.0

BF = jnp.bfloat16
F32 = jnp.float32
GROUP = 4
GELU_C = math.sqrt(2.0 / math.pi)
GELU_A = 0.044715

C_Q = (0, 128)
C_KVS = (128, 512)
C_OUT = (512, 640)
ATTN = 640
C_UP = (0, 512)
C_DOWN = (512, 1024)
FEED = 1024
VMEM_LIMIT = 56 * 1024 * 1024


def dot_nn(a, b):
    return lax.dot_general(a, b, (((1,), (0,)), ((), ())), preferred_element_type=F32)


def dot_nt(a, b):
    return lax.dot_general(a, b, (((1,), (1,)), ((), ())), preferred_element_type=F32)


def dot_tn(a, b):
    return lax.dot_general(a, b, (((0,), (0,)), ((), ())), preferred_element_type=F32)


def iota(shape, axis):
    return lax.broadcasted_iota(jnp.int32, shape, axis)


MESH = pl.DeviceIdType.MESH


def flipped(axis, bit):
    mine = lax.axis_index(axis)
    return mine + bit - 2 * bit * ((mine // bit) % 2)


def remote(source, target, send_sem, recv_sem, axis, bit):
    return pltpu.make_async_remote_copy(
        src_ref=source,
        dst_ref=target,
        send_sem=send_sem,
        recv_sem=recv_sem,
        device_id={axis: flipped(axis, bit)},
        device_id_type=MESH,
    )


HEADS = (("head", 1), ("head", 2))


def call(
    kernel, outs, in_specs, out_specs, operands, after=(), flows=(), ident=0, greet=(), greet_all=(), hold=None, **options
):
    used, spare, token, riders = len(operands), len(after), len(outs), len(flows)
    asks = [flow.ask for flow in flows]
    pairs = sorted({ask[1:] for ask in asks} | set(greet))
    pairs = [pair for pair in pairs if pair[0] not in greet_all]
    grid = options.get("grid")
    scratch = list(options.pop("scratch_shapes", []))
    far = pl.BlockSpec(memory_space=pl.ANY)

    def run(*refs):
        ins, rest = refs[:used], refs[used + spare:]
        sends, rest = rest[:riders], rest[riders:]
        results, token_ref, rest = rest[:token], rest[token], rest[token + 1:]
        lands, rest = rest[:riders], rest[riders:]
        if riders:
            rest, (send_sems, recv_sems) = rest[:-2], rest[-2:]

        def copies():
            if not riders:
                return []
            return [
                remote(sends[at], lands[at], send_sems.at[at], recv_sems.at[at], axis, bit)
                for at, (_, axis, bit) in enumerate(asks)
            ]

        def launch():
            barrier = pltpu.get_barrier_semaphore()
            for axis, bit in pairs:
                pl.semaphore_signal(
                    barrier, inc=1, device_id={axis: flipped(axis, bit)}, device_id_type=MESH
                )
            others = 0
            for axis in greet_all:
                count = lax.axis_size(axis)
                for step in range(1, count):
                    peer = (lax.axis_index(axis) + step) % count
                    pl.semaphore_signal(barrier, inc=1, device_id={axis: peer}, device_id_type=MESH)
                others += count - 1
            pl.semaphore_wait(barrier, len(pairs) + others)
            if hold is None:
                fly()

        def fly():
            for copy in copies():
                copy.start()

        def settle():
            for copy in copies():
                copy.wait()

        if riders or greet or greet_all:
            pl.when(pl.program_id(0) == 0)(launch) if grid else launch()
        token_ref[...] = jnp.zeros((1, 128), F32)
        if hold is not None and grid:
            if riders:
                pl.when(pl.program_id(0) == hold)(fly)
            kernel(*ins, *results, *rest)
        elif hold is not None:
            kernel(*ins, *results, *rest, fly=fly)
        else:
            kernel(*ins, *results, *rest)
        if riders:
            pl.when(pl.program_id(0) == grid[0] - 1)(settle) if grid else settle()

    if riders or greet or greet_all:
        options["compiler_params"] = pltpu.CompilerParams(
            vmem_limit_bytes=VMEM_LIMIT, collective_id=ident, has_side_effects=True
        )
    if riders:
        scratch += [pltpu.SemaphoreType.DMA((riders,))] * 2
    token_spec = (
        pl.BlockSpec((1, 128), lambda i: (0, 0)) if grid else pl.BlockSpec(memory_space=pltpu.VMEM)
    )
    got = pl.pallas_call(
        run,
        out_shape=list(outs)
        + [jax.ShapeDtypeStruct((1, 128), F32)]
        + [jax.ShapeDtypeStruct(ask[0].shape, ask[0].dtype) for ask in asks],
        in_specs=list(in_specs) + [far] * (spare + riders),
        out_specs=list(out_specs) + [token_spec] + [far] * riders,
        scratch_shapes=scratch,
        **options,
    )(*operands, *after, *[ask[0] for ask in asks])
    for flow, value in zip(flows, got[token + 1:]):
        flow.give(value)
    return (*got[:token], got[token][0, 0])


class Flow:
    def __init__(self, steps):
        self.steps, self.parts = steps, None
        self.give(None)

    @property
    def value(self):
        return self.parts

    def give(self, got):
        try:
            self.ask = self.steps.send(got)
        except StopIteration as stop:
            self.ask, self.parts = None, stop.value

    def finish(self):
        while self.ask is not None:
            self.give(swap(*self.ask))
        return add_up(*self.parts) if isinstance(self.parts, tuple) else self.parts


def norm_stats(stream):
    average = jnp.mean(stream, -1, keepdims=True)
    variance = jnp.mean(stream * stream, -1, keepdims=True) - average * average
    inv_std = lax.rsqrt(variance + EPSILON)
    return (stream - average) * inv_std, inv_std


def norm_apply(stream, gain, bias):
    normed, _ = norm_stats(stream)
    return (normed * gain + bias).astype(BF)


def norm_back(upstream, stream, gain):
    normed, inv_std = norm_stats(stream)
    scaled = upstream * gain
    back = inv_std * (
        scaled
        - jnp.mean(scaled, -1, keepdims=True)
        - normed * jnp.mean(scaled * normed, -1, keepdims=True)
    )
    pair = jnp.concatenate(
        [jnp.sum(upstream * normed, 0, keepdims=True), jnp.sum(upstream, 0, keepdims=True)], 0
    )
    return back, pair


def allowed_mask(shape):
    return iota(shape, len(shape) - 1) < iota(shape, len(shape) - 2)


def log_total(x, axis):
    top = jnp.max(x, axis, keepdims=True)
    return top + jnp.log(jnp.sum(jnp.exp(x - top), axis, keepdims=True))


def balance(scores, keep):
    allowed = allowed_mask(scores.shape)
    plan = jnp.where(allowed, scores / TEMPER, NEGATIVE)
    for _ in range(SINK):
        for axis in (-2, -1):
            plan = jnp.where(allowed, plan - log_total(plan, axis), NEGATIVE)
            if keep is not None:
                keep.append(plan)
    return jnp.where(allowed, jnp.exp(plan), 0.0)


def balance_back(scores, upstream):
    allowed = allowed_mask(scores.shape)
    plans = []
    perm = balance(scores, plans)
    grad = jnp.where(allowed, upstream * perm, 0.0)
    for step in reversed(range(2 * SINK)):
        axis = (-2, -1)[step % 2]
        share = jnp.exp(plans[step])
        grad = jnp.where(allowed, grad - share * jnp.sum(grad, axis, keepdims=True), 0.0)
    return grad / TEMPER


def kron_rows(perm_rows, length):
    own, blocks = perm_rows.shape
    rows = own * BLOCK
    tall = jnp.broadcast_to(perm_rows[:, None, :], (own, BLOCK, blocks)).reshape(rows, blocks)
    spread = (iota((blocks, length), 1) // BLOCK == iota((blocks, length), 0)).astype(BF)
    wide = dot_nn(tall.astype(BF), spread)
    same = (iota((rows, length), 0) & (BLOCK - 1)) == (iota((rows, length), 1) & (BLOCK - 1))
    return jnp.where(same, wide, 0.0).astype(BF)


def group_mask(first_block, rows):
    shape = (rows, 2 * rows)
    row, slot = iota(shape, 0), iota(shape, 1)
    row_block = row // BLOCK
    in_sorted = slot < rows
    place = jnp.where(in_sorted, slot, slot - rows)
    same = (place // BLOCK) == row_block
    sorted_ok = in_sorted & (row_block + first_block >= 1)
    own_ok = (slot >= rows) & (place <= row)
    return same & (sorted_ok | own_ok)


def await_weights(sources, low, w_ref, sems, j):
    source = sources[0].at[:, 0, :, low:low + w_ref.shape[3]]
    pltpu.make_async_copy(source, w_ref.at[j], sems.at[j]).wait()


def turned(p):
    mine = lax.axis_index("head")
    low, high = mine % 2, (mine // 2) % 2
    rest = mine - low - 2 * high
    return rest + (1 - low if p & 1 else low) + 2 * (1 - high if p & 2 else high)


def load_weights(sources, low, w_ref, sems, order=(0, 1, 2, 3)):
    copies = []
    for p in order:
        if len(sources) > 1:
            source = sources[p]
        else:
            source = sources[0].at[:, turned(p), :, low:low + w_ref.shape[3]]
        copies.append(pltpu.make_async_copy(source, w_ref.at[p], sems.at[p]))
        copies[-1].start()
    return copies


def attend_forward_kernel(low, count, hidden_ref, stream_ref, nrm_ref, *refs):
    sources = refs[:count]
    (
        mid_out, hid2_out, hid_ref, kv_out, q_out, skv_out, attw_out, mixed_out, permo_out, sort_out,
        w_ref, perm_scr, acc_scr, piece_scr, sems, send_sems, recv_sems,
    ) = refs[count:]
    length, width = hid_ref.shape
    rows = stream_ref.shape[0]
    pairs = w_ref.shape[0]
    own_blocks = rows // BLOCK
    blocks = length // BLOCK
    my = lax.axis_index("head")
    own = pl.multiple_of(my * rows, rows)
    own_block = pl.multiple_of(my * own_blocks, own_blocks)
    lower = iota((1, 128), 1) < HD
    copies = load_weights(sources, low, w_ref, sems)

    def hop(at, source, target, which):
        return remote(
            piece_scr.at[source], piece_scr.at[target], send_sems.at[at], recv_sems.at[at], *HEADS[which]
        )

    far, near, cross = hop(0, 0, 2, 1), hop(1, 0, 1, 0), hop(2, 2, 3, 0)
    piece_scr[0] = hidden_ref[...]
    far.start()
    near.start()
    for copy in copies:
        copy.wait()

    def project(p):
        tile = turned(p)
        at = pl.ds(pl.multiple_of(tile * rows, rows), rows)
        blocks_at = pl.ds(pl.multiple_of(tile * own_blocks, own_blocks), own_blocks)
        hid_ref[at, :] = piece_scr[p]

        def columns(j, _):
            w = w_ref[j, :, :, C_KVS[0]:C_KVS[1]].reshape(width, C_KVS[1] - C_KVS[0])
            got = dot_nn(piece_scr[p], w)
            kv_out[j, at, :] = got[:, :256].astype(BF)
            sort_out[j, blocks_at, :] = jnp.sum(got[:, 256:].reshape(own_blocks, BLOCK, 128), 1) / math.sqrt(BLOCK)
            return 0

        lax.fori_loop(0, pairs, columns, 0)

    project(0)
    near.wait()
    project(1)
    far.wait()
    cross.start()
    project(2)
    cross.wait()
    project(3)

    scores = jnp.stack(
        [sort_out[h // 2][:, (h % 2) * BLOCK:(h % 2) * BLOCK + blocks] for h in range(2 * pairs)]
    )
    perm_scr[...] = balance(scores, None)
    permo_out[...] = perm_scr[:, pl.ds(own_block, own_blocks), :]
    acc_scr[...] = stream_ref[...]
    take = GROUP * BLOCK

    def attend(j, _):
        wq = w_ref[j, :, :, C_Q[0]:C_Q[1]].reshape(width, 128)
        q = dot_nn(hid_ref[pl.ds(own, rows), :], wq).astype(BF)
        q_out[j] = q
        mixes = []
        for h in range(2):
            kron = kron_rows(permo_out[2 * j + h], length)
            skv = dot_nn(kron, kv_out[j, :, h * 128:(h + 1) * 128]).astype(BF)
            skv_out[j, h] = skv
            q_mine = jnp.where(lower if h == 0 else ~lower, q, jnp.zeros_like(q))
            kv_own = kv_out[j, pl.ds(own, rows), h * 128:(h + 1) * 128]
            pieces = []
            for g in range(rows // take):
                cut = slice(g * take, (g + 1) * take)
                kv_set = jnp.concatenate([skv[cut], kv_own[cut]], 0)
                raw = dot_nt(q_mine[cut], kv_set) * (1.0 / math.sqrt(HD))
                raw = jnp.where(group_mask(own_block + g * GROUP, take), raw, NEGATIVE)
                grown = jnp.exp(raw - jnp.max(raw, -1, keepdims=True))
                share = grown / jnp.sum(grown, -1, keepdims=True)
                attw_out[j, h, cut, :] = share
                pieces.append(dot_nn(share.astype(BF), kv_set))
            mixes.append(jnp.concatenate(pieces, 0))
        mixed = jnp.where(lower, mixes[1], mixes[0]).astype(BF)
        mixed_out[j] = mixed
        w_o = w_ref[j, :, :, C_OUT[0]:C_OUT[1]].reshape(width, 128)
        acc_scr[...] += dot_nt(mixed, w_o)
        return 0

    lax.fori_loop(0, pairs, attend, 0)

    middle = acc_scr[...]
    mid_out[...] = middle
    hid2_out[...] = norm_apply(middle, nrm_ref[0:1, :], nrm_ref[1:2, :])


def feed_forward_kernel(low, count, mid_ref, hid2_ref, nrm_ref, *refs):
    sources = refs[:count]
    stream_out, hnext_out, upw_out, act_out, w_ref, acc_scr, sems = refs[count:]
    width = mid_ref.shape[1]
    pairs = w_ref.shape[0]
    load_weights(sources, low, w_ref, sems)
    acc_scr[...] = mid_ref[...]
    def feed(j, _):
        await_weights(sources, low, w_ref, sems, j)
        w_up = w_ref[j, :, :, C_UP[0]:C_UP[1]].reshape(width, 512)
        upward = dot_nn(hid2_ref[...], w_up)
        upw_out[j] = upward
        bent = jnp.tanh(GELU_C * (upward + GELU_A * upward * upward * upward))
        act = (0.5 * upward * (1.0 + bent)).astype(BF)
        act_out[j] = act
        w_dn = w_ref[j, :, :, C_DOWN[0]:C_DOWN[1]].reshape(width, 512)
        acc_scr[...] += dot_nt(act, w_dn)
        return 0

    lax.fori_loop(0, pairs, feed, 0)
    result = acc_scr[...]
    stream_out[...] = result
    hnext_out[...] = norm_apply(result, nrm_ref[0:1, :], nrm_ref[1:2, :])


VM = pl.BlockSpec(memory_space=pltpu.VMEM)
SM = pl.BlockSpec(memory_space=pltpu.SMEM)
FAR = pl.BlockSpec(memory_space=pl.ANY)
shape = jax.ShapeDtypeStruct


def settings(flops, traffic, name):
    return dict(
        compiler_params=pltpu.CompilerParams(vmem_limit_bytes=VMEM_LIMIT),
        cost_estimate=pl.CostEstimate(flops=flops, bytes_accessed=traffic, transcendentals=0),
        name=name,
    )


def weight_slots(sources, pairs, columns):
    parts, depth = (sources[0].shape[0], sources[0].shape[-2])
    return pltpu.VMEM((pairs, parts, depth, columns), BF)


def attend_forward(low, hidden, stream, sources, nrm, after=(), flows=(), ident=0):
    rows, width = stream.shape
    pairs = lax.axis_size("head")
    length = rows * pairs
    own_blocks, blocks = rows // BLOCK, length // BLOCK
    outs = [
        shape((rows, width), F32),
        shape((rows, width), BF),
        shape((length, width), BF),
        shape((pairs, length, 256), BF),
        shape((pairs, rows, 128), BF),
        shape((pairs, 2, rows, 128), BF),
        shape((pairs, 2, rows, 2 * GROUP * BLOCK), F32),
        shape((pairs, rows, 128), BF),
        shape((2 * pairs, own_blocks, blocks), F32),
        shape((pairs, blocks, 128), F32),
    ]
    return call(
        functools.partial(attend_forward_kernel, low, len(sources)),
        outs,
        [VM] * 3 + [FAR] * len(sources),
        [VM] * len(outs),
        (hidden, stream, nrm, *sources),
        after,
        flows,
        ident,
        HEADS,
        scratch_shapes=[
            weight_slots(sources, pairs, ATTN),
            pltpu.VMEM((2 * pairs, blocks, blocks), F32),
            pltpu.VMEM((rows, width), F32),
            pltpu.VMEM((pairs, rows, width), BF),
            pltpu.SemaphoreType.DMA((pairs,)),
            pltpu.SemaphoreType.DMA((3,)),
            pltpu.SemaphoreType.DMA((3,)),
        ],
        **settings(18_000_000_000, 10_000_000, "attend_forward"),
    )


def feed_forward(low, middle, hidden, sources, nrm, after=(), flows=(), ident=0):
    rows, width = middle.shape
    pairs = lax.axis_size("head")
    outs = [
        shape((rows, width), F32),
        shape((rows, width), BF),
        shape((pairs, rows, 512), F32),
        shape((pairs, rows, 512), BF),
    ]
    return call(
        functools.partial(feed_forward_kernel, low, len(sources)),
        outs,
        [VM] * 3 + [FAR] * len(sources),
        [VM] * len(outs),
        (middle, hidden, nrm, *sources),
        after,
        scratch_shapes=[
            weight_slots(sources, pairs, FEED),
            pltpu.VMEM((rows, width), F32),
            pltpu.SemaphoreType.DMA((pairs,)),
        ],
        **settings(8_000_000_000, 8_000_000, "feed_forward"),
    )


def put(wgrad_scr, j, columns, value):
    parts, depth = wgrad_scr.shape[1:3]
    size = columns[1] - columns[0]
    wgrad_scr[j, :, :, columns[0]:columns[1]] = value.astype(BF).reshape(parts, depth, size)


def take_part(ref, index, features):
    depth = ref.shape[1]
    if depth == features:
        return ref[index].astype(F32)
    fold = depth // features
    whole = ref[index // fold].astype(F32).reshape(fold, features, ref.shape[2])
    return jnp.sum(jnp.where(iota(whole.shape, 0) == index % fold, whole, 0.0), 0)


def near_first(at):
    return 2 * at + 1 - 5 * (at // 2)


def feed_backward_kernel(
    low, count, dy_ref, above_ref, carry_ref, gain_above_ref, gain_two_ref,
    mid_ref, hid2_ref, upw_ref, act_ref, *refs
):
    sources = refs[:count]
    (
        here_out, there_out, carry_out, pair_above_out, pair_two_out,
        w_ref, acc_scr, low_scr, wgrad_scr, near_scr, sems, send_sems, recv_sems,
    ) = refs[count:]
    width = carry_ref.shape[1]
    pairs = w_ref.shape[0]
    load_weights(sources, low, w_ref, sems, (1, 3, 0, 2))

    back, pair = norm_back(dy_ref[...], above_ref[...], gain_above_ref[...])
    pair_above_out[...] = pair
    upstream = carry_ref[...] + back
    carry_out[...] = upstream
    low_scr[...] = upstream.astype(BF)
    acc_scr[...] = jnp.zeros_like(acc_scr)

    def to_near(at):
        return remote(
            wgrad_scr.at[near_first(at)], near_scr.at[at], send_sems.at[at], recv_sems.at[at], *HEADS[0]
        )

    def feed(at, _):
        j = near_first(at)
        await_weights(sources, low, w_ref, sems, j)
        rounded = low_scr[...]
        w_dn = w_ref[j, :, :, C_DOWN[0]:C_DOWN[1]].reshape(width, 512)
        grad_act = dot_nn(rounded, w_dn)
        x = upw_ref[j]
        squared = x * x
        bent = jnp.tanh(GELU_C * (x + GELU_A * squared * x))
        slope = 0.5 * (1.0 + bent) + 0.5 * x * (1.0 - bent * bent) * (
            GELU_C * (1.0 + 3.0 * GELU_A * squared)
        )
        grad_up = (grad_act * slope).astype(BF)
        put(wgrad_scr, j, C_DOWN, dot_tn(rounded, act_ref[j]))
        put(wgrad_scr, j, C_UP, dot_tn(hid2_ref[...], grad_up))
        w_up = w_ref[j, :, :, C_UP[0]:C_UP[1]].reshape(width, 512)
        acc_scr[...] += dot_nt(grad_up, w_up)

        @pl.when(at < pairs // 2)
        def _():
            to_near(at).start()

        return 0

    lax.fori_loop(0, pairs, feed, 0)

    back, pair = norm_back(acc_scr[...], mid_ref[...], gain_two_ref[...])
    pair_two_out[...] = pair
    carry_out[...] += back
    odd = lax.axis_index("dp") % 2
    for x in range(pairs // 2):
        to_near(x).wait()
        for at in range(here_out.shape[1]):
            for out, way in ((here_out, odd), (there_out, 1 - odd)):
                out[x, at] = (
                    take_part(wgrad_scr.at[2 * x], 2 * at + way, out.shape[2])
                    + take_part(near_scr.at[x], 2 * at + way, out.shape[2])
                ).astype(BF)


def attend_backward_kernel(
    low, count, carry_ref, hid_ref, kv_ref, q_ref, skv_ref, attw_ref, mixed_ref, permo_ref, sort_ref,
    *refs
):
    sources = refs[:count]
    (
        dy_out, mine_out, across_out,
        w_ref, ghid_scr, gkv_scr, gsrt_scr, gq_scr, dperm_scr, low_scr, wgrad_scr, near_scr,
        gsend_scr, gnear_scr, afar_scr, gfar_scr, sems, send_sems, recv_sems,
    ) = refs[count:]
    length, width = hid_ref.shape
    rows = carry_ref.shape[0]
    pairs, parts, depth = w_ref.shape[:3]
    own_blocks = rows // BLOCK
    blocks = length // BLOCK
    my = lax.axis_index("head")
    own = pl.multiple_of(my * rows, rows)
    own_block = pl.multiple_of(my * own_blocks, own_blocks)
    lower = iota((1, 128), 1) < HD
    take = GROUP * BLOCK
    copies = load_weights(sources, low, w_ref, sems)
    low_scr[...] = carry_ref[...].astype(BF)
    dperm_scr[...] = jnp.zeros_like(dperm_scr)
    for copy in copies:
        copy.wait()
    scale_key = 1.0 / math.sqrt(HD)

    def attend(j, _):
        rounded = low_scr[...]
        w_o = w_ref[j, :, :, C_OUT[0]:C_OUT[1]].reshape(width, 128)
        grad_mixed = dot_nn(rounded, w_o).astype(BF)
        put(wgrad_scr, j, C_OUT, dot_tn(rounded, mixed_ref[j]))
        q = q_ref[j]
        zero = jnp.zeros_like(q)
        queries = []
        for h in range(2):
            key_lanes = lower if h == 0 else ~lower
            kron = kron_rows(permo_ref[2 * j + h], length)
            kv_all = kv_ref[j, :, h * 128:(h + 1) * 128]
            kv_own = kv_ref[j, pl.ds(own, rows), h * 128:(h + 1) * 128]
            skv = skv_ref[j, h]
            q_mine = jnp.where(key_lanes, q, zero)
            gm_mine = jnp.where(key_lanes, zero, grad_mixed)
            scale = jnp.where(key_lanes, scale_key, 1.0)
            gq, g_sorted, g_own = [], [], []
            for g in range(rows // take):
                cut = slice(g * take, (g + 1) * take)
                kv_set = jnp.concatenate([skv[cut], kv_own[cut]], 0)
                share = attw_ref[j, h, cut, :]
                grad_share = dot_nt(gm_mine[cut], kv_set)
                grad_raw = (
                    share * (grad_share - jnp.sum(share * grad_share, -1, keepdims=True))
                ).astype(BF)
                gq.append(dot_nn(grad_raw, kv_set) * scale_key)
                grad_set = (
                    dot_tn(grad_raw, q_mine[cut]) + dot_tn(share.astype(BF), gm_mine[cut])
                ) * scale
                g_sorted.append(grad_set[:take])
                g_own.append(grad_set[take:])
            queries.append(jnp.concatenate(gq, 0))
            grad_sorted = jnp.concatenate(g_sorted, 0).astype(BF)
            crossed = dot_nt(grad_sorted, kv_all)
            same = (iota((rows, length), 0) & (BLOCK - 1)) == (iota((rows, length), 1) & (BLOCK - 1))
            crossed = jnp.where(same, crossed, 0.0).reshape(own_blocks, BLOCK, length)
            dperm_scr[2 * j + h] = jnp.sum(crossed, 1)
            ghid_scr[:, 0:128] = dot_tn(kron, grad_sorted)
            ghid_scr[pl.ds(own, rows), 0:128] += jnp.concatenate(g_own, 0)
            gkv_scr[j, :, h * 128:(h + 1) * 128] = ghid_scr[:, 0:128].astype(BF)
        gq_scr[j] = jnp.where(lower, queries[0], queries[1]).astype(BF)
        return 0

    lax.fori_loop(0, pairs, attend, 0)

    heads = 2 * pairs
    gather = (iota((length, blocks), 0) // BLOCK == iota((length, blocks), 1)).astype(F32)
    dperm = lax.dot_general(
        dperm_scr[...].reshape(heads * own_blocks, length),
        gather,
        (((1,), (0,)), ((), ())),
        precision=lax.Precision.HIGHEST,
        preferred_element_type=F32,
    ).reshape(heads, own_blocks, blocks)
    scores = jnp.stack(
        [sort_ref[h // 2][:, (h % 2) * BLOCK:(h % 2) * BLOCK + blocks] for h in range(heads)]
    )
    full = jnp.concatenate([dperm] * (blocks // own_blocks), 1)
    block_at = iota(full.shape, 1)
    full = jnp.where((block_at >= own_block) & (block_at < own_block + own_blocks), full, 0.0)
    grad_sort = balance_back(scores, full) / math.sqrt(BLOCK)
    blank = jnp.zeros((blocks, 128 - 2 * blocks), F32)
    for j in range(pairs):
        gsrt_scr[j] = jnp.concatenate([grad_sort[2 * j], grad_sort[2 * j + 1], blank], 1)

    ghid_scr[...] = jnp.zeros_like(ghid_scr)

    def inward_of(j):
        spread = jnp.broadcast_to(gsrt_scr[j][:, None, :], (blocks, BLOCK, 128)).reshape(length, 128)
        return jnp.concatenate([gkv_scr[j], spread.astype(BF)], 1)

    def inward(j, _):
        w = w_ref[j, :, :, C_KVS[0]:C_KVS[1]].reshape(width, C_KVS[1] - C_KVS[0])
        ghid_scr[...] += dot_nt(inward_of(j), w)
        wq = w_ref[j, :, :, C_Q[0]:C_Q[1]].reshape(width, 128)
        ghid_scr[pl.ds(own, rows), :] += dot_nt(gq_scr[j], wq)
        return 0

    lax.fori_loop(0, pairs, inward, 0)

    def piece(p):
        return ghid_scr[pl.ds(pl.multiple_of(turned(p) * rows, rows), rows), :]

    for p in (1, 3):
        gsend_scr[p // 2] = piece(p).astype(BF)
    near = remote(gsend_scr, gnear_scr, send_sems.at[2], recv_sems.at[2], *HEADS[0])
    near.start()

    def to_near(at):
        return remote(
            wgrad_scr.at[near_first(at)], near_scr.at[at], send_sems.at[at], recv_sems.at[at], *HEADS[0]
        )

    def weigh(at, _):
        j = near_first(at)
        put(wgrad_scr, j, C_KVS, dot_tn(hid_ref[...], inward_of(j)))
        put(wgrad_scr, j, C_Q, dot_tn(hid_ref[pl.ds(own, rows), :], gq_scr[j]))

        @pl.when(at < pairs // 2)
        def _():
            to_near(at).start()

        return 0

    lax.fori_loop(0, pairs // 2, weigh, 0)
    near.wait()
    afar_scr[...] = (piece(2) + gnear_scr[1].astype(F32)).astype(BF)
    far = remote(afar_scr, gfar_scr, send_sems.at[3], recv_sems.at[3], *HEADS[1])
    far.start()
    lax.fori_loop(pairs // 2, pairs, weigh, 0)
    for x in range(pairs // 2):
        to_near(x).wait()
        out = across_out if x else mine_out
        for at in range(parts):
            out[at] = (wgrad_scr[2 * x, at].astype(F32) + near_scr[x, at].astype(F32)).astype(BF)
    far.wait()
    dy_out[...] = piece(0) + gnear_scr[0].astype(F32) + gfar_scr[...].astype(F32)


def feed_backward(low, dy, above, carry, gain_above, sources, gain_two, kept, features, after=(), flows=(), ident=0):
    rows, width = carry.shape
    pairs = lax.axis_size("head")
    slots = weight_slots(sources, pairs, FEED)
    half = shape((pairs // 2, lax.axis_size("dp") // 2, features, FEED), BF)
    outs = [half, half, shape((rows, width), F32), shape((2, width), F32), shape((2, width), F32)]
    return call(
        functools.partial(feed_backward_kernel, low, len(sources)),
        outs,
        [VM] * (5 + len(kept)) + [FAR] * len(sources),
        [VM] * 5,
        (dy, above, carry, gain_above, gain_two, *kept, *sources),
        after,
        flows,
        ident,
        HEADS[:1],
        scratch_shapes=[
            slots,
            pltpu.VMEM((rows, width), F32),
            pltpu.VMEM((rows, width), BF),
            slots,
            pltpu.VMEM((pairs // 2,) + slots.shape[1:], BF),
            pltpu.SemaphoreType.DMA((pairs,)),
            pltpu.SemaphoreType.DMA((2,)),
            pltpu.SemaphoreType.DMA((2,)),
        ],
        **settings(12_000_000_000, 12_000_000, "feed_backward"),
    )


def attend_backward(low, carry, sources, kept, after=(), flows=(), ident=0):
    rows, width = carry.shape
    pairs = lax.axis_size("head")
    length = rows * pairs
    own_blocks, blocks = rows // BLOCK, length // BLOCK
    slots = weight_slots(sources, pairs, ATTN)
    return call(
        functools.partial(attend_backward_kernel, low, len(sources)),
        [shape((rows, width), F32)] + [shape(slots.shape[1:], BF)] * 2,
        [VM] * (1 + len(kept)) + [FAR] * len(sources),
        [VM] * 3,
        (carry, *kept, *sources),
        after,
        flows,
        ident,
        HEADS,
        scratch_shapes=[
            slots,
            pltpu.VMEM((length, width), F32),
            pltpu.VMEM((pairs, length, 256), BF),
            pltpu.VMEM((pairs, blocks, 128), F32),
            pltpu.VMEM((pairs, rows, 128), BF),
            pltpu.VMEM((2 * pairs, own_blocks, length), F32),
            pltpu.VMEM((rows, width), BF),
            slots,
            pltpu.VMEM((pairs // 2,) + slots.shape[1:], BF),
            pltpu.VMEM((2, rows, width), BF),
            pltpu.VMEM((2, rows, width), BF),
            pltpu.VMEM((rows, width), BF),
            pltpu.VMEM((rows, width), BF),
            pltpu.SemaphoreType.DMA((pairs,)),
            pltpu.SemaphoreType.DMA((4,)),
            pltpu.SemaphoreType.DMA((4,)),
        ],
        **settings(20_000_000_000, 16_000_000, "attend_backward"),
    )


def embed_kernel(base_ref, tok_ref, table_ref, out_ref, tall_ref):
    features, vocab = table_ref.shape
    count = out_ref.shape[1]
    bins = vocab // 256

    @pl.when(pl.program_id(0) == 0)
    def _():
        for at in range(bins):
            tall_ref[at * features:(at + 1) * features, :] = table_ref[:, at * 256:(at + 1) * 256]

    local = tok_ref[...] - base_ref[0]
    high, low = local >> 8, local & 255
    hot = (iota((256, count), 0) == low).astype(BF)
    found = dot_nn(tall_ref[...], hot)
    total = jnp.zeros((features, count), F32)
    for at in range(bins):
        total = jnp.where(high == at, found[at * features:(at + 1) * features, :], total)
    out_ref[...] = total.astype(BF)


def embed_lookup(base, tokens, table, after=()):
    features, vocab = table.shape
    count = tokens.shape[1]
    tile = 512
    return call(
        embed_kernel,
        [jax.ShapeDtypeStruct((features, count), BF)],
        [
            pl.BlockSpec(memory_space=pltpu.SMEM),
            pl.BlockSpec((1, tile), lambda i: (0, i)),
            pl.BlockSpec((features, vocab), lambda i: (0, 0)),
        ],
        [pl.BlockSpec((features, tile), lambda i: (0, i))],
        (base, tokens, table),
        after,
        grid=(count // tile,),
        scratch_shapes=[pltpu.VMEM((features * (vocab // 256), 256), BF)],
        compiler_params=pltpu.CompilerParams(vmem_limit_bytes=VMEM_LIMIT),
        cost_estimate=pl.CostEstimate(flops=15_000_000_000, bytes_accessed=4_000_000, transcendentals=0),
        name="embed_lookup",
    )


def stages_of_all():
    return [("head", bit) for bit in bits_of("head")] + [("dp", bit) for bit in reversed(bits_of("dp"))]


def embed_back_kernel(
    base_ref, tok_ref, grad_ref, head_ref, *refs, scale, count_pairs
):
    pair_refs = refs[:count_pairs]
    out_ref, square_out, pair_out, acc_ref, sum_scr, come_scr, send_sems, recv_sems = refs[count_pairs:]
    pieces, features, tile = grad_ref.shape
    count = pieces * tile
    bins = acc_ref.shape[0] // features
    step = pl.program_id(0)
    stages = stages_of_all()
    first_hop = pl.num_programs(0) - len(stages) - 1
    hop_step = [0] + [first_hop + at for at in range(1, len(stages) + 1)]

    def hop(at):
        return remote(sum_scr, come_scr.at[at], send_sems.at[at], recv_sems.at[at], *stages[at])

    for at in range(len(stages) + 1):

        @pl.when(step == hop_step[at])
        def _(at=at):
            if at == 0:
                for place, pair_ref in enumerate(pair_refs):
                    sum_scr[place] = pair_ref[...]
            else:
                hop(at - 1).wait()
                sum_scr[...] += come_scr[at - 1]
            if at < len(stages):
                hop(at).start()
            else:
                pair_out[...] = sum_scr[...]

    local = tok_ref[...] - base_ref[0]
    high, low = local >> 8, local & 255
    hot = (iota((256, count), 0) == low).astype(BF)
    grad = jnp.concatenate([grad_ref[at] for at in range(pieces)], 1)
    hot_high = (iota((bins, count), 0) == high).astype(BF)
    wide = jnp.concatenate([grad * hot_high[at:at + 1, :] for at in range(bins)], 0)
    found = dot_nt(wide, hot)

    @pl.when(step == 0)
    def _():
        acc_ref[...] = found

    @pl.when(step > 0)
    def _():
        acc_ref[...] += found

    @pl.when(step == pl.num_programs(0) - 1)
    def _():
        squares = jnp.zeros((features, 256), F32)
        for at in range(bins):
            cut = slice(at * 256, (at + 1) * 256)
            total = scale * acc_ref[at * features:(at + 1) * features, :] + head_ref[:, cut].astype(F32)
            out_ref[:, cut] = total
            squares += total * total
        square_out[...] = squares


def embed_back(base, tokens, grad, head_grad, pair_grads, after=(), flows=(), ident=0):
    pieces, features, tile = grad.shape
    vocab = head_grad.shape[1]
    width = pair_grads[0].shape[1]
    count_pairs = len(pair_grads)
    all_pairs = (count_pairs, 2, width)
    stages = len(stages_of_all())
    still = lambda i: (0, 0)
    return call(
        functools.partial(embed_back_kernel, scale=math.sqrt(width), count_pairs=count_pairs),
        [shape((features, vocab), F32), shape((features, 256), F32), shape(all_pairs, F32)],
        [
            SM,
            pl.BlockSpec((1, 4 * tile), lambda i: (0, i)),
            pl.BlockSpec((4, features, tile), lambda i: (i, 0, 0)),
            pl.BlockSpec((features, vocab), still),
        ]
        + [pl.BlockSpec((2, width), still)] * count_pairs,
        [
            pl.BlockSpec((features, vocab), still),
            pl.BlockSpec((features, 256), still),
            pl.BlockSpec(all_pairs, lambda i: (0, 0, 0)),
        ],
        (base, tokens, grad, head_grad, *pair_grads),
        after,
        flows,
        ident,
        tuple(stages_of_all()),
        hold=1,
        grid=(pieces // 4,),
        scratch_shapes=[
            pltpu.VMEM((features * (vocab // 256), 256), F32),
            pltpu.VMEM(all_pairs, F32),
            pltpu.VMEM((stages,) + all_pairs, F32),
            pltpu.SemaphoreType.DMA((stages,)),
            pltpu.SemaphoreType.DMA((stages,)),
        ],
        **settings(15_000_000_000, 4_000_000, "embed_back"),
    )


def last_sums_kernel(
    a_ref, a_more_ref, b_ref, b_more_ref, other_ref, other_more_ref, third_ref, square_ref, pair_ref, loss_ref, share_ref,
    out_ref, other_out, total_out,
    sum_scr, low_scr, come_scr, part_scr, parts_scr, send_sems, recv_sems, part_send, part_recv, *, bits, shared
):
    count = a_ref.shape[0]
    for t in range(count):
        sum_scr[t, :, 0:ATTN] = a_ref[t].astype(F32) + a_more_ref[t].astype(F32)
        sum_scr[t, :, ATTN:] = b_ref[t].astype(F32) + b_more_ref[t].astype(F32)
    def meanwhile():
        other = other_ref[...].astype(F32) + other_more_ref[...].astype(F32)
        other_out[...] = other
        pairs = pair_ref[...]
        square = jnp.sum(square_ref[...]) + jnp.sum(pairs * pairs) / shared + jnp.sum(other * other)
        for piece in third_ref:
            value = piece[...]
            square = square + jnp.sum(value * value)
        return square

    def send(at, place, columns, bit):
        part = (place, slice(None), columns)
        copy = remote(low_scr.at[part], come_scr.at[part], send_sems.at[at], recv_sems.at[at], "dp", bit)
        copy.start()
        return copy

    flags = [(lax.axis_index("dp") // bit) % 2 for bit in bits]
    if len(bits) == 2:
        near, far = flags
        near_bit, far_bit = bits
        copies = []
        for t in range(2):
            low_scr[t, :, ATTN:] = sum_scr[2 * t + 1 - near, :, ATTN:].astype(BF)
            copies.append(send(2 * t, t, pl.ds(ATTN, FEED), near_bit))
            low_scr[t, :, :ATTN] = sum_scr[2 * (1 - far) + t, :, :ATTN].astype(BF)
            copies.append(send(2 * t + 1, t, pl.ds(0, ATTN), far_bit))
        square = meanwhile()
        for copy in copies:
            copy.wait()
        for t in range(2):
            sum_scr[t, :, ATTN:] = sum_scr[2 * t + near, :, ATTN:] + come_scr[t, :, ATTN:].astype(F32)
            sum_scr[t, :, :ATTN] = sum_scr[2 * far + t, :, :ATTN] + come_scr[t, :, :ATTN].astype(F32)
        low_scr[2, :, ATTN:] = sum_scr[1 - far, :, ATTN:].astype(BF)
        low_scr[2, :, :ATTN] = sum_scr[1 - near, :, :ATTN].astype(BF)
        copies = [send(4, 2, pl.ds(ATTN, FEED), far_bit), send(5, 2, pl.ds(0, ATTN), near_bit)]
        for copy in copies:
            copy.wait()
        out_ref[:, ATTN:] = sum_scr[far, :, ATTN:] + come_scr[2, :, ATTN:].astype(F32)
        out_ref[:, :ATTN] = sum_scr[near, :, :ATTN] + come_scr[2, :, :ATTN].astype(F32)
    else:
        at = 0
        for bit, flag in zip(bits, flags):
            half = count // 2
            copies = []
            for t in range(half):
                low_scr[at] = sum_scr[2 * t + 1 - flag].astype(BF)
                copies.append(send(at, at, slice(None), bit))
                at += 1
            for t in range(half):
                copies[t].wait()
                sum_scr[t] = sum_scr[2 * t + flag] + come_scr[at - half + t].astype(F32)
            count = half
        square = meanwhile()
        out_ref[...] = sum_scr[0]
    value = out_ref[...]
    square = square + jnp.sum(value * value)
    row, lane = iota((8, 128), 0), iota((8, 128), 1)
    part_scr[...] = jnp.where(
        row == 0, jnp.where(lane == 0, square, jnp.where(lane == 1, loss_ref[...], jnp.where(lane == 2, share_ref[...], 0.0))), 0.0
    )
    place = 0
    for axis in ("head", "dp"):
        count = lax.axis_size(axis)
        hops = []
        here = place + lax.axis_index(axis)
        parts_scr[here] = part_scr[...]
        for step in range(1, count):
            at = place + step - 1
            hops.append(
                pltpu.make_async_remote_copy(
                    src_ref=part_scr,
                    dst_ref=parts_scr.at[here],
                    send_sem=part_send.at[at],
                    recv_sem=part_recv.at[at],
                    device_id={axis: (lax.axis_index(axis) + step) % count},
                    device_id_type=MESH,
                )
            )
            hops[-1].start()
        for hop in hops:
            hop.wait()
        part_scr[...] = jnp.sum(parts_scr[place:place + count], 0)
        place += count
    total_out[...] = part_scr[...]


def last_sums(attn, feed, other, thirds, squares, pair_grads, loss, count_share, bits, ident):
    def flat(value):
        return value.reshape((-1,) + value.shape[-2:])

    operands = [flat(one) for one in (*attn, *feed)] + [*other]
    count, features = operands[0].shape[:2]
    columns = ATTN + FEED
    stages = lax.axis_size("head") + lax.axis_size("dp")
    one = shape((features, columns), F32)
    fixed, extra = len(operands), len(thirds)

    def kernel(*refs):
        last_sums_kernel(
            *refs[:fixed], refs[fixed:fixed + extra], *refs[fixed + extra:], bits=bits,
            shared=lax.axis_size("dp") * lax.axis_size("head"),
        )

    return call(
        kernel,
        [one, one, shape((8, 128), F32)],
        [VM] * (fixed + extra + 4),
        [VM] * 3,
        (*operands, *thirds, squares, pair_grads, loss, count_share),
        ident=ident,
        greet_all=("head", "dp"),
        scratch_shapes=[
            pltpu.VMEM((count, features, columns), F32),
            pltpu.VMEM((count - 1, features, columns), BF),
            pltpu.VMEM((count - 1, features, columns), BF),
            pltpu.VMEM((8, 128), F32),
            pltpu.VMEM((stages, 8, 128), F32),
            pltpu.SemaphoreType.DMA((max(6, count - 1),)),
            pltpu.SemaphoreType.DMA((max(6, count - 1),)),
            pltpu.SemaphoreType.DMA((stages,)),
            pltpu.SemaphoreType.DMA((stages,)),
        ],
        **settings(1_000_000, 4_000_000, "last_sums"),
    )


def update_kernel(layers, sort_width, total_ref, table_grad_ref, norm_grad_ref, *refs):
    packs, ins, outs = refs[:layers], list(refs[layers:layers + 18]), list(refs[layers + 18:])
    norm = jnp.sqrt(total_ref[0:1, 0:1])
    factor = jnp.minimum(1.0, CLIP_LIMIT / (norm + 1e-06))

    def run(member, at, grad):
        weight_ref, first_ref, second_ref = ins[3 * member:3 * member + 3]
        rate = RATE_NORM if member == 5 else RATE_MATRIX
        scale = factor.reshape((1,) * grad.ndim)
        new, one, two = adamw(weight_ref[at], grad, first_ref[at], second_ref[at], scale, rate)
        results = (new, one, two) if member == 5 else (new, new.astype(BF), one, two)
        for target, result in zip(outs[4 * member:], results):
            target[at] = result

    def table_part(step, _):
        at = (slice(None), pl.ds(pl.multiple_of(step * 512, 512), 512))
        run(0, at, table_grad_ref[at])
        return 0

    lax.fori_loop(0, table_grad_ref.shape[1] // 512, table_part, 0)
    kv, srt = C_KVS[0], C_KVS[0] + 256
    starts = ((0, kv, kv + 64, srt), (64, kv + 192, kv + 128, srt + sort_width))
    for layer, pack in enumerate(packs):
        for h, (q, k, v, sort) in enumerate(starts):
            parts = [pack[:, at:at + HD] for at in (q, k, v)] + [pack[:, sort:sort + sort_width]]
            run(1, (layer, slice(None), h, slice(None)), jnp.concatenate(parts, 1))
        out = pack[:, C_OUT[0]:C_OUT[1]].T
        for h in range(2):
            run(2, (layer, h), out[(1 - h) * HD:(2 - h) * HD])
        run(3, layer, pack[:, ATTN + C_UP[0]:ATTN + C_UP[1]])
        run(4, layer, pack[:, ATTN + C_DOWN[0]:ATTN + C_DOWN[1]])
    size = ins[15].shape[2]
    mine = pl.ds(pl.multiple_of(lax.axis_index("head") * size, size), size)
    run(5, slice(None), norm_grad_ref[:, :, mine])


def update(totals, packs, table_grad, norm_grad, sort_width, members):
    outs = []
    for weight, _, _ in members[:-1]:
        full = shape(weight.shape, F32)
        outs += [full, shape(weight.shape, BF), full, full]
    outs += [shape(members[-1][0].shape, F32)] * 3
    operands = [totals, table_grad, norm_grad, *packs]
    for member in members:
        operands += member
    return call(
        functools.partial(update_kernel, len(packs), sort_width),
        outs,
        [VM] * len(operands),
        [VM] * len(outs),
        operands,
        **settings(1_000_000, 30_000_000, "update"),
    )[:-1]


def start_kernel(raw_ref, nrm_ref, stream_out, hid_out, *, scale):
    stream = raw_ref[...].astype(F32).T * scale
    stream_out[...] = stream
    hid_out[...] = norm_apply(stream, nrm_ref[0:1, :], nrm_ref[1:2, :])


def start_stream(raw, nrm, after=()):
    width, rows = raw.shape
    vm = pl.BlockSpec(memory_space=pltpu.VMEM)
    return call(
        functools.partial(start_kernel, scale=math.sqrt(width)),
        [
            jax.ShapeDtypeStruct((rows, width), F32),
            jax.ShapeDtypeStruct((rows, width), BF),
        ],
        [vm] * 2,
        [vm] * 2,
        (raw, nrm),
        after,
        name="start_stream",
    )


def finish_kernel(
    dy_ref, above_ref, carry_ref, gain_ref, pair_out, spread_out, piece_scr, own_sem, dp_send, dp_recv, send_sems, recv_sems, *, fly
):
    back, pair = norm_back(dy_ref[...], above_ref[...], gain_ref[...])
    pair_out[...] = pair
    piece_scr[...] = (carry_ref[...] + back).T.reshape(piece_scr.shape).astype(BF)
    count = piece_scr.shape[0]
    mine = lax.axis_index("dp")
    here = spread_out.at[0, mine]
    copies = [pltpu.make_async_copy(piece_scr.at[mine], here, own_sem)]
    for step in range(count - 1):
        peer = (mine + step + 1) % count
        copies.append(
            pltpu.make_async_remote_copy(
                src_ref=piece_scr.at[peer],
                dst_ref=here,
                send_sem=dp_send.at[step],
                recv_sem=dp_recv.at[step],
                device_id={"dp": peer},
                device_id_type=MESH,
            )
        )
    for copy in copies:
        copy.start()
    fly()
    for copy in copies:
        copy.wait()

    def hop(at, source, target, axis, bit):
        return remote(spread_out.at[source], spread_out.at[target], send_sems.at[at], recv_sems.at[at], axis, bit)

    far, near = hop(0, 0, 2, *HEADS[1]), hop(1, 0, 1, *HEADS[0])
    far.start()
    near.start()
    far.wait()
    cross = hop(2, 2, 3, *HEADS[0])
    cross.start()
    near.wait()
    cross.wait()


def finish_stream(dy, above, carry, gain, after=(), flows=(), ident=0):
    rows, width = above.shape
    dp, pairs = lax.axis_size("dp"), lax.axis_size("head")
    features = width // dp
    return call(
        finish_kernel,
        [shape((2, width), F32), shape((pairs, dp, features, rows), BF)],
        [VM] * 4,
        [VM, FAR],
        (dy, above, carry, gain),
        after,
        flows,
        ident,
        HEADS,
        ("dp",),
        hold=0,
        scratch_shapes=[
            pltpu.VMEM((dp, features, rows), BF),
            pltpu.SemaphoreType.DMA,
            pltpu.SemaphoreType.DMA((dp - 1,)),
            pltpu.SemaphoreType.DMA((dp - 1,)),
            pltpu.SemaphoreType.DMA((3,)),
            pltpu.SemaphoreType.DMA((3,)),
        ],
        name="finish_stream",
    )


def to_lanes(column):
    return jnp.broadcast_to(column, (column.shape[0], 128)).T[0:1, :]


def to_rows(line):
    return jnp.broadcast_to(line, (128, line.shape[1])).T[:, 0:1]


SLOTS = 8
SLOT_HOPS = (("head", 1, 4), ("head", 2, 2), ("dp", 1, 1))
GREET_SLOTS = HEADS + (("dp", 1),)


def head_forward_kernel(
    final_ref, table_ref, goal_ref, count_ref, rows_out, line_out, loss_out,
    rows_scr, stat_scr, come_scr, send_sems, recv_sems, stat_send, stat_recv
):
    def hop(at, source, target, which):
        axis, bit, _ = SLOT_HOPS[which]
        return remote(rows_scr.at[source], rows_scr.at[target], send_sems.at[at], recv_sems.at[at], axis, bit)

    rows_scr[0] = final_ref[...]
    core_own, low_own = hop(0, 0, 4, 0), hop(1, 0, 1, 2)
    far = [hop(2, 0, 2, 1), hop(3, 1, 3, 1)]
    core = [hop(4, 1, 5, 0), hop(5, 2, 6, 0), hop(6, 3, 7, 0)]
    core_own.start()
    low_own.start()
    far[0].start()

    def slot(at, _):
        @pl.when(at == 1)
        def _():
            core_own.wait()
            low_own.wait()
            far[1].start()
            core[0].start()

        @pl.when(at == 3)
        def _():
            core[0].wait()

        @pl.when(at == 4)
        def _():
            far[0].wait()
            core[1].start()
            far[1].wait()
            core[2].start()

        @pl.when(at == 6)
        def _():
            core[1].wait()
            core[2].wait()

        late = at // 4
        place = (1 - late) * (at // 2 + 4 * (at % 2)) + late * (2 + at % 2 + 4 * ((at // 2) % 2))
        logits = dot_nn(rows_scr[place], table_ref[...])
        top = jnp.max(logits, 1, keepdims=True)
        sums = jnp.sum(jnp.exp(logits - top), 1, keepdims=True)
        hit = iota(logits.shape, 1).astype(F32) == to_rows(goal_ref[place])
        pick = jnp.sum(jnp.where(hit, logits, 0.0), 1, keepdims=True)
        stat_scr[place, 0:1, :] = to_lanes(top)
        stat_scr[place, 1:2, :] = to_lanes(sums)
        stat_scr[place, 2:3, :] = to_lanes(pick)
        return 0

    lax.fori_loop(0, SLOTS, slot, 0)
    for at, (axis, bit, mask) in enumerate(SLOT_HOPS):
        meet = remote(stat_scr, come_scr.at[at], stat_send.at[at], stat_recv.at[at], axis, bit)
        meet.start()
        meet.wait()
        for place in range(SLOTS):
            mine, theirs = stat_scr[place], come_scr[at, place ^ mask]
            peak = jnp.maximum(mine[0:1], theirs[0:1])
            stat_scr[place, 1:2, :] = mine[1:2] * jnp.exp(mine[0:1] - peak) + theirs[1:2] * jnp.exp(
                theirs[0:1] - peak
            )
            stat_scr[place, 0:1, :] = peak
            stat_scr[place, 2:3, :] = mine[2:3] + theirs[2:3]
    loss = jnp.zeros((1, 1), F32)
    for place in range(SLOTS):
        mine = stat_scr[place]
        lse = mine[0:1] + jnp.log(mine[1:2])
        line_out[place, 0:1, :] = lse
        line_out[place, 1:2, :] = count_ref[place]
        loss += jnp.sum((lse - mine[2:3]) * count_ref[place], 1, keepdims=True)
    loss_out[...] = loss
    rows_out[...] = rows_scr[...]


def head_forward(final, table, goals, counted, ident):
    rows, width = final.shape
    hops = len(SLOT_HOPS)
    return call(
        head_forward_kernel,
        [shape((SLOTS, rows, width), BF), shape((SLOTS, 2, rows), F32), shape((1, 1), F32)],
        [VM] * 4,
        [VM] * 3,
        (final, table, goals, counted),
        ident=ident,
        greet=GREET_SLOTS,
        scratch_shapes=[
            pltpu.VMEM((SLOTS, rows, width), BF),
            pltpu.VMEM((SLOTS, 8, rows), F32),
            pltpu.VMEM((hops, SLOTS, 8, rows), F32),
            pltpu.SemaphoreType.DMA((7,)),
            pltpu.SemaphoreType.DMA((7,)),
            pltpu.SemaphoreType.DMA((hops,)),
            pltpu.SemaphoreType.DMA((hops,)),
        ],
        **settings(18_000_000_000, 6_000_000, "head_forward"),
    )


def head_backward_kernel(
    rows_ref, table_ref, goal_ref, line_ref, dy_out, gtab_out,
    acc_scr, grad_scr, send_scr, core_scr, far_scr, low_scr, keep_scr,
    core_send, core_recv, far_send, far_recv, low_send, low_recv
):
    rows = rows_ref.shape[1]

    def to_core(place):
        return remote(
            send_scr.at[place + 4], core_scr.at[place], core_send.at[place], core_recv.at[place], *HEADS[0]
        )

    def to_far(place):
        return remote(
            send_scr.at[place + 2], far_scr.at[place], far_send.at[place], far_recv.at[place], *HEADS[1]
        )

    to_low = remote(send_scr.at[1], low_scr, low_send, low_recv, "dp", 1)

    def pair(at, _):
        base = 6 - 4 * (at % 2) - 2 * (at // 2)
        for q in range(2):
            place = base + q + (at // 3) * (1 - 2 * q)
            logits = dot_nn(rows_ref[place], table_ref[...])
            hit = iota(logits.shape, 1).astype(F32) == to_rows(goal_ref[place])
            line = line_ref[place]
            chance = jnp.exp(logits - to_rows(line[0:1]))
            grad = ((chance - jnp.where(hit, 1.0, 0.0)) * to_rows(line[1:2])).astype(BF)
            grad_scr[q * rows:(q + 1) * rows, :] = grad
            part = dot_nt(grad, table_ref[...])

            @pl.when((at == 0) | (at == 2))
            def _():
                send_scr[place] = part.astype(BF)
                to_core(place - 4).start()

            @pl.when(at == 1)
            def _():
                to_core(place).wait()
                send_scr[place] = (part + core_scr[place].astype(F32)).astype(BF)
                to_far(place - 2).start()

            @pl.when(at == 3)
            def _():
                to_core(place).wait()
                to_far(place).wait()
                whole = part + core_scr[place].astype(F32) + far_scr[place].astype(F32)
                if q == 0:
                    send_scr[1] = whole.astype(BF)
                    to_low.start()
                else:
                    keep_scr[...] = whole

        both = [rows_ref[base + q + (at // 3) * (1 - 2 * q)] for q in range(2)]
        part = dot_tn(jnp.concatenate(both, 0), grad_scr[...])

        @pl.when(at == 0)
        def _():
            acc_scr[...] = part

        @pl.when(at > 0)
        def _():
            acc_scr[...] += part

        return 0

    lax.fori_loop(0, SLOTS // 2, pair, 0)
    gtab_out[...] = acc_scr[...].astype(BF)
    to_low.wait()
    dy_out[...] = keep_scr[...] + low_scr[...].astype(F32)


def head_backward(rows_all, table, goals, lines, ident):
    _, rows, width = rows_all.shape
    vocab = table.shape[1]
    return call(
        head_backward_kernel,
        [shape((rows, width), F32), shape((width, vocab), BF)],
        [VM] * 4,
        [VM] * 2,
        (rows_all, table, goals, lines),
        ident=ident,
        greet=GREET_SLOTS,
        scratch_shapes=[
            pltpu.VMEM((width, vocab), F32),
            pltpu.VMEM((2 * rows, vocab), BF),
            pltpu.VMEM((SLOTS, rows, width), BF),
            pltpu.VMEM((4, rows, width), BF),
            pltpu.VMEM((2, rows, width), BF),
            pltpu.VMEM((rows, width), BF),
            pltpu.VMEM((rows, width), F32),
            pltpu.SemaphoreType.DMA((4,)),
            pltpu.SemaphoreType.DMA((4,)),
            pltpu.SemaphoreType.DMA((2,)),
            pltpu.SemaphoreType.DMA((2,)),
            pltpu.SemaphoreType.DMA,
            pltpu.SemaphoreType.DMA,
        ],
        **settings(36_000_000_000, 14_000_000, "head_backward"),
    )


def swap(value, axis, bit):
    return lax.ppermute(value, axis, [(at, at ^ bit) for at in range(lax.axis_size(axis))])


def has_bit(axis, bit):
    return (lax.axis_index(axis) & bit) != 0


def bits_of(axis):
    size = lax.axis_size(axis)
    return [1 << at for at in reversed(range(size.bit_length() - 1))]


def in_order(mine, other, axis, bit, dim):
    flag = has_bit(axis, bit)
    return jnp.concatenate([jnp.where(flag, other, mine), jnp.where(flag, mine, other)], dim)


def gather_dp(value):
    bits = bits_of("dp")
    whole = value.reshape((1,) * len(bits) + value.shape)
    for dim, bit in enumerate(bits):
        whole = in_order(whole, swap(whole, "dp", bit), "dp", bit, dim)
    return whole.reshape((-1,) + value.shape)


def split(value, axis, bit, dim):
    flag = has_bit(axis, bit).astype(jnp.int32)
    low = value.astype(BF)
    return (
        lax.dynamic_index_in_dim(low, flag, dim, False),
        lax.dynamic_index_in_dim(low, 1 - flag, dim, False),
    )


def nothing_of(value):
    return value[(0,) * value.ndim].astype(F32) * 0.0


def add_up(*values):
    result = values[0].astype(F32)
    for value in values[1:]:
        result = result + (value.astype(F32) if value.ndim else value)
    return result


def sum_all(value, combine=jnp.add):
    for axis in ("head", "dp"):
        for bit in reversed(bits_of(axis)):
            value = combine(value, swap(value, axis, bit))
    return value


def pack_weights(attn_in, attn_out, ffn_up, ffn_down):
    features = attn_in.shape[0]
    low = attn_in.astype(BF)
    q, k, v = low[..., :HD], low[..., HD:2 * HD], low[..., 2 * HD:3 * HD]
    s = low[..., 3 * HD:].reshape(features, -1)
    blank = jnp.zeros((features, 128 - s.shape[1]), BF)
    out = attn_out.astype(BF)
    out = jnp.concatenate([out[1], out[0]], 0).T
    return jnp.concatenate(
        [
            q[:, 0], q[:, 1], k[:, 0], v[:, 0], v[:, 1], k[:, 1], s, blank,
            out, ffn_up.astype(BF), ffn_down.astype(BF).T,
        ],
        1,
    )


def depth_of(features):
    return max(64, features)


class Gather:
    def __init__(self, packed):
        bits = bits_of("dp")
        value = packed.reshape((1,) * len(bits) + packed.shape)
        for dim, bit in enumerate(bits[:-1]):
            value = in_order(value, swap(value, "dp", bit), "dp", bit, dim)
        self.value = value

    def finish(self):
        bits = bits_of("dp")
        across = swap(self.value, "head", 2)
        got = []
        for value in (self.value, across):
            whole = in_order(value, swap(value, "dp", bits[-1]), "dp", bits[-1], len(bits) - 1)
            got += [whole, swap(whole, "head", 1)]
        features, columns = self.value.shape[-2:]
        return [one.reshape(-1, depth_of(features), columns) for one in got]


def gather_rest(packed):
    dp, head = lax.axis_size("dp"), lax.axis_size("head")
    features, columns = packed.shape
    whole = lax.all_gather(packed, ("dp", "head"), axis=0, tiled=True)
    fold = depth_of(features) // features
    if fold > 1:
        whole = whole.reshape(dp // fold, fold, head, features, columns).transpose(0, 2, 1, 3, 4)
    return whole.reshape(dp // fold, head, fold * features, columns)


def adamw(weight, gradient, moment_one, moment_two, factor, step_rate):
    gradient = gradient * factor
    moment_one = BETA_ONE * moment_one + (1.0 - BETA_ONE) * gradient
    moment_two = BETA_TWO * moment_two + (1.0 - BETA_TWO) * gradient * gradient
    adam_step = (
        moment_one
        / (1.0 - BETA_ONE**STEP)
        / (jnp.sqrt(moment_two / (1.0 - BETA_TWO**STEP)) + ADAM_FLOOR)
    )
    return (weight - step_rate * (adam_step + WEIGHT_DECAY * weight), moment_one, moment_two)


def body(
    tokens, targets, lengths,
    table, table_first, table_second,
    attn_in, attn_in_first, attn_in_second,
    attn_out, attn_out_first, attn_out_second,
    ffn_up, ffn_up_first, ffn_up_second,
    ffn_down, ffn_down_first, ffn_down_second,
    norms, norms_first, norms_second,
):
    dp, head = lax.axis_size("dp"), lax.axis_size("head")
    my_dp, my_head = lax.axis_index("dp"), lax.axis_index("head")
    seq_count, length = tokens.shape
    features, vocab = table.shape
    width = features * dp
    layers = attn_in.shape[0]
    rows = length // head
    total_tokens = dp * length
    odd = my_dp & 1
    outer = [[at for at in range(dp) if at % 2 == way] for way in range(2)]

    lines = jnp.concatenate([tokens, targets, jnp.broadcast_to(lengths[:, None], (seq_count, 128))], 1)
    lines = gather_dp(lines.reshape(-1))
    all_tokens = lines[:, :length].reshape(1, total_tokens)
    positions = jnp.arange(length, dtype=jnp.int32)
    counted = (positions[None, :] < lines[:, 2 * length:2 * length + 1]).astype(F32)
    nrm = norms
    for bit in (1, 2):
        nrm = in_order(nrm, swap(nrm, "head", bit), "head", bit, 2)

    low_table = table.astype(BF)
    packs = [
        pack_weights(attn_in[at], attn_out[at], ffn_up[at], ffn_down[at]) for at in range(layers)
    ]
    leader = Gather(packs[0][:, :ATTN])
    idents = iter(range(1, 64))

    half = vocab // 2
    other = swap(lax.dynamic_slice_in_dim(low_table, (1 - odd) * half, half, 1), "dp", 1)
    mine = lax.dynamic_slice_in_dim(low_table, odd * half, half, 1)
    head_table = in_order(mine, other, "dp", 1, 0)

    base = (my_head * vocab).astype(jnp.int32).reshape(1)
    found, token = embed_lookup(base, all_tokens, low_table, [leader.value])
    rest_weights = gather_rest(jnp.concatenate([packs[0][:, ATTN:]] + packs[1:], 1))
    found = found.reshape(features, dp, head, rows)
    for bit in (1, 2):
        flag = (my_head & bit) // bit
        found = found.reshape(features, dp, -1, 2, rows) if bit == 1 else found.reshape(features, dp, 2, rows)
        dim = 3 if bit == 1 else 2
        other = swap(lax.dynamic_index_in_dim(found, 1 - flag, dim, False), "head", bit)
        found = lax.dynamic_index_in_dim(found, flag, dim, False) + other
    found = lax.all_to_all(found, "dp", split_axis=1, concat_axis=0, tiled=True)
    stream, hidden, token = start_stream(found.reshape(width, rows), nrm[0])
    head_table = lax.all_gather(
        head_table + token.astype(BF), "dp", axis=0, tiled=True, axis_index_groups=outer
    )
    sources = [((leader.finish(), 0), ([rest_weights], 0))]
    for at in range(1, layers):
        start = FEED + (at - 1) * (ATTN + FEED)
        sources.append((([rest_weights], start), ([rest_weights], start + ATTN)))

    kept = []
    for at in range(layers):
        (for_attend, attend_low), (for_feed, feed_low) = sources[at]
        middle, hidden_two, *saved, token = attend_forward(
            attend_low, hidden, stream, for_attend, nrm[2 * at + 1], ident=next(idents)
        )
        result, hidden, upward, active_rows, _ = feed_forward(
            feed_low, middle, hidden_two, for_feed, nrm[2 * at + 2]
        )
        kept.append((stream, (middle, hidden_two, upward, active_rows), saved))
        stream = result

    def line_of(values):
        values = values.reshape(dp, head, rows)
        order = [(my_dp ^ y, my_head ^ (x * 2 + c)) for c in range(2) for x in range(2) for y in range(2)]
        picked = [
            lax.dynamic_slice(values, (d, h, 0), (1, 1, rows)).reshape(rows) for d, h in order
        ]
        return jnp.concatenate(picked)

    goals = line_of(lines[:, length:2 * length]) - (my_head * vocab + odd * half).astype(jnp.int32)
    goals = goals.astype(F32).reshape(SLOTS, 1, rows)
    rows_all, stat_lines, loss_here, token = head_forward(
        hidden, head_table, goals, line_of(counted).reshape(SLOTS, 1, rows), next(idents)
    )
    loss_here = loss_here / (2 * head)
    count_total = jnp.sum(counted)
    dy, grad_half, token = head_backward(rows_all, head_table, goals, stat_lines, next(idents))
    grad_half = lax.psum_scatter(
        grad_half, "dp", scatter_dimension=0, tiled=True, axis_index_groups=outer
    ).reshape(2, features, half)

    carry = jnp.zeros((rows, width), F32)
    above = stream
    pair_grads = [None] * (2 * layers + 1)
    bits = bits_of("dp")

    def shaped(value):
        return value.reshape((2,) * len(bits) + (features, value.shape[-1]))

    def attn_steps(mine, theirs):
        across = yield theirs, "head", 2
        here, there = split(shaped(add_up(mine, across)), "dp", bits[-1], len(bits) - 1)
        return here, (yield there, "dp", bits[-1])

    def feed_steps(here, there):
        value = add_up(here, (yield there, "dp", bits[-1]))
        parts = value[0], (yield value[1].astype(BF), "head", 2)
        return tuple(part.reshape((2,) * (len(bits) - 1) + part.shape[-2:]) for part in parts)

    def last_steps(attn, feed):
        value = jnp.concatenate([add_up(*attn.parts), add_up(*feed.parts)], -1)
        for dim, bit in reversed(list(enumerate(bits[:-1]))):
            here, there = split(value, "dp", bit, dim)
            parts = here, (yield there, "dp", bit)
            value = add_up(*parts)
        return parts

    attns, feeds, lasts = [None] * layers, [None] * layers, [None] * layers

    def active(*candidates):
        return [flow for flow in candidates if flow is not None and flow.ask is not None]

    for at in reversed(range(layers)):
        stream_in, for_feed, for_attend = kept[at]
        (attend_sources, attend_low), (feed_sources, feed_low) = sources[at]
        above_attn, above_feed = (attns + [None])[at + 1], (feeds + [None])[at + 1]
        top_attn, top_feed = (attns + [None] * 2)[at + 2], (feeds + [None] * 2)[at + 2]
        here, there, carry, pair_above, pair_two, token = feed_backward(
            feed_low, dy, above, carry, nrm[2 * at + 2, 0:1], feed_sources, nrm[2 * at + 1, 0:1], for_feed,
            features, [grad_half] if at == 0 else [], active(top_attn, above_attn if at == 0 else None), next(idents),
        )
        feeds[at] = Flow(feed_steps(here, there))
        if at + 2 < layers:
            lasts[at + 2] = Flow(last_steps(top_attn, top_feed))
        dy, *attn_sums, token = attend_backward(
            attend_low, carry, attend_sources, for_attend, [],
            active(feeds[at], above_attn, above_feed, *lasts), next(idents),
        )
        attns[at] = Flow(attn_steps(*attn_sums))
        pair_grads[2 * at + 2] = pair_above
        pair_grads[2 * at + 1] = pair_two
        above = stream_in
    def once(value, axis, bit):
        return (yield value, axis, bit)

    grad_half = Flow(once(lax.dynamic_index_in_dim(grad_half, 1 - odd, 0, False), "dp", 1)), (
        lax.dynamic_index_in_dim(grad_half, odd, 0, False)
    )
    lasts[1] = Flow(last_steps(attns[1], feeds[1]))
    pair_grads[0], spread, token = finish_stream(
        dy, above, carry, nrm[0, 0:1], [], active(attns[0], grad_half[0], *lasts), next(idents)
    )

    head_grad = in_order(grad_half[1], grad_half[0].value, "dp", 1, 1)
    spread = spread.reshape(head * dp, features, rows)
    by_rows = all_tokens.reshape(dp, head, rows)
    order = [lax.dynamic_index_in_dim(by_rows, my_head ^ p, 1, False) for p in range(head)]
    grad_table, squares, grad_norms, token = embed_back(
        base, jnp.stack(order).reshape(1, total_tokens), spread, head_grad,
        pair_grads, [],
        active(attns[0], feeds[0], *lasts), next(idents),
    )
    sort_width = attn_in.shape[3] - 3 * HD
    thirds = [flow.finish() for flow in lasts[2:]]
    while lasts[1].ask is not None:
        lasts[1].give(swap(*lasts[1].ask))
    lower, other, totals, token = last_sums(
        attns[0].parts, feeds[0].parts, lasts[1].parts, thirds, squares, grad_norms, loss_here.reshape(1, 1),
        (count_total / (dp * head)).reshape(1, 1),
        tuple(reversed(bits[:-1])), next(idents),
    )
    results = update(
        totals, [lower, other] + thirds, grad_table, grad_norms, sort_width,
        [
            (table, table_first, table_second),
            (attn_in, attn_in_first, attn_in_second),
            (attn_out, attn_out_first, attn_out_second),
            (ffn_up, ffn_up_first, ffn_up_second),
            [one.transpose(0, 2, 1) for one in (ffn_down, ffn_down_first, ffn_down_second)],
            (norms, norms_first, norms_second),
        ],
    )
    results = list(results)
    results[16:20] = [one.transpose(0, 2, 1) for one in results[16:20]]
    return (totals[0, 1:3], jnp.sqrt(totals[0, 0]), *results)


def solution(mesh):
    ints = [P("dp", None), P("dp", None), P("dp")]
    by_table = P("dp", "head")
    by_in = P(None, "dp", "head", None)
    by_out = P(None, "head", None, "dp")
    by_up = P(None, "dp", "head")
    by_down = P(None, "head", "dp")
    by_norm = P(None, None, "head")
    in_specs, out_specs = list(ints), [P(), P()]
    for spec in (by_table, by_in, by_out, by_up, by_down):
        in_specs += [spec] * 3
        out_specs += [spec] * 4
    in_specs += [by_norm] * 3
    out_specs += [by_norm] * 3
    return jax.shard_map(
        body, mesh=mesh, in_specs=tuple(in_specs), out_specs=tuple(out_specs), check_vma=False
    )
```
